32 devices in a mesh: vox: 8 (over z, core), fsdp: 4 (over y, x).
Axes of the slice: x: 2, y: 2, z: 4, core: 2. Of those that a mesh axis runs over, the one named last changes fastest.
Arguments:
- tokens: bfloat16 [4, 3072, 1024], P('fsdp', 'vox'), may hold values from -6 to 6
- gain: float32 [1024], replicated, may hold values from 0.5 to 1.5
- w_qkv: bfloat16 [1024, 3072], P('fsdp'), may hold values from -0.1875 to 0.1875
- w_out: bfloat16 [1024, 1024], P('fsdp'), may hold values from -0.1875 to 0.1875
- logit_scale: float32 [16], replicated, may hold values from 4 to 240
- key_blocks: int32 [4, 48, 8], P('fsdp', 'vox'), may hold values from 0 to 47, as said below
- slot_count: int32 [4, 48], P('fsdp', 'vox'), may hold values from 1 to 8, as said below
- valid_voxels: int32 [4, 48], P('fsdp'), may hold values from 8 to 64
- cotangent: bfloat16 [4, 3072, 1024], P('fsdp', 'vox'), may hold values from -6 to 6
Outputs:
- mixed: bfloat16 [4, 3072, 1024], P('fsdp', 'vox')
- d_tokens: bfloat16 [4, 3072, 1024], P('fsdp', 'vox')
- d_wqkv: float32 [1024, 3072], P('fsdp', 'vox')
- d_wout: float32 [1024, 1024], P('fsdp', 'vox')
- d_gain: float32 [1024], replicated
- d_scale: float32 [16], replicated
The draws below stay inside these ranges and needn't reach their ends.
Inputs may be any that keep to these rules, and one draw needn't show every extreme that they name: `key_blocks`: slot 0 of every block names the block itself; every listed block lies in the same scene within 3 blocks of its query block, and that distance is reached. Slots from slot_count on are not used.
All inputs are finite; a program needn't handle non-finite values.
Results may differ from the reference program's by a relative error of at most 0.012.
The reference program's roundings to bfloat16 on the way count: a program that leaves them out, or rounds other values in their place, can miss the bound.
Values may be sent and summed in bfloat16 or wider, within the bound.
No kernel may reach another device: no remote copies, remote signals or barrier semaphores. Data moves between devices by JAX's collectives and lax.ppermute only.
A program may use at most 128 MiB of HBM per device.

```python
import jax
import jax.numpy as jnp
from jax import lax

D = 1024
HEADS = 16
HD = 64
BLK = 64
SLOTS = 8
BLK_DEV = 6
SVOX = 3072
SCENES = 4
N_VOX = 8
N_FSDP = 4


def window_lists(key):
    offset_key, ceiling_key, count_key = jax.random.split(key, 3)
    total_blocks = BLK_DEV * N_VOX
    reach_blocks = BLK_DEV // 2
    own_index = jnp.arange(total_blocks, dtype=jnp.int32)
    local_index = own_index % BLK_DEV
    device = own_index // BLK_DEV
    first_edge = jnp.logical_and(local_index == 0, device > 0)
    last_edge = jnp.logical_and(local_index == BLK_DEV - 1, device < N_VOX - 1)
    offsets = jax.random.randint(offset_key, (N_FSDP, total_blocks, SLOTS), -reach_blocks, reach_blocks + 1, dtype=jnp.int32)
    targets = jnp.clip(own_index[None, :, None] + offsets, 0, total_blocks - 1)
    position = jnp.arange(SLOTS, dtype=jnp.int32)[None, None, :]
    targets = jnp.where(position == 0, own_index[None, :, None], targets)
    targets = jnp.where(jnp.logical_and(position == 1, first_edge[None, :, None]), (own_index - reach_blocks)[None, :, None], targets)
    targets = jnp.where(jnp.logical_and(position == 1, last_edge[None, :, None]), (own_index + reach_blocks)[None, :, None], targets)
    ceilings = jax.random.randint(ceiling_key, (N_FSDP, N_VOX, 1), 2, SLOTS + 1, dtype=jnp.int32)
    numbers = jax.random.randint(count_key, (N_FSDP, N_VOX, BLK_DEV), 0, 1048576, dtype=jnp.int32)
    counts = (numbers % ceilings + 1).reshape(N_FSDP, total_blocks)
    edge_block = jnp.logical_or(first_edge, last_edge)[None, :]
    counts = jnp.where(edge_block, jnp.maximum(counts, 2), counts)
    counts = jnp.where((local_index == 1)[None, :], SLOTS, counts)
    return (targets, counts)


def draw_key_blocks(key, part):
    targets, counts = window_lists(jax.random.fold_in(key, 7))
    return targets


def draw_slot_count(key, part):
    targets, counts = window_lists(jax.random.fold_in(key, 7))
    return counts


def draw_valid_voxels(key, part):
    key = jax.random.fold_in(key, 3)
    full_key, size_key = jax.random.split(key)
    total_blocks = BLK_DEV * N_VOX
    choose_full = jax.random.randint(full_key, (N_FSDP, total_blocks), 0, 2, dtype=jnp.int32)
    partial_size = jax.random.randint(size_key, (N_FSDP, total_blocks), 8, BLK + 1, dtype=jnp.int32)
    voxels = jnp.where(choose_full == 1, BLK, partial_size)
    return voxels.at[:, 0].set(8)


def draw_logit_scale(key, part):
    key = jax.random.fold_in(key, 5)
    level = jax.random.uniform(key, (HEADS,), jnp.float32)
    return jnp.exp(jnp.log(4.0) + (jnp.log(24.0) - jnp.log(4.0)) * level)


def levels(rng, extent, shards, least, largest):
    level, own = 1.0, jax.random.fold_in(rng, 6)
    for dim, shards_of in shards:
        steps = jnp.exp(jax.random.uniform(jax.random.fold_in(own, dim), (shards_of,), jnp.float32, least / len(shards), largest / len(shards)))
        level = level * jnp.repeat(steps, extent[dim] // shards_of).reshape([-1 if axis == dim else 1 for axis in range(len(extent))])
    return level


def bell_draw(stream_key, extent, scale, reach, shards=(), kind=jnp.bfloat16):
    array = jax.random.normal(stream_key, extent, jnp.float32) * scale
    if len(shards) > 0:
        array = levels(stream_key, extent, shards, -0.22, 0.18) * array
    return jnp.clip(array, min=-reach, max=reach).astype(kind)


def setup_inputs(seed: int = 0) -> dict:
    keys = jax.random.split(jax.random.key(seed), 10)
    tokens = bell_draw(keys[0], (SCENES, SVOX, D), 1.0, 6.0, ((0, 4), (1, 8)))
    gain = jnp.clip(1.0 + 0.1 * jax.random.normal(keys[1], (D,), jnp.float32), 0.5, 1.5)
    w_qkv = bell_draw(keys[2], (D, 3 * D), D ** -0.5, 0.1875, ((0, 4),))
    w_out = bell_draw(keys[3], (D, D), D ** -0.5, 0.1875, ((0, 4),))
    logit_scale = draw_logit_scale(jax.random.fold_in(keys[9], 71), 0)
    key_blocks = draw_key_blocks(jax.random.fold_in(keys[9], 71), 0)
    slot_count = draw_slot_count(jax.random.fold_in(keys[9], 71), 0)
    valid_voxels = draw_valid_voxels(jax.random.fold_in(keys[9], 71), 0)
    cotangent = bell_draw(keys[8], (SCENES, SVOX, D), 1.0, 6.0, ((0, 4), (1, 8)))
    return dict(tokens=tokens, gain=gain, w_qkv=w_qkv, w_out=w_out, logit_scale=logit_scale, key_blocks=key_blocks, slot_count=slot_count, valid_voxels=valid_voxels, cotangent=cotangent)


EPS = 1e-06

def unit_rows(vectors):
    lengths = jnp.sqrt(lax.optimization_barrier(jnp.sum(vectors * vectors, axis=-1, keepdims=True)) + EPS)
    return (vectors / lengths, lengths)

def unit_back(unit, lengths, grads):
    return (grads - unit * lax.optimization_barrier(jnp.sum(unit * grads, axis=-1, keepdims=True))) / lengths

def pair_heads(query_part, key_part, value_part, grad_part, scale_pair, slot_index, slot_mask, key_live, query_live):
    block_total, block_rows, pair_width = query_part.shape
    pool_size = key_part.shape[0]
    head_size = pair_width // 2
    query_unit, query_len = unit_rows(query_part.astype(jnp.float32).reshape(block_total, block_rows, 2, head_size))
    key_unit, key_len = unit_rows(key_part.astype(jnp.float32).reshape(pool_size, block_rows, 2, head_size))
    query_low = query_unit.astype(jnp.bfloat16)
    key_low = key_unit.astype(jnp.bfloat16)
    picked_keys = jnp.take(key_low, slot_index, axis=0)
    picked_values = jnp.take(value_part.reshape(pool_size, block_rows, 2, head_size), slot_index, axis=0)
    cosine = jnp.einsum('bihd,bsjhd->bhisj', query_low.astype(jnp.float32), picked_keys.astype(jnp.float32))
    allowed = jnp.logical_and(slot_mask[:, :, None], jnp.take(key_live, slot_index, axis=0))[:, None, None, :, :]
    scale_view = scale_pair[None, :, None, None, None]
    scores = jnp.where(allowed, cosine * scale_view, -jnp.inf)
    row_peak = lax.optimization_barrier(jnp.max(scores, axis=(3, 4), keepdims=True))
    raised = jnp.where(allowed, jnp.exp(scores - row_peak), 0.0)
    weights = raised / lax.optimization_barrier(jnp.sum(raised, axis=(3, 4), keepdims=True))
    weights_low = weights.astype(jnp.bfloat16)
    row_keep = query_live[:, :, None, None]
    mixed_part = jnp.einsum('bhisj,bsjhd->bihd', weights_low.astype(jnp.float32), picked_values.astype(jnp.float32))
    mixed_part = jnp.where(row_keep, mixed_part, 0.0)
    upstream = jnp.where(row_keep, grad_part.reshape(block_total, block_rows, 2, head_size), jnp.zeros((), jnp.bfloat16))
    weight_grad = jnp.einsum('bihd,bsjhd->bhisj', upstream.astype(jnp.float32), picked_values.astype(jnp.float32))
    value_term = jnp.einsum('bhisj,bihd->bsjhd', weights_low.astype(jnp.float32), upstream.astype(jnp.float32))
    centre = lax.optimization_barrier(jnp.sum(weights * weight_grad, axis=(3, 4), keepdims=True))
    score_grad = weights * (weight_grad - centre)
    scale_grad = lax.optimization_barrier(jnp.sum(score_grad * cosine, axis=(0, 2, 3, 4)))
    cosine_grad = (score_grad * scale_view).astype(jnp.bfloat16)
    query_unit_grad = jnp.einsum('bhisj,bsjhd->bihd', cosine_grad.astype(jnp.float32), picked_keys.astype(jnp.float32))
    key_entry_grad = jnp.einsum('bhisj,bihd->bsjhd', cosine_grad.astype(jnp.float32), query_low.astype(jnp.float32))
    query_grad = unit_back(query_unit, query_len, query_unit_grad)
    empty_pool = jnp.zeros((pool_size, block_rows, 2, head_size), jnp.float32)
    key_unit_grad = empty_pool.at[slot_index].add(key_entry_grad)
    key_grad = unit_back(key_unit, key_len, key_unit_grad)
    value_grad = empty_pool.at[slot_index].add(value_term)
    return (mixed_part.reshape(block_total, block_rows, pair_width), query_grad.reshape(block_total, block_rows, pair_width), key_grad.reshape(pool_size, block_rows, pair_width), value_grad.reshape(pool_size, block_rows, pair_width), scale_grad)

def merge_heads(stacked):
    pair_total, block_total, block_rows, pair_width = stacked.shape
    return jnp.transpose(stacked, (1, 2, 0, 3)).reshape(block_total * block_rows, pair_total * pair_width)

def scene_pass(scene_tokens, scene_blocks, scene_counts, scene_voxels, scene_cotangent, gain, w_qkv, w_out, logit_scale):
    model_width = scene_tokens.shape[1]
    block_total = scene_blocks.shape[0]
    wide_tokens = scene_tokens.astype(jnp.float32)
    inverse = lax.rsqrt(lax.optimization_barrier(jnp.mean(wide_tokens * wide_tokens, axis=1, keepdims=True)) + EPS)
    normed = (wide_tokens * inverse * gain).astype(jnp.bfloat16)
    packed = jnp.dot(normed, w_qkv, preferred_element_type=jnp.float32).astype(jnp.bfloat16)
    upstream_all = jnp.dot(scene_cotangent, w_out.T, preferred_element_type=jnp.float32).astype(jnp.bfloat16)
    slot_mask = jnp.arange(SLOTS, dtype=jnp.int32)[None, :] < scene_counts[:, None]
    voxel_live = jnp.arange(BLK, dtype=jnp.int32)[None, :] < scene_voxels[:, None]
    packed_grid = packed.reshape(block_total, BLK, 3 * model_width)
    upstream_grid = upstream_all.reshape(block_total, BLK, model_width)
    pair_width = 2 * HD

    def one_pair(pair_index):
        start = pair_index * pair_width
        query_part = lax.dynamic_slice_in_dim(packed_grid, start, pair_width, 2)
        key_part = lax.dynamic_slice_in_dim(packed_grid, model_width + start, pair_width, 2)
        value_part = lax.dynamic_slice_in_dim(packed_grid, 2 * model_width + start, pair_width, 2)
        grad_part = lax.dynamic_slice_in_dim(upstream_grid, start, pair_width, 2)
        scale_pair = lax.dynamic_slice_in_dim(logit_scale, pair_index * 2, 2)
        return pair_heads(query_part, key_part, value_part, grad_part, scale_pair, scene_blocks, slot_mask, voxel_live, voxel_live)
    outputs = lax.map(one_pair, jnp.arange(HEADS // 2, dtype=jnp.int32))
    attention = merge_heads(outputs[0]).astype(jnp.bfloat16)
    mixed = (wide_tokens + jnp.dot(attention, w_out, preferred_element_type=jnp.float32)).astype(jnp.bfloat16)
    out_grad = jnp.dot(attention.T, scene_cotangent, preferred_element_type=jnp.float32)
    grad_packed = jnp.concatenate([merge_heads(outputs[1]), merge_heads(outputs[2]), merge_heads(outputs[3])], axis=1).astype(jnp.bfloat16)
    qkv_grad = jnp.dot(normed.T, grad_packed, preferred_element_type=jnp.float32)
    normed_grad = jnp.dot(grad_packed, w_qkv.T, preferred_element_type=jnp.float32)
    gain_grad = lax.optimization_barrier(jnp.sum(normed_grad * wide_tokens * inverse, axis=0))
    scaled_grad = normed_grad * gain
    token_grad = scene_cotangent.astype(jnp.float32) + inverse * (scaled_grad - wide_tokens * inverse * inverse * lax.optimization_barrier(jnp.mean(scaled_grad * wide_tokens, axis=1, keepdims=True)))
    scale_grad = outputs[4].reshape(HEADS)
    return (mixed, token_grad.astype(jnp.bfloat16), qkv_grad, out_grad, gain_grad, scale_grad)

def reference(tokens, gain, w_qkv, w_out, logit_scale, key_blocks, slot_count, valid_voxels, cotangent):

    def one_scene(inputs):
        scene_tokens, scene_blocks, scene_counts, scene_voxels, scene_cotangent = inputs
        return scene_pass(scene_tokens, scene_blocks, scene_counts, scene_voxels, scene_cotangent, gain, w_qkv, w_out, logit_scale)
    results = lax.map(one_scene, (tokens, key_blocks, slot_count, valid_voxels, cotangent))
    return (results[0], results[1], lax.optimization_barrier(jnp.sum(results[2], axis=0)), lax.optimization_barrier(jnp.sum(results[3], axis=0)), lax.optimization_barrier(jnp.sum(results[4], axis=0)), lax.optimization_barrier(jnp.sum(results[5], axis=0)))
```

```python
import functools

import jax
import jax.numpy as jnp
from jax import lax
from jax.experimental import pallas as pl
from jax.experimental.pallas import tpu as pltpu
from jax.sharding import PartitionSpec as P

HEADS = 16
HD = 64
PAIR = 2 * HD
BLK = 64
WINDOW = 8
EPS = 1e-06
LOG2E = 1.4426950408889634
BF = jnp.bfloat16
F32 = jnp.float32


def dot(a, b, dims=((1,), (0,))):
    return lax.dot_general(a, b, (dims, ((), ())), preferred_element_type=F32)


def head_sums(x, same_head):
    high = x.astype(BF)
    low = (x - high.astype(F32)).astype(BF)
    return dot(high, same_head) + dot(low, same_head)


def unit_rows(x, same_head):
    length = jnp.sqrt(head_sums(x * x, same_head) + EPS)
    return x / length, length


def unit_back(unit, length, grad, same_head):
    return (grad - unit * head_sums(unit * grad, same_head)) / length


def attention_kernel(
    mult_ref, valid_ref, scale_ref,
    q_ref, k_ref, v_ref, kb_ref, vb_ref, ka_ref, va_ref, u_ref,
    att_ref, dq_ref, dk_ref, dv_ref, rim_b_ref, rim_a_ref, ds_ref,
    k_unit, k_len, k_low, k_turn, v_low, v_turn, mult, s_ref, g_ref, e_ref, w_low, c_low, dk, dv,
):
    rows = q_ref.shape[0]
    margin = kb_ref.shape[0]
    pool = rows + 2 * margin
    reach = margin // BLK
    steps = rows // PAIR
    span = WINDOW * BLK
    pair = pl.program_id(0)

    lane = lax.broadcasted_iota(jnp.int32, (BLK, PAIR), 1)
    row = lax.broadcasted_iota(jnp.int32, (BLK, PAIR), 0)
    head_a = lax.broadcasted_iota(jnp.int32, (PAIR, PAIR), 0) < HD
    head_b = lax.broadcasted_iota(jnp.int32, (PAIR, PAIR), 1) < HD
    same_head = jnp.where(head_a == head_b, 1.0, 0.0).astype(BF)
    first_lanes = head_b

    @pl.when(pair == 0)
    def _():
        for t in range(steps):
            for w in range(WINDOW):
                count = jnp.where(lane < BLK, mult_ref[2 * t, w], mult_ref[2 * t + 1, w])
                live = row < valid_ref[2 * t + w]
                mult[t, w * BLK : (w + 1) * BLK, :] = jnp.where(live, count, 0).astype(F32)

    def split_heads(x):
        return jnp.concatenate(
            [jnp.where(first_lanes, x, 0.0), jnp.where(first_lanes, 0.0, x)], axis=0
        ).astype(BF)

    for src_k, src_v, at, count in (
        (kb_ref, vb_ref, 0, margin), (k_ref, v_ref, margin, rows), (ka_ref, va_ref, margin + rows, margin)
    ):
        for part in range(0, count, 128 if count % 128 == 0 else 64):
            size = 128 if count % 128 == 0 else 64
            place = slice(at + part, at + part + size)
            unit, length = unit_rows(src_k[part : part + size, :].astype(F32), same_head)
            k_unit[place, :] = unit
            k_len[place, :] = length
            k_low[place, :] = unit.astype(BF)
            v_low[place, :] = src_v[part : part + size, :]
    for part in range(0, pool, 128):
        place = slice(part, part + 128)
        k_turn[:, place] = jnp.transpose(k_low[place, :].astype(F32)).astype(BF)
        v_turn[:, place] = jnp.transpose(v_low[place, :].astype(F32)).astype(BF)

    dk[...] = jnp.zeros_like(dk)
    dv[...] = jnp.zeros_like(dv)
    wide_lane = lax.broadcasted_iota(jnp.int32, (1, 2 * PAIR), 1)
    scale = jnp.where(wide_lane < PAIR, scale_ref[2 * pair], scale_ref[2 * pair + 1])
    ds = jnp.zeros((8, 2 * PAIR), F32)

    for t in range(steps):
        own = slice(t * PAIR, (t + 1) * PAIR)
        window = slice(t * PAIR, t * PAIR + span)
        q_unit, q_len = unit_rows(q_ref[own, :].astype(F32), same_head)
        q_split = split_heads(q_unit)
        live = jnp.concatenate(
            [row < valid_ref[2 * t + reach], row < valid_ref[2 * t + 1 + reach]], axis=0
        )
        u_split = split_heads(jnp.where(live, u_ref[own, :].astype(F32), 0.0))
        s_ref[...] = dot(k_low[window, :], q_split, ((1,), (1,)))
        g_ref[...] = dot(v_low[window, :], u_split, ((1,), (1,)))

        def mult_of(part):
            half = mult[t, part, :]
            return jnp.concatenate([half, half], axis=1)

        parts = [slice(i, i + 32) for i in range(0, span, 32)]
        peak = jnp.full((8, 2 * PAIR), -1e30, F32)
        stretch = scale * LOG2E
        for part in parts:
            raised = jnp.where(mult_of(part) > 0.0, s_ref[part, :] * stretch, -1e30)
            peak = jnp.maximum(peak, jnp.max(raised.reshape(4, 8, 2 * PAIR), axis=0))
        peak = jnp.max(peak, axis=0, keepdims=True)
        total = jnp.zeros((8, 2 * PAIR), F32)
        centre = jnp.zeros((8, 2 * PAIR), F32)
        for part in parts:
            count = mult_of(part)
            shifted = jnp.where(count > 0.0, s_ref[part, :] * stretch - peak, -1e30)
            e = jnp.exp2(shifted) * count
            e_ref[part, :] = e
            total = total + jnp.sum(e.reshape(4, 8, 2 * PAIR), axis=0)
            centre = centre + jnp.sum((e * g_ref[part, :]).reshape(4, 8, 2 * PAIR), axis=0)
        share = 1.0 / jnp.sum(total, axis=0, keepdims=True)
        centre = jnp.sum(centre, axis=0, keepdims=True) * share
        for part in parts:
            w = e_ref[part, :] * share
            w_low[part, :] = w.astype(BF)
            sg = w * (g_ref[part, :] - centre)
            ds = ds + jnp.sum((sg * s_ref[part, :]).reshape(4, 8, 2 * PAIR), axis=0)
            c_low[part, :] = (sg * scale).astype(BF)

        def by_query(turned):
            return jnp.transpose(
                jnp.concatenate([turned[:HD, :PAIR], turned[HD:, PAIR:]], axis=0)
            )

        mixed = by_query(dot(v_turn[:, window], w_low[...]))
        att_ref[own, :] = jnp.where(live, mixed, 0.0).astype(BF)
        q_grad = by_query(dot(k_turn[:, window], c_low[...]))
        dq_ref[own, :] = unit_back(q_unit, q_len, q_grad, same_head).astype(BF)
        dv[window, :] += dot(w_low[...], u_split)
        dk[window, :] += dot(c_low[...], q_split)

    for part in range(0, pool, 64):
        place = slice(part, part + 64)
        grad_k = unit_back(k_unit[place, :], k_len[place, :], dk[place, :], same_head)
        grad_v = dv[place, :]
        if part < margin:
            rim_b_ref[0, place, :] = grad_k
            rim_b_ref[1, place, :] = grad_v
        elif part < margin + rows:
            here = slice(part - margin, part - margin + 64)
            dk_ref[here, :] = grad_k
            dv_ref[here, :] = grad_v
        else:
            here = slice(part - margin - rows, part - margin - rows + 64)
            rim_a_ref[0, here, :] = grad_k
            rim_a_ref[1, here, :] = grad_v
    ds_ref[0, :, :] = ds


def attention(packed, before, after, upstream, mult, valid, scales):
    rows, width3 = packed.shape
    width = width3 // 3
    margin = before.shape[0]
    pool = rows + 2 * margin
    pairs = width // PAIR
    steps = rows // PAIR
    span = WINDOW * BLK

    def at(offset):
        return lambda p, *_: (0, offset + p)

    return pl.pallas_call(
        attention_kernel,
        grid_spec=pltpu.PrefetchScalarGridSpec(
            num_scalar_prefetch=3,
            grid=(pairs,),
            in_specs=[
                pl.BlockSpec((rows, PAIR), at(0)),
                pl.BlockSpec((rows, PAIR), at(pairs)),
                pl.BlockSpec((rows, PAIR), at(2 * pairs)),
                pl.BlockSpec((margin, PAIR), at(0)),
                pl.BlockSpec((margin, PAIR), at(pairs)),
                pl.BlockSpec((margin, PAIR), at(0)),
                pl.BlockSpec((margin, PAIR), at(pairs)),
                pl.BlockSpec((rows, PAIR), at(0)),
            ],
            out_specs=[
                pl.BlockSpec((rows, PAIR), at(0)),
                pl.BlockSpec((rows, PAIR), at(0)),
                pl.BlockSpec((rows, PAIR), at(0)),
                pl.BlockSpec((rows, PAIR), at(0)),
                pl.BlockSpec((2, margin, PAIR), lambda p, *_: (0, 0, p)),
                pl.BlockSpec((2, margin, PAIR), lambda p, *_: (0, 0, p)),
                pl.BlockSpec((1, 8, 2 * PAIR), lambda p, *_: (p, 0, 0)),
            ],
            scratch_shapes=[
                pltpu.VMEM((pool, PAIR), F32),
                pltpu.VMEM((pool, PAIR), F32),
                pltpu.VMEM((pool, PAIR), BF),
                pltpu.VMEM((PAIR, pool), BF),
                pltpu.VMEM((pool, PAIR), BF),
                pltpu.VMEM((PAIR, pool), BF),
                pltpu.VMEM((steps, span, PAIR), F32),
                pltpu.VMEM((span, 2 * PAIR), F32),
                pltpu.VMEM((span, 2 * PAIR), F32),
                pltpu.VMEM((span, 2 * PAIR), F32),
                pltpu.VMEM((span, 2 * PAIR), BF),
                pltpu.VMEM((span, 2 * PAIR), BF),
                pltpu.VMEM((pool, PAIR), F32),
                pltpu.VMEM((pool, PAIR), F32),
            ],
        ),
        out_shape=[
            jax.ShapeDtypeStruct((rows, width), BF),
            jax.ShapeDtypeStruct((rows, width), BF),
            jax.ShapeDtypeStruct((rows, width), F32),
            jax.ShapeDtypeStruct((rows, width), F32),
            jax.ShapeDtypeStruct((2, margin, width), F32),
            jax.ShapeDtypeStruct((2, margin, width), F32),
            jax.ShapeDtypeStruct((pairs, 8, 2 * PAIR), F32),
        ],
        compiler_params=pltpu.CompilerParams(vmem_limit_bytes=40 * 1024 * 1024),
        cost_estimate=pl.CostEstimate(
            flops=2 * 6 * pairs * steps * span * 256 * 128,
            bytes_accessed=packed.size * 2 + rows * width * 14,
            transcendentals=pairs * steps * span * 256,
        ),
        name="block_attention",
    )(mult, valid, scales, packed, packed, packed, before, before, after, after, upstream)


def pick_groups(array, axis, unit, core):
    shape = array.shape
    split = shape[:axis] + (shape[axis] // (2 * unit), 2, unit) + shape[axis + 1 :]
    picked = lax.dynamic_index_in_dim(array.reshape(split), core, axis + 1, keepdims=False)
    return picked.reshape(shape[:axis] + (shape[axis] // 2,) + shape[axis + 1 :])


def in_order(core, own, other, axis):
    first = jnp.where(core == 0, own, other)
    second = jnp.where(core == 0, other, own)
    return jnp.concatenate([first, second], axis=axis)


def on_device(
    tokens, gain, w_qkv, w_out, logit_scale, key_blocks, slot_count, valid_voxels, cotangent
):
    own_tokens = tokens[0]
    own_cotangent = cotangent[0]
    own_rows, model_width = own_tokens.shape
    rows = 2 * own_rows
    own_blocks = key_blocks.shape[1]
    blocks = 2 * own_blocks
    slot_total = key_blocks.shape[2]
    reach = own_blocks // 2
    margin = reach * BLK
    n_vox = lax.axis_size("vox")
    n_chip = n_vox // 2
    place = lax.axis_index("vox")
    core = place % 2
    chip = place // 2
    chip_columns = 3 * model_width // n_chip
    unit = 128 if chip_columns % 256 == 0 and w_out.shape[0] % 256 == 0 else 64
    swap = [(i, i ^ 1) for i in range(n_vox)]
    up = [(i, i + 2) for i in range(n_vox - 2)]
    down = [(j, i) for i, j in up]
    same_core = [[2 * i + c for i in range(n_chip)] for c in range(2)]

    qkv_half = lax.all_gather(pick_groups(w_qkv, 1, unit, core), "fsdp", axis=0, tiled=True)
    out_half = lax.all_gather(pick_groups(w_out, 0, unit, core), "fsdp", axis=0, tiled=True)

    other_tokens = lax.ppermute(own_tokens, "vox", swap)
    other_cotangent = lax.ppermute(own_cotangent, "vox", swap)
    lists = jnp.concatenate([key_blocks[0], slot_count[0][:, None]], axis=1)
    all_lists = in_order(
        core, lists, lax.ppermute(lists.astype(F32), "vox", swap).astype(jnp.int32), 0
    )
    chip_tokens = in_order(core, own_tokens, other_tokens, 0)
    chip_cotangent = in_order(core, own_cotangent, other_cotangent, 0)

    first_block = chip * blocks
    pool_blocks = blocks + 2 * reach
    window_id = (
        all_lists[:, :slot_total] - first_block + reach
        - 2 * (jnp.arange(blocks, dtype=jnp.int32) // 2)[:, None]
    )
    used = jnp.arange(slot_total, dtype=jnp.int32)[None, :] < all_lists[:, slot_total:]
    hits = jnp.logical_and(
        window_id[:, :, None] == jnp.arange(WINDOW, dtype=jnp.int32), used[:, :, None]
    )
    mult = jnp.sum(hits.astype(jnp.int32), axis=1)
    scene_total = valid_voxels.shape[1]
    pool_ids = first_block - reach + jnp.arange(pool_blocks, dtype=jnp.int32)
    valid = jnp.take(valid_voxels[0], jnp.clip(pool_ids, 0, scene_total - 1))
    scales = pick_groups(logit_scale, 0, unit // HD, core)

    wide = chip_tokens.astype(F32)
    inverse = lax.rsqrt(jnp.mean(wide * wide, axis=1, keepdims=True) + EPS)
    normed = (wide * inverse * gain).astype(BF)
    packed = dot(normed, qkv_half).astype(BF)
    width = packed.shape[1] // 3
    before = lax.ppermute(packed[rows - margin :, width:], "vox", up)
    after = lax.ppermute(packed[:margin, width:], "vox", down)
    upstream = dot(chip_cotangent, out_half, ((1,), (1,))).astype(BF)

    att, dq, dk, dv, rim_b, rim_a, ds = attention(
        packed, before, after, upstream, mult, valid, scales
    )
    back_a = lax.ppermute(rim_b, "vox", down)
    back_b = lax.ppermute(rim_a, "vox", up)

    out_grad = dot(att, chip_cotangent, ((0,), (0,)))
    mixed_part = dot(att, out_half)
    mixed_mine = lax.dynamic_slice_in_dim(mixed_part, core * own_rows, own_rows, 0)
    mixed_theirs = lax.dynamic_slice_in_dim(mixed_part, (1 - core) * own_rows, own_rows, 0)
    mixed = (
        own_tokens.astype(F32) + (mixed_mine + lax.ppermute(mixed_theirs, "vox", swap))
    ).astype(BF)

    def with_rims(grad, index):
        return jnp.concatenate(
            [
                grad[:margin] + back_b[index],
                grad[margin : rows - margin],
                grad[rows - margin :] + back_a[index],
            ],
            axis=0,
        ).astype(BF)

    grad_packed = jnp.concatenate([dq, with_rims(dk, 0), with_rims(dv, 1)], axis=1)
    qkv_grad = dot(normed, grad_packed, ((0,), (0,)))
    ngrad_part = dot(grad_packed, qkv_half, ((1,), (1,)))
    ngrad_mine = lax.dynamic_slice_in_dim(ngrad_part, core * own_rows, own_rows, 0)
    ngrad_theirs = lax.dynamic_slice_in_dim(ngrad_part, (1 - core) * own_rows, own_rows, 0)
    normed_grad = ngrad_mine + lax.ppermute(ngrad_theirs, "vox", swap)

    own_wide = own_tokens.astype(F32)
    own_inverse = lax.rsqrt(jnp.mean(own_wide * own_wide, axis=1, keepdims=True) + EPS)
    gain_grad = jnp.sum(normed_grad * own_wide * own_inverse, axis=0)
    scaled_grad = normed_grad * gain
    token_grad = own_cotangent.astype(F32) + own_inverse * (
        scaled_grad
        - own_wide
        * own_inverse
        * own_inverse
        * jnp.mean(scaled_grad * own_wide, axis=1, keepdims=True)
    )

    group_heads = unit // HD
    scale_part = jnp.sum(ds.reshape(-1, 8, 2, PAIR), axis=(1, 3)).reshape(-1, 1, group_heads)
    mine = (jnp.arange(2) == core)[None, :, None]
    scale_grad = jnp.where(mine, scale_part, 0.0).reshape(HEADS)
    summed_gain, summed_scale = lax.psum((gain_grad, scale_grad), ("vox", "fsdp"))

    out_part = lax.psum_scatter(
        out_grad.astype(BF), "fsdp", scatter_dimension=0, tiled=True
    )
    out_sum = lax.psum_scatter(
        out_part, "vox", scatter_dimension=1, tiled=True, axis_index_groups=same_core
    ).astype(F32)
    qkv_part = lax.psum_scatter(
        qkv_grad.astype(BF), "fsdp", scatter_dimension=0, tiled=True
    )
    qkv_sum = lax.psum_scatter(
        qkv_part, "vox", scatter_dimension=1, tiled=True, axis_index_groups=same_core
    ).astype(F32)

    half = out_sum.shape[1] // 2
    out_mine = lax.dynamic_slice_in_dim(out_sum, core * half, half, 1)
    out_theirs = lax.ppermute(
        lax.dynamic_slice_in_dim(out_sum, (1 - core) * half, half, 1), "vox", swap
    )
    sets = out_sum.shape[0] // unit
    out_both = in_order(
        core,
        out_mine.reshape(sets, 1, unit, half),
        out_theirs.reshape(sets, 1, unit, half),
        1,
    )
    summed_out = out_both.reshape(2 * sets * unit, half)

    height, held = qkv_sum.shape
    qkv_other = lax.ppermute(qkv_sum, "vox", swap)
    qkv_both = in_order(
        core,
        qkv_sum.reshape(height, held // unit, 1, unit),
        qkv_other.reshape(height, held // unit, 1, unit),
        2,
    ).reshape(height, 2 * held)
    summed_qkv = lax.dynamic_slice_in_dim(qkv_both, core * held, held, 1)

    return (
        mixed[None],
        token_grad.astype(BF)[None],
        summed_qkv,
        summed_out,
        summed_gain,
        summed_scale,
    )


def solution(mesh):
    return jax.shard_map(
        on_device,
        mesh=mesh,
        in_specs=(
            P("fsdp", "vox", None),
            P(),
            P("fsdp", None),
            P("fsdp", None),
            P(),
            P("fsdp", "vox", None),
            P("fsdp", "vox"),
            P("fsdp", None),
            P("fsdp", "vox", None),
        ),
        out_specs=(
            P("fsdp", "vox", None),
            P("fsdp", "vox", None),
            P("fsdp", "vox"),
            P("fsdp", "vox"),
            P(),
            P(),
        ),
        check_vma=False,
    )
```

```python
import functools

import jax
import jax.numpy as jnp
from jax import lax
from jax.experimental import pallas as pl
from jax.experimental.pallas import tpu as pltpu
from jax.sharding import PartitionSpec as P

HEADS = 16
HD = 64
PAIR = 2 * HD
BLK = 64
WINDOW = 8
EPS = 1e-06
LOG2E = 1.4426950408889634
BF = jnp.bfloat16
F32 = jnp.float32


def dot(a, b, dims=((1,), (0,))):
    return lax.dot_general(a, b, (dims, ((), ())), preferred_element_type=F32)


def head_sums(x, same_head):
    high = x.astype(BF)
    low = (x - high.astype(F32)).astype(BF)
    return dot(high, same_head) + dot(low, same_head)


def unit_rows(x, same_head):
    length = jnp.sqrt(head_sums(x * x, same_head) + EPS)
    return x / length, length


def unit_back(unit, length, grad, same_head):
    return (grad - unit * head_sums(unit * grad, same_head)) / length


def attention_kernel(
    mult_ref, valid_ref, scale_ref,
    q_ref, k_ref, v_ref, kb_ref, vb_ref, ka_ref, va_ref, u_ref,
    att_ref, dq_ref, dk_ref, dv_ref, rim_b_ref, rim_a_ref, ds_ref,
    k_unit, k_len, k_low, k_turn, v_low, v_turn, mult, s_ref, g_ref, e_ref, w_low, c_low, dk, dv,
):
    rows = q_ref.shape[0]
    margin = kb_ref.shape[0]
    pool = rows + 2 * margin
    reach = margin // BLK
    steps = rows // PAIR
    span = WINDOW * BLK
    pair = pl.program_id(0)

    lane = lax.broadcasted_iota(jnp.int32, (BLK, PAIR), 1)
    row = lax.broadcasted_iota(jnp.int32, (BLK, PAIR), 0)
    head_a = lax.broadcasted_iota(jnp.int32, (PAIR, PAIR), 0) < HD
    head_b = lax.broadcasted_iota(jnp.int32, (PAIR, PAIR), 1) < HD
    same_head = jnp.where(head_a == head_b, 1.0, 0.0).astype(BF)
    first_lanes = head_b

    @pl.when(pair == 0)
    def _():
        for t in range(steps):
            for w in range(WINDOW):
                count = jnp.where(lane < BLK, mult_ref[2 * t, w], mult_ref[2 * t + 1, w])
                live = row < valid_ref[2 * t + w]
                mult[t, w * BLK : (w + 1) * BLK, :] = jnp.where(live, count, 0).astype(F32)

    def split_heads(x):
        return jnp.concatenate(
            [jnp.where(first_lanes, x, 0.0), jnp.where(first_lanes, 0.0, x)], axis=0
        ).astype(BF)

    for src_k, src_v, at, count in (
        (kb_ref, vb_ref, 0, margin), (k_ref, v_ref, margin, rows), (ka_ref, va_ref, margin + rows, margin)
    ):
        for part in range(0, count, 128 if count % 128 == 0 else 64):
            size = 128 if count % 128 == 0 else 64
            place = slice(at + part, at + part + size)
            unit, length = unit_rows(src_k[part : part + size, :].astype(F32), same_head)
            k_unit[place, :] = unit
            k_len[place, :] = length
            k_low[place, :] = unit.astype(BF)
            v_low[place, :] = src_v[part : part + size, :]
    for part in range(0, pool, 128):
        place = slice(part, part + 128)
        k_turn[:, place] = jnp.transpose(k_low[place, :].astype(F32)).astype(BF)
        v_turn[:, place] = jnp.transpose(v_low[place, :].astype(F32)).astype(BF)

    dk[...] = jnp.zeros_like(dk)
    dv[...] = jnp.zeros_like(dv)
    wide_lane = lax.broadcasted_iota(jnp.int32, (1, 2 * PAIR), 1)
    scale = jnp.where(wide_lane < PAIR, scale_ref[2 * pair], scale_ref[2 * pair + 1])
    ds = jnp.zeros((8, 2 * PAIR), F32)

    for t in range(steps):
        own = slice(t * PAIR, (t + 1) * PAIR)
        window = slice(t * PAIR, t * PAIR + span)
        q_unit, q_len = unit_rows(q_ref[own, :].astype(F32), same_head)
        q_split = split_heads(q_unit)
        live = jnp.concatenate(
            [row < valid_ref[2 * t + reach], row < valid_ref[2 * t + 1 + reach]], axis=0
        )
        u_split = split_heads(jnp.where(live, u_ref[own, :].astype(F32), 0.0))
        s_ref[...] = dot(k_low[window, :], q_split, ((1,), (1,)))
        g_ref[...] = dot(v_low[window, :], u_split, ((1,), (1,)))

        def mult_of(part):
            half = mult[t, part, :]
            return jnp.concatenate([half, half], axis=1)

        parts = [slice(i, i + 32) for i in range(0, span, 32)]
        peak = jnp.full((8, 2 * PAIR), -1e30, F32)
        stretch = scale * LOG2E
        for part in parts:
            raised = jnp.where(mult_of(part) > 0.0, s_ref[part, :] * stretch, -1e30)
            peak = jnp.maximum(peak, jnp.max(raised.reshape(4, 8, 2 * PAIR), axis=0))
        peak = jnp.max(peak, axis=0, keepdims=True)
        total = jnp.zeros((8, 2 * PAIR), F32)
        centre = jnp.zeros((8, 2 * PAIR), F32)
        for part in parts:
            count = mult_of(part)
            shifted = jnp.where(count > 0.0, s_ref[part, :] * stretch - peak, -1e30)
            e = jnp.exp2(shifted) * count
            e_ref[part, :] = e
            total = total + jnp.sum(e.reshape(4, 8, 2 * PAIR), axis=0)
            centre = centre + jnp.sum((e * g_ref[part, :]).reshape(4, 8, 2 * PAIR), axis=0)
        share = 1.0 / jnp.sum(total, axis=0, keepdims=True)
        centre = jnp.sum(centre, axis=0, keepdims=True) * share
        for part in parts:
            w = e_ref[part, :] * share
            w_low[part, :] = w.astype(BF)
            sg = w * (g_ref[part, :] - centre)
            ds = ds + jnp.sum((sg * s_ref[part, :]).reshape(4, 8, 2 * PAIR), axis=0)
            c_low[part, :] = (sg * scale).astype(BF)

        def by_query(turned):
            return jnp.transpose(
                jnp.concatenate([turned[:HD, :PAIR], turned[HD:, PAIR:]], axis=0)
            )

        mixed = by_query(dot(v_turn[:, window], w_low[...]))
        att_ref[own, :] = jnp.where(live, mixed, 0.0).astype(BF)
        q_grad = by_query(dot(k_turn[:, window], c_low[...]))
        dq_ref[own, :] = unit_back(q_unit, q_len, q_grad, same_head).astype(BF)
        dv[window, :] += dot(w_low[...], u_split)
        dk[window, :] += dot(c_low[...], q_split)

    for part in range(0, pool, 64):
        place = slice(part, part + 64)
        grad_k = unit_back(k_unit[place, :], k_len[place, :], dk[place, :], same_head)
        grad_v = dv[place, :]
        if part < margin:
            rim_b_ref[0, place, :] = grad_k.astype(BF)
            rim_b_ref[1, place, :] = grad_v.astype(BF)
        elif part < margin + rows:
            here = slice(part - margin, part - margin + 64)
            dk_ref[here, :] = grad_k
            dv_ref[here, :] = grad_v
        else:
            here = slice(part - margin - rows, part - margin - rows + 64)
            rim_a_ref[0, here, :] = grad_k.astype(BF)
            rim_a_ref[1, here, :] = grad_v.astype(BF)
    ds_ref[0, :, :] = ds


def attention(packed, before, after, upstream, mult, valid, scales, pairs):
    rows, width3 = packed.shape
    width = width3 // 3
    margin = before.shape[0]
    pool = rows + 2 * margin
    count = len(pairs)
    steps = rows // PAIR
    span = WINDOW * BLK
    first, stride = pairs[0], pairs[1] - pairs[0]

    def at(offset):
        return lambda p, *_: (0, offset + p)

    return pl.pallas_call(
        attention_kernel,
        grid_spec=pltpu.PrefetchScalarGridSpec(
            num_scalar_prefetch=3,
            grid=(count,),
            in_specs=[
                pl.BlockSpec((rows, PAIR), at(0)),
                pl.BlockSpec((rows, PAIR), at(count)),
                pl.BlockSpec((rows, PAIR), at(2 * count)),
                pl.BlockSpec((margin, PAIR), at(0)),
                pl.BlockSpec((margin, PAIR), at(count)),
                pl.BlockSpec((margin, PAIR), at(0)),
                pl.BlockSpec((margin, PAIR), at(count)),
                pl.BlockSpec((rows, PAIR), lambda p, *_: (0, first + stride * p)),
            ],
            out_specs=[
                pl.BlockSpec((rows, PAIR), at(0)),
                pl.BlockSpec((rows, PAIR), at(0)),
                pl.BlockSpec((rows, PAIR), at(0)),
                pl.BlockSpec((rows, PAIR), at(0)),
                pl.BlockSpec((2, margin, PAIR), lambda p, *_: (0, 0, p)),
                pl.BlockSpec((2, margin, PAIR), lambda p, *_: (0, 0, p)),
                pl.BlockSpec((1, 8, 2 * PAIR), lambda p, *_: (p, 0, 0)),
            ],
            scratch_shapes=[
                pltpu.VMEM((pool, PAIR), F32),
                pltpu.VMEM((pool, PAIR), F32),
                pltpu.VMEM((pool, PAIR), BF),
                pltpu.VMEM((PAIR, pool), BF),
                pltpu.VMEM((pool, PAIR), BF),
                pltpu.VMEM((PAIR, pool), BF),
                pltpu.VMEM((steps, span, PAIR), F32),
                pltpu.VMEM((span, 2 * PAIR), F32),
                pltpu.VMEM((span, 2 * PAIR), F32),
                pltpu.VMEM((span, 2 * PAIR), F32),
                pltpu.VMEM((span, 2 * PAIR), BF),
                pltpu.VMEM((span, 2 * PAIR), BF),
                pltpu.VMEM((pool, PAIR), F32),
                pltpu.VMEM((pool, PAIR), F32),
            ],
        ),
        out_shape=[
            jax.ShapeDtypeStruct((rows, width), BF),
            jax.ShapeDtypeStruct((rows, width), BF),
            jax.ShapeDtypeStruct((rows, width), F32),
            jax.ShapeDtypeStruct((rows, width), F32),
            jax.ShapeDtypeStruct((2, margin, width), BF),
            jax.ShapeDtypeStruct((2, margin, width), BF),
            jax.ShapeDtypeStruct((count, 8, 2 * PAIR), F32),
        ],
        compiler_params=pltpu.CompilerParams(vmem_limit_bytes=40 * 1024 * 1024),
        cost_estimate=pl.CostEstimate(
            flops=8 * 2 * 6 * count * steps * span * 256 * 128,
            bytes_accessed=packed.size * 2 + rows * width * 14,
            transcendentals=count * steps * span * 256,
        ),
        name="block_attention",
    )(mult, valid, scales, packed, packed, packed, before, before, after, after, upstream)


def pick_groups(array, axis, unit, core):
    size = array.shape[axis]
    picked = [
        jnp.where(
            core == 0,
            lax.slice_in_dim(array, at, at + unit, axis=axis),
            lax.slice_in_dim(array, at + unit, at + 2 * unit, axis=axis),
        )
        for at in range(0, size, 2 * unit)
    ]
    return jnp.concatenate(picked, axis=axis)


def spread_groups(array, axis, unit, core):
    groups = jnp.split(array, array.shape[axis] // unit, axis=axis)
    parts = []
    for group in groups:
        empty = jnp.zeros_like(group)
        parts += [jnp.where(core == 0, group, empty), jnp.where(core == 0, empty, group)]
    return jnp.concatenate(parts, axis=axis)


def in_order(core, own, other, axis):
    first = jnp.where(core == 0, own, other)
    second = jnp.where(core == 0, other, own)
    return jnp.concatenate([first, second], axis=axis)


def xor_blocks(blocks, index):
    odd = (index & 1) == 1
    high = (index & 2) == 2
    near = [jnp.where(odd, blocks[k ^ 1], blocks[k]) for k in range(4)]
    return [jnp.where(high, near[k ^ 2], near[k]) for k in range(4)]


ORDER = (1, 3, 2, 0)
CHUNKS = ((0, 3), (1, 2))


def square(value, step):
    return lax.ppermute(value, "fsdp", [(i, i ^ step) for i in range(4)])


def gather_square(shard):
    half = shard.shape[0] // 2
    near = square(shard, 1)
    far = square(shard, 2)
    top = square(far[:half], 1)
    low = square(near[half:], 2)
    return [near, jnp.concatenate([top, low], axis=0), far, shard]


def chips(value, step, n_vox):
    return lax.ppermute(value, "vox", [(i, i ^ (2 * step)) for i in range(n_vox)])


def reduce_square(normed_blocks, grad):
    half = grad.shape[1] // 2
    one, three, two, zero = normed_blocks
    left, right = grad[:, :half], grad[:, half:]
    t = ((0,), (0,))

    def both(a, b):
        return jnp.concatenate([a, b], axis=1)

    got_left = square(dot(both(one, three), left, t).astype(BF), 1)
    got_right = square(dot(both(three, two), right, t).astype(BF), 2)
    size = zero.shape[1]
    pass_left = dot(two, left, t) + got_left[size:].astype(F32)
    pass_right = dot(one, right, t) + got_right[:size].astype(F32)
    end_left = square(pass_left.astype(BF), 2)
    end_right = square(pass_right.astype(BF), 1)
    kept_left = dot(zero, left, t) + got_left[:size].astype(F32)
    kept_right = dot(zero, right, t) + got_right[size:].astype(F32)
    return jnp.concatenate(
        [kept_left + end_left.astype(F32), kept_right + end_right.astype(F32)], axis=1
    )


def on_device(
    tokens, gain, w_qkv, w_out, logit_scale, key_blocks, slot_count, valid_voxels, cotangent
):
    own_tokens = tokens[0]
    own_cotangent = cotangent[0]
    own_rows, model_width = own_tokens.shape
    rows = 2 * own_rows
    own_blocks = key_blocks.shape[1]
    blocks = 2 * own_blocks
    slot_total = key_blocks.shape[2]
    reach = own_blocks // 2
    margin = reach * BLK
    n_vox = lax.axis_size("vox")
    n_fsdp = lax.axis_size("fsdp")
    n_chip = n_vox // 2
    place = lax.axis_index("vox")
    scene = lax.axis_index("fsdp")
    core = place % 2
    chip = place // 2
    fast = n_vox == 8 and n_fsdp == 4
    unit = 128 if fast else 64
    swap = [(i, i ^ 1) for i in range(n_vox)]
    up = [(i, i + 2) for i in range(n_vox - 2)]
    down = [(j, i) for i, j in up]
    part_width = model_width // 2

    def columns_of(array, pairs):
        return jnp.concatenate(
            [
                array[:, base + p * PAIR : base + (p + 1) * PAIR]
                for base in range(0, array.shape[1], part_width)
                for p in pairs
            ],
            axis=1,
        )

    core_qkv = pick_groups(w_qkv, 1, unit, core)
    core_out = pick_groups(w_out, 0, unit, core)
    if fast:
        qkv_chunks = [
            jnp.concatenate(gather_square(columns_of(core_qkv, pairs)), axis=0) for pairs in CHUNKS
        ]
        one, three, two, zero = gather_square(core_out)
        out_half = jnp.concatenate(xor_blocks([zero, one, two, three], scene), axis=0)
    else:
        qkv_chunks = [
            lax.all_gather(columns_of(core_qkv, pairs), "fsdp", axis=0, tiled=True)
            for pairs in CHUNKS
        ]
        out_half = lax.all_gather(core_out, "fsdp", axis=0, tiled=True)

    other_tokens = lax.ppermute(own_tokens, "vox", swap)
    other_cotangent = lax.ppermute(own_cotangent, "vox", swap)
    lists = jnp.concatenate([key_blocks[0], slot_count[0][:, None]], axis=1)
    all_lists = in_order(
        core, lists, lax.ppermute(lists.astype(F32), "vox", swap).astype(jnp.int32), 0
    )
    chip_tokens = in_order(core, own_tokens, other_tokens, 0)
    chip_cotangent = in_order(core, own_cotangent, other_cotangent, 0)

    first_block = chip * blocks
    pool_blocks = blocks + 2 * reach
    window_id = (
        all_lists[:, :slot_total] - first_block + reach
        - 2 * (jnp.arange(blocks, dtype=jnp.int32) // 2)[:, None]
    )
    used = jnp.arange(slot_total, dtype=jnp.int32)[None, :] < all_lists[:, slot_total:]
    hits = jnp.logical_and(
        window_id[:, :, None] == jnp.arange(WINDOW, dtype=jnp.int32), used[:, :, None]
    )
    mult = jnp.sum(hits.astype(jnp.int32), axis=1)
    scene_total = valid_voxels.shape[1]
    pool_ids = first_block - reach + jnp.arange(pool_blocks, dtype=jnp.int32)
    valid = jnp.take(valid_voxels[0], jnp.clip(pool_ids, 0, scene_total - 1))
    group_heads = unit // HD
    scales = pick_groups(logit_scale, 0, group_heads, core)

    wide = chip_tokens.astype(F32)
    inverse = lax.rsqrt(jnp.mean(wide * wide, axis=1, keepdims=True) + EPS)
    normed = (wide * inverse * gain).astype(BF)
    if fast:
        turned = xor_blocks(jnp.split(normed, 4, axis=1), scene)
        normed_blocks = [turned[k] for k in ORDER]
        normed = jnp.concatenate(normed_blocks, axis=1)

    packed_chunks, halos = [], []
    for weight in qkv_chunks:
        packed = dot(normed, weight).astype(BF)
        width = packed.shape[1] // 3
        before = lax.ppermute(packed[rows - margin :, width:], "vox", up)
        after = lax.ppermute(packed[:margin, width:], "vox", down)
        packed_chunks.append(packed)
        halos.append((before, after))
    upstream = dot(chip_cotangent, out_half, ((1,), (1,))).astype(BF)

    mixed_part = 0.0
    ngrad_part = 0.0
    scale_parts = {}
    qkv_sums, out_sums = [], []
    for chunk, pairs in enumerate(CHUNKS):
        chunk_scales = jnp.concatenate([scales[2 * p : 2 * p + 2] for p in pairs])
        att, dq, dk, dv, rim_b, rim_a, ds = attention(
            packed_chunks[chunk], *halos[chunk], upstream, mult, valid, chunk_scales, pairs
        )
        back_a = lax.ppermute(rim_b, "vox", down).astype(F32)
        back_b = lax.ppermute(rim_a, "vox", up).astype(F32)
        head_sums_of = jnp.sum(ds.reshape(-1, 8, 2, PAIR), axis=(1, 3))
        for i, p in enumerate(pairs):
            scale_parts[p] = head_sums_of[i]

        out_rows = jnp.concatenate([out_half[p * PAIR : (p + 1) * PAIR] for p in pairs], axis=0)
        mixed_part = mixed_part + dot(att, out_rows)
        out_grad = dot(att, chip_cotangent, ((0,), (0,)))

        def with_rims(grad, index):
            return jnp.concatenate(
                [
                    grad[:margin] + back_b[index],
                    grad[margin : rows - margin],
                    grad[rows - margin :] + back_a[index],
                ],
                axis=0,
            ).astype(BF)

        grad_packed = jnp.concatenate([dq, with_rims(dk, 0), with_rims(dv, 1)], axis=1)
        ngrad_part = ngrad_part + dot(grad_packed, qkv_chunks[chunk], ((1,), (1,)))
        if fast:
            even, low = chip % 2 == 0, chip < 2
            quarter = model_width // 4
            cols = [out_grad[:, k * quarter : (k + 1) * quarter] for k in range(4)]
            kept = [jnp.where(even, cols[k], cols[k + 1]) for k in (0, 2)]
            sent = [jnp.where(even, cols[k + 1], cols[k]) for k in (0, 2)]
            got = chips(jnp.concatenate(sent, axis=1).astype(BF), 1, n_vox).astype(F32)
            kept = [kept[0] + got[:, :quarter], kept[1] + got[:, quarter:]]
            got = chips(jnp.where(low, kept[1], kept[0]).astype(BF), 2, n_vox).astype(F32)
            out_sums.append(jnp.where(low, kept[0], kept[1]) + got)

            part = reduce_square(normed_blocks, grad_packed)
            groups = [part[:, k * PAIR : (k + 1) * PAIR] for k in range(6)]
            sets = ((0, 3, 4), (1, 2, 5)) if chunk == 0 else ((0, 1, 3), (2, 4, 5))
            evens, odds = [jnp.concatenate([groups[k] for k in s], axis=1) for s in sets]
            got = chips(jnp.where(even, odds, evens).astype(BF), 1, n_vox).astype(F32)
            kept = jnp.where(even, evens, odds) + got
            left, right = kept[:, : 2 * PAIR], kept[:, PAIR:]
            got = chips(jnp.where(low, right, left).astype(BF), 2, n_vox).astype(F32)
            qkv_sums.append(jnp.where(low, left, right) + got)
        else:
            out_sums.append(out_grad)
            qkv_sums.append(dot(normed, grad_packed, ((0,), (0,))))

    mixed_mine = lax.dynamic_slice_in_dim(mixed_part, core * own_rows, own_rows, 0)
    mixed_theirs = lax.dynamic_slice_in_dim(mixed_part, (1 - core) * own_rows, own_rows, 0)
    mixed = (
        own_tokens.astype(F32) + (mixed_mine + lax.ppermute(mixed_theirs, "vox", swap))
    ).astype(BF)

    ngrad_mine = lax.dynamic_slice_in_dim(ngrad_part, core * own_rows, own_rows, 0)
    ngrad_theirs = lax.dynamic_slice_in_dim(ngrad_part, (1 - core) * own_rows, own_rows, 0)
    normed_grad = ngrad_mine + lax.ppermute(ngrad_theirs, "vox", swap)
    if fast:
        held = jnp.split(normed_grad, 4, axis=1)
        normed_grad = jnp.concatenate(
            xor_blocks([held[ORDER.index(k)] for k in range(4)], scene), axis=1
        )

    own_wide = own_tokens.astype(F32)
    own_inverse = lax.rsqrt(jnp.mean(own_wide * own_wide, axis=1, keepdims=True) + EPS)
    gain_grad = jnp.sum(normed_grad * own_wide * own_inverse, axis=0)
    scaled_grad = normed_grad * gain
    token_grad = own_cotangent.astype(F32) + own_inverse * (
        scaled_grad
        - own_wide
        * own_inverse
        * own_inverse
        * jnp.mean(scaled_grad * own_wide, axis=1, keepdims=True)
    )

    scale_part = jnp.concatenate([scale_parts[p] for p in range(len(scale_parts))])
    scale_grad = spread_groups(scale_part, 0, group_heads, core)
    if fast:
        small = jnp.concatenate([gain_grad, scale_grad, jnp.zeros((112,), F32)]).reshape(9, 128)
        for step in (1, 2):
            small = small + square(small, step)
        for step in (1, 2, 4):
            small = small + lax.ppermute(small, "vox", [(i, i ^ step) for i in range(n_vox)])
        small = small.reshape(-1)
        summed_gain, summed_scale = small[:model_width], small[model_width : model_width + HEADS]
    else:
        summed_gain, summed_scale = lax.psum((gain_grad, scale_grad), ("vox", "fsdp"))

    if fast:
        by_pair = {}
        for pairs, total in zip(CHUNKS, out_sums):
            for i, p in enumerate(pairs):
                by_pair[p] = total[i * PAIR : (i + 1) * PAIR]
        turned = xor_blocks([by_pair[p] for p in range(4)], scene)
        out_sum = turned[0]
        for step in (1, 2, 3):
            out_sum = out_sum + square(turned[step].astype(BF), step).astype(F32)
        half = out_sum.shape[1] // 2
        first, second = out_sum[:, :half], out_sum[:, half:]
        out_other = lax.ppermute(jnp.where(core == 0, second, first), "vox", swap)
        summed_out = in_order(core, jnp.where(core == 0, first, second), out_other, 0)

        a0, a1 = qkv_sums[0][:, :PAIR], qkv_sums[0][:, PAIR:]
        b0, b1 = qkv_sums[1][:, :PAIR], qkv_sums[1][:, PAIR:]

        def by_chip(options):
            value = options[3]
            for k in range(3):
                value = jnp.where(chip == k, options[k], value)
            return value

        g0 = by_chip((a0, a0, b1, b0))
        g1 = by_chip((b0, a1, a0, b1))
        g2 = by_chip((b1, b0, a1, a1))
        got = lax.ppermute(jnp.where(core == 0, g2, g0), "vox", swap)
        summed_qkv = jnp.concatenate(
            [
                jnp.where(core == 0, g0, g1),
                got,
                jnp.where(core == 0, g1, g2),
            ],
            axis=1,
        )
    else:
        by_pair = {}
        cols = {}
        for pairs, out_total, qkv_total in zip(CHUNKS, out_sums, qkv_sums):
            for i, p in enumerate(pairs):
                by_pair[p] = out_total[i * PAIR : (i + 1) * PAIR]
                for j in range(3):
                    at = (2 * j + i) * PAIR
                    cols[4 * j + p] = qkv_total[:, at : at + PAIR]
        out_total = jnp.concatenate([by_pair[p] for p in range(4)], axis=0)
        qkv_total = jnp.concatenate([cols[k] for k in range(12)], axis=1)
        out_total = spread_groups(out_total, 0, unit, core)
        qkv_total = lax.psum_scatter(qkv_total, "fsdp", scatter_dimension=0, tiled=True)
        qkv_total = spread_groups(qkv_total, 1, unit, core)
        summed_qkv = lax.psum_scatter(qkv_total, "vox", scatter_dimension=1, tiled=True)
        out_total = lax.psum_scatter(out_total, "fsdp", scatter_dimension=0, tiled=True)
        summed_out = lax.psum_scatter(out_total, "vox", scatter_dimension=1, tiled=True)

    return (
        mixed[None],
        token_grad.astype(BF)[None],
        summed_qkv,
        summed_out,
        summed_gain,
        summed_scale,
    )


def solution(mesh):
    return jax.shard_map(
        on_device,
        mesh=mesh,
        in_specs=(
            P("fsdp", "vox", None),
            P(),
            P("fsdp", None),
            P("fsdp", None),
            P(),
            P("fsdp", "vox", None),
            P("fsdp", "vox"),
            P("fsdp", None),
            P("fsdp", "vox", None),
        ),
        out_specs=(
            P("fsdp", "vox", None),
            P("fsdp", "vox", None),
            P("fsdp", "vox"),
            P("fsdp", "vox"),
            P(),
            P(),
        ),
        check_vma=False,
    )
```

```python
import functools

import jax
import jax.numpy as jnp
from jax import lax
from jax.experimental import pallas as pl
from jax.experimental.pallas import tpu as pltpu
from jax.sharding import PartitionSpec as P

HEADS = 16
HD = 64
PAIR = 2 * HD
BLK = 64
WINDOW = 8
EPS = 1e-06
LOG2E = 1.4426950408889634
BF = jnp.bfloat16
F32 = jnp.float32


def dot(a, b, dims=((1,), (0,))):
    return lax.dot_general(a, b, (dims, ((), ())), preferred_element_type=F32)


def head_sums(x, same_head):
    high = x.astype(BF)
    low = (x - high.astype(F32)).astype(BF)
    return dot(high, same_head) + dot(low, same_head)


def unit_rows(x, same_head):
    length = jnp.sqrt(head_sums(x * x, same_head) + EPS)
    return x / length, length


def unit_back(unit, length, grad, same_head):
    return (grad - unit * head_sums(unit * grad, same_head)) / length


def attention_kernel(
    mult_ref, valid_ref, scale_ref,
    q_ref, k_ref, v_ref, kb_ref, vb_ref, ka_ref, va_ref, u_ref,
    att_ref, dq_ref, dk_ref, dv_ref, rim_b_ref, rim_a_ref, ds_ref,
    k_unit, k_len, k_low, k_turn, v_low, v_turn, mult, s_ref, g_ref, e_ref, w_low, c_low, dk, dv,
):
    rows = q_ref.shape[0]
    margin = kb_ref.shape[0]
    pool = rows + 2 * margin
    reach = margin // BLK
    steps = rows // PAIR
    span = WINDOW * BLK
    pair = pl.program_id(0)

    lane = lax.broadcasted_iota(jnp.int32, (BLK, PAIR), 1)
    row = lax.broadcasted_iota(jnp.int32, (BLK, PAIR), 0)
    head_a = lax.broadcasted_iota(jnp.int32, (PAIR, PAIR), 0) < HD
    head_b = lax.broadcasted_iota(jnp.int32, (PAIR, PAIR), 1) < HD
    same_head = jnp.where(head_a == head_b, 1.0, 0.0).astype(BF)
    first_lanes = head_b

    @pl.when(pair == 0)
    def _():
        for t in range(steps):
            for w in range(WINDOW):
                count = jnp.where(lane < BLK, mult_ref[2 * t, w], mult_ref[2 * t + 1, w])
                live = row < valid_ref[2 * t + w]
                mult[t, w * BLK : (w + 1) * BLK, :] = jnp.where(live, count, 0).astype(F32)

    def split_heads(x):
        return jnp.concatenate(
            [jnp.where(first_lanes, x, 0.0), jnp.where(first_lanes, 0.0, x)], axis=0
        ).astype(BF)

    for src_k, src_v, at, count in (
        (kb_ref, vb_ref, 0, margin), (k_ref, v_ref, margin, rows), (ka_ref, va_ref, margin + rows, margin)
    ):
        for part in range(0, count, 128 if count % 128 == 0 else 64):
            size = 128 if count % 128 == 0 else 64
            place = slice(at + part, at + part + size)
            unit, length = unit_rows(src_k[part : part + size, :].astype(F32), same_head)
            k_unit[place, :] = unit
            k_len[place, :] = length
            k_low[place, :] = unit.astype(BF)
            v_low[place, :] = src_v[part : part + size, :]
    for part in range(0, pool, 128):
        place = slice(part, part + 128)
        k_turn[:, place] = jnp.transpose(k_low[place, :].astype(F32)).astype(BF)
        v_turn[:, place] = jnp.transpose(v_low[place, :].astype(F32)).astype(BF)

    dk[...] = jnp.zeros_like(dk)
    dv[...] = jnp.zeros_like(dv)
    wide_lane = lax.broadcasted_iota(jnp.int32, (1, 2 * PAIR), 1)
    scale = jnp.where(wide_lane < PAIR, scale_ref[2 * pair], scale_ref[2 * pair + 1])
    ds = jnp.zeros((8, 2 * PAIR), F32)

    for t in range(steps):
        own = slice(t * PAIR, (t + 1) * PAIR)
        window = slice(t * PAIR, t * PAIR + span)
        q_unit, q_len = unit_rows(q_ref[own, :].astype(F32), same_head)
        q_split = split_heads(q_unit)
        live = jnp.concatenate(
            [row < valid_ref[2 * t + reach], row < valid_ref[2 * t + 1 + reach]], axis=0
        )
        u_split = split_heads(jnp.where(live, u_ref[own, :].astype(F32), 0.0))
        s_ref[...] = dot(k_low[window, :], q_split, ((1,), (1,)))
        g_ref[...] = dot(v_low[window, :], u_split, ((1,), (1,)))

        def mult_of(part):
            half = mult[t, part, :]
            return jnp.concatenate([half, half], axis=1)

        parts = [slice(i, i + 32) for i in range(0, span, 32)]
        peak = jnp.full((8, 2 * PAIR), -1e30, F32)
        stretch = scale * LOG2E
        for part in parts:
            raised = jnp.where(mult_of(part) > 0.0, s_ref[part, :] * stretch, -1e30)
            peak = jnp.maximum(peak, jnp.max(raised.reshape(4, 8, 2 * PAIR), axis=0))
        peak = jnp.max(peak, axis=0, keepdims=True)
        total = jnp.zeros((8, 2 * PAIR), F32)
        centre = jnp.zeros((8, 2 * PAIR), F32)
        for part in parts:
            count = mult_of(part)
            shifted = jnp.where(count > 0.0, s_ref[part, :] * stretch - peak, -1e30)
            e = jnp.exp2(shifted) * count
            e_ref[part, :] = e
            total = total + jnp.sum(e.reshape(4, 8, 2 * PAIR), axis=0)
            centre = centre + jnp.sum((e * g_ref[part, :]).reshape(4, 8, 2 * PAIR), axis=0)
        share = 1.0 / jnp.sum(total, axis=0, keepdims=True)
        centre = jnp.sum(centre, axis=0, keepdims=True) * share
        for part in parts:
            w = e_ref[part, :] * share
            w_low[part, :] = w.astype(BF)
            sg = w * (g_ref[part, :] - centre)
            ds = ds + jnp.sum((sg * s_ref[part, :]).reshape(4, 8, 2 * PAIR), axis=0)
            c_low[part, :] = (sg * scale).astype(BF)

        def by_query(turned):
            return jnp.transpose(
                jnp.concatenate([turned[:HD, :PAIR], turned[HD:, PAIR:]], axis=0)
            )

        mixed = by_query(dot(v_turn[:, window], w_low[...]))
        att_ref[own, :] = jnp.where(live, mixed, 0.0).astype(BF)
        q_grad = by_query(dot(k_turn[:, window], c_low[...]))
        dq_ref[own, :] = unit_back(q_unit, q_len, q_grad, same_head).astype(BF)
        dv[window, :] += dot(w_low[...], u_split)
        dk[window, :] += dot(c_low[...], q_split)

    for part in range(0, pool, 64):
        place = slice(part, part + 64)
        grad_k = unit_back(k_unit[place, :], k_len[place, :], dk[place, :], same_head)
        grad_v = dv[place, :]
        if part < margin:
            rim_b_ref[0, place, :] = grad_k.astype(BF)
            rim_b_ref[1, place, :] = grad_v.astype(BF)
        elif part < margin + rows:
            here = slice(part - margin, part - margin + 64)
            dk_ref[here, :] = grad_k
            dv_ref[here, :] = grad_v
        else:
            here = slice(part - margin - rows, part - margin - rows + 64)
            rim_a_ref[0, here, :] = grad_k.astype(BF)
            rim_a_ref[1, here, :] = grad_v.astype(BF)
    ds_ref[0, :, :] = ds


def attention(packed, before, after, upstream, mult, valid, scales, index, count, pair):
    rows, width3 = packed.shape
    margin = before.shape[0]
    pool = rows + 2 * margin
    steps = rows // PAIR
    span = WINDOW * BLK

    def at(offset):
        return lambda p, *_: (0, offset)

    return pl.pallas_call(
        attention_kernel,
        grid_spec=pltpu.PrefetchScalarGridSpec(
            num_scalar_prefetch=3,
            grid=(1,),
            in_specs=[
                pl.BlockSpec((rows, PAIR), at(index)),
                pl.BlockSpec((rows, PAIR), at(count + index)),
                pl.BlockSpec((rows, PAIR), at(2 * count + index)),
                pl.BlockSpec((margin, PAIR), at(index)),
                pl.BlockSpec((margin, PAIR), at(count + index)),
                pl.BlockSpec((margin, PAIR), at(index)),
                pl.BlockSpec((margin, PAIR), at(count + index)),
                pl.BlockSpec((rows, PAIR), at(pair)),
            ],
            out_specs=[
                pl.BlockSpec((rows, PAIR), at(0)),
                pl.BlockSpec((rows, PAIR), at(0)),
                pl.BlockSpec((rows, PAIR), at(0)),
                pl.BlockSpec((rows, PAIR), at(0)),
                pl.BlockSpec((2, margin, PAIR), lambda p, *_: (0, 0, 0)),
                pl.BlockSpec((2, margin, PAIR), lambda p, *_: (0, 0, 0)),
                pl.BlockSpec((1, 8, 2 * PAIR), lambda p, *_: (0, 0, 0)),
            ],
            scratch_shapes=[
                pltpu.VMEM((pool, PAIR), F32),
                pltpu.VMEM((pool, PAIR), F32),
                pltpu.VMEM((pool, PAIR), BF),
                pltpu.VMEM((PAIR, pool), BF),
                pltpu.VMEM((pool, PAIR), BF),
                pltpu.VMEM((PAIR, pool), BF),
                pltpu.VMEM((steps, span, PAIR), F32),
                pltpu.VMEM((span, 2 * PAIR), F32),
                pltpu.VMEM((span, 2 * PAIR), F32),
                pltpu.VMEM((span, 2 * PAIR), F32),
                pltpu.VMEM((span, 2 * PAIR), BF),
                pltpu.VMEM((span, 2 * PAIR), BF),
                pltpu.VMEM((pool, PAIR), F32),
                pltpu.VMEM((pool, PAIR), F32),
            ],
        ),
        out_shape=[
            jax.ShapeDtypeStruct((rows, PAIR), BF),
            jax.ShapeDtypeStruct((rows, PAIR), BF),
            jax.ShapeDtypeStruct((rows, PAIR), F32),
            jax.ShapeDtypeStruct((rows, PAIR), F32),
            jax.ShapeDtypeStruct((2, margin, PAIR), BF),
            jax.ShapeDtypeStruct((2, margin, PAIR), BF),
            jax.ShapeDtypeStruct((1, 8, 2 * PAIR), F32),
        ],
        compiler_params=pltpu.CompilerParams(vmem_limit_bytes=40 * 1024 * 1024),
        cost_estimate=pl.CostEstimate(
            flops=8 * 2 * 6 * steps * span * 256 * 128,
            bytes_accessed=rows * PAIR * 20,
            transcendentals=steps * span * 256,
        ),
        name="block_attention",
    )(mult, valid, scales, packed, packed, packed, before, before, after, after, upstream)


def pick_kernel(core_ref, qkv_ref, out_ref, *picked):
    core = core_ref[0]
    for chunk, pairs in enumerate(CHUNKS):
        at = 0
        for base in range(0, qkv_ref.shape[1], 8 * PAIR):
            for p in pairs:
                start = pl.multiple_of(base + 2 * p * PAIR + core * PAIR, PAIR)
                picked[chunk][:, at : at + PAIR] = qkv_ref[:, pl.ds(start, PAIR)]
                at += PAIR
    picked[-1][...] = out_ref[pl.ds(pl.multiple_of(core * PAIR, PAIR), PAIR), :]


def pick_weights(w_qkv, w_out, core):
    height, columns = w_qkv.shape
    part = columns // 4
    return pl.pallas_call(
        pick_kernel,
        grid_spec=pltpu.PrefetchScalarGridSpec(
            num_scalar_prefetch=1,
            grid=(1,),
            in_specs=[
                pl.BlockSpec(w_qkv.shape, lambda i, *_: (0, 0)),
                pl.BlockSpec(w_out.shape, lambda i, *_: (0, 0)),
            ],
            out_specs=[
                pl.BlockSpec((height, part), lambda i, *_: (0, 0)),
                pl.BlockSpec((height, part), lambda i, *_: (0, 0)),
                pl.BlockSpec((PAIR, w_out.shape[1]), lambda i, *_: (0, 0)),
            ],
        ),
        out_shape=[
            jax.ShapeDtypeStruct((height, part), BF),
            jax.ShapeDtypeStruct((height, part), BF),
            jax.ShapeDtypeStruct((PAIR, w_out.shape[1]), BF),
        ],
        compiler_params=pltpu.CompilerParams(vmem_limit_bytes=16 * 1024 * 1024),
        name="pick_weights",
    )(jnp.reshape(core, (1,)).astype(jnp.int32), w_qkv, w_out)


def gate(value, *others):
    return lax.optimization_barrier((value,) + others)[0]


def pick_groups(array, axis, unit, core):
    size = array.shape[axis]
    picked = [
        jnp.where(
            core == 0,
            lax.slice_in_dim(array, at, at + unit, axis=axis),
            lax.slice_in_dim(array, at + unit, at + 2 * unit, axis=axis),
        )
        for at in range(0, size, 2 * unit)
    ]
    return jnp.concatenate(picked, axis=axis)


def spread_groups(array, axis, unit, core):
    groups = jnp.split(array, array.shape[axis] // unit, axis=axis)
    parts = []
    for group in groups:
        empty = jnp.zeros_like(group)
        parts += [jnp.where(core == 0, group, empty), jnp.where(core == 0, empty, group)]
    return jnp.concatenate(parts, axis=axis)


def in_order(core, own, other, axis):
    first = jnp.where(core == 0, own, other)
    second = jnp.where(core == 0, other, own)
    return jnp.concatenate([first, second], axis=axis)


def xor_blocks(blocks, index):
    odd = (index & 1) == 1
    high = (index & 2) == 2
    near = [jnp.where(odd, blocks[k ^ 1], blocks[k]) for k in range(4)]
    return [jnp.where(high, near[k ^ 2], near[k]) for k in range(4)]


ORDER = (1, 3, 2, 0)
CHUNKS = ((0, 3), (1, 2))


def square(value, step):
    return lax.ppermute(value, "fsdp", [(i, i ^ step) for i in range(4)])


def gather_near(shard):
    return square(shard, 1), square(shard, 2)


def gather_far(near, far):
    half = near.shape[0] // 2
    top = square(far[:half], 1)
    low = square(near[half:], 2)
    return jnp.concatenate([top, low], axis=0)


def chips(value, step, n_vox):
    return lax.ppermute(value, "vox", [(i, i ^ (2 * step)) for i in range(n_vox)])


def reduce_first(normed, grad):
    half = grad.shape[1] // 2
    size = normed.shape[1] // 4
    t = ((0,), (0,))
    to_x = dot(normed[:, : 2 * size], grad[:, :half], t).astype(BF)
    to_y = dot(normed[:, size : 3 * size], grad[:, half:], t).astype(BF)
    return to_x, to_y


def reduce_second(normed, grad, from_x, from_y):
    half = grad.shape[1] // 2
    size = normed.shape[1] // 4
    left, right = grad[:, :half], grad[:, half:]
    one, two = normed[:, :size], normed[:, 2 * size : 3 * size]
    t = ((0,), (0,))
    to_y = (dot(two, left, t) + from_x[size:].astype(F32)).astype(BF)
    to_x = (dot(one, right, t) + from_y[:size].astype(F32)).astype(BF)
    return to_x, to_y


def reduce_kept(normed, grad):
    size = normed.shape[1] // 4
    return dot(normed[:, 3 * size :], grad, ((0,), (0,)))


def on_device(
    tokens, gain, w_qkv, w_out, logit_scale, key_blocks, slot_count, valid_voxels, cotangent
):
    own_tokens = tokens[0]
    own_cotangent = cotangent[0]
    own_rows, model_width = own_tokens.shape
    rows = 2 * own_rows
    own_blocks = key_blocks.shape[1]
    blocks = 2 * own_blocks
    slot_total = key_blocks.shape[2]
    reach = own_blocks // 2
    margin = reach * BLK
    n_vox = lax.axis_size("vox")
    n_fsdp = lax.axis_size("fsdp")
    n_chip = n_vox // 2
    place = lax.axis_index("vox")
    scene = lax.axis_index("fsdp")
    core = place % 2
    chip = place // 2
    fast = n_vox == 8 and n_fsdp == 4
    unit = 128 if fast else 64
    swap = [(i, i ^ 1) for i in range(n_vox)]
    up = [(i, i + 2) for i in range(n_vox - 2)]
    down = [(j, i) for i, j in up]
    part_width = model_width // 2

    def columns_of(array, pairs):
        return jnp.concatenate(
            [
                array[:, base + p * PAIR : base + (p + 1) * PAIR]
                for base in range(0, array.shape[1], part_width)
                for p in pairs
            ],
            axis=1,
        )

    if fast:
        shard_0, shard_1, shard_out = pick_weights(w_qkv, w_out, core)
        near_0, far_0 = gather_near(shard_0)
        diag_0 = gather_far(near_0, far_0)
        near_out, far_out = gather_near(gate(shard_out, near_0, far_0))
        diag_out = gather_far(near_out, far_out)
        near_1, far_1 = gather_near(gate(shard_1, diag_0, near_out, far_out))
        weights_0 = jnp.concatenate([near_0, diag_0, far_0, shard_0], axis=0)
        out_half = jnp.concatenate(
            xor_blocks([shard_out, near_out, far_out, diag_out], scene), axis=0
        )
    else:
        core_qkv = pick_groups(w_qkv, 1, unit, core)
        core_out = pick_groups(w_out, 0, unit, core)
        weights_0, weights_1 = [
            lax.all_gather(columns_of(core_qkv, pairs), "fsdp", axis=0, tiled=True)
            for pairs in CHUNKS
        ]
        out_half = lax.all_gather(core_out, "fsdp", axis=0, tiled=True)

    other_tokens = lax.ppermute(own_tokens, "vox", swap)
    other_cotangent = lax.ppermute(own_cotangent, "vox", swap)
    lists = jnp.concatenate([key_blocks[0], slot_count[0][:, None]], axis=1)
    all_lists = in_order(
        core, lists, lax.ppermute(lists.astype(F32), "vox", swap).astype(jnp.int32), 0
    )
    chip_tokens = in_order(core, own_tokens, other_tokens, 0)
    chip_cotangent = in_order(core, own_cotangent, other_cotangent, 0)

    first_block = chip * blocks
    pool_blocks = blocks + 2 * reach
    window_id = (
        all_lists[:, :slot_total] - first_block + reach
        - 2 * (jnp.arange(blocks, dtype=jnp.int32) // 2)[:, None]
    )
    used = jnp.arange(slot_total, dtype=jnp.int32)[None, :] < all_lists[:, slot_total:]
    hits = jnp.logical_and(
        window_id[:, :, None] == jnp.arange(WINDOW, dtype=jnp.int32), used[:, :, None]
    )
    mult = jnp.sum(hits.astype(jnp.int32), axis=1)
    scene_total = valid_voxels.shape[1]
    pool_ids = first_block - reach + jnp.arange(pool_blocks, dtype=jnp.int32)
    valid = jnp.take(valid_voxels[0], jnp.clip(pool_ids, 0, scene_total - 1))
    group_heads = unit // HD
    scales = pick_groups(logit_scale, 0, group_heads, core)

    wide = chip_tokens.astype(F32)
    inverse = lax.rsqrt(jnp.mean(wide * wide, axis=1, keepdims=True) + EPS)
    normed = (wide * inverse * gain).astype(BF)
    if fast:
        turned = xor_blocks(jnp.split(normed, 4, axis=1), scene)
        normed = jnp.concatenate([turned[k] for k in ORDER], axis=1)

    def project(weight):
        packed = dot(normed, weight).astype(BF)
        width = packed.shape[1] // 3
        before = lax.ppermute(packed[rows - margin :, width:], "vox", up)
        after = lax.ppermute(packed[:margin, width:], "vox", down)
        return packed, before, after

    def heads_of(inputs, upstream, chunk, index):
        p = CHUNKS[chunk][index]
        return attention(
            *inputs, upstream, mult, valid, scales[2 * p : 2 * p + 2], index, len(CHUNKS[chunk]), p
        )

    def return_rims(result):
        return lax.ppermute(result[4], "vox", down), lax.ppermute(result[5], "vox", up)

    def with_rims(grad, back_b, back_a):
        return jnp.concatenate(
            [
                grad[:margin] + back_b.astype(F32),
                grad[margin : rows - margin],
                grad[rows - margin :] + back_a.astype(F32),
            ],
            axis=0,
        ).astype(BF)

    def gradients(results, rims):
        columns = [result[1] for result in results]
        for index in range(2):
            for result, (back_a, back_b) in zip(results, rims):
                columns.append(with_rims(result[2 + index], back_b[index], back_a[index]))
        return jnp.concatenate(columns, axis=1)

    def out_rows(pairs):
        return jnp.concatenate([out_half[p * PAIR : (p + 1) * PAIR] for p in pairs], axis=0)

    def attended(results):
        return jnp.concatenate([result[0] for result in results], axis=1)

    even, low = chip % 2 == 0, chip < 2
    quarter = model_width // 4

    def out_first(out_grad):
        cols = [out_grad[:, k * quarter : (k + 1) * quarter] for k in range(4)]
        kept = [jnp.where(even, cols[k], cols[k + 1]) for k in (0, 2)]
        sent = [jnp.where(even, cols[k + 1], cols[k]) for k in (0, 2)]
        return kept, jnp.concatenate(sent, axis=1).astype(BF)

    def out_second(kept, got):
        kept = [kept[0] + got[:, :quarter].astype(F32), kept[1] + got[:, quarter:].astype(F32)]
        return jnp.where(low, kept[0], kept[1]), jnp.where(low, kept[1], kept[0]).astype(BF)

    def groups_of(part, chunk):
        groups = [part[:, k * PAIR : (k + 1) * PAIR] for k in range(6)]
        sets = ((0, 3, 4), (1, 2, 5)) if chunk == 0 else ((0, 1, 3), (2, 4, 5))
        evens, odds = [jnp.concatenate([groups[k] for k in s], axis=1) for s in sets]
        return jnp.where(even, evens, odds), jnp.where(even, odds, evens).astype(BF)

    def halves_of(kept):
        left, right = kept[:, : 2 * PAIR], kept[:, PAIR:]
        return jnp.where(low, left, right), jnp.where(low, right, left).astype(BF)

    def kept_sum(kept, end_x, end_y, from_x, from_y):
        size = kept.shape[0]
        return kept + jnp.concatenate(
            [
                from_x[:size].astype(F32) + end_y.astype(F32),
                from_y[size:].astype(F32) + end_x.astype(F32),
            ],
            axis=1,
        )

    packed_0 = project(weights_0)
    upstream = dot(chip_cotangent, out_half, ((1,), (1,))).astype(BF)
    first = heads_of(packed_0, upstream, 0, 0)
    rims_first = return_rims(first)
    if fast:
        diag_1 = gather_far(near_1, far_1)
        second_in = gate(upstream, near_1, far_1)
    else:
        second_in = upstream
    second = heads_of(packed_0, second_in, 0, 1)
    rims_second = return_rims(second)
    if fast:
        weights_1 = jnp.concatenate([near_1, diag_1, far_1, shard_1], axis=0)
    packed_1 = project(weights_1)

    att_0 = attended((first, second))
    grad_0 = gradients((first, second), (rims_first, rims_second))
    if fast:
        to_x, to_y = reduce_first(normed, grad_0)
        from_x0, from_y0 = square(to_x, 1), square(to_y, 2)
        rest_0 = gate(grad_0, to_x, to_y)
    else:
        rest_0 = grad_0
    out_grad_0 = dot(att_0, chip_cotangent, ((0,), (0,)))
    mixed_0 = dot(att_0, out_rows(CHUNKS[0]))
    ngrad_0 = dot(rest_0, weights_0, ((1,), (1,)))
    if fast:
        out_kept_0, out_sent = out_first(out_grad_0)
        out_got_0 = chips(out_sent, 1, n_vox)
        kept_0 = reduce_kept(normed, rest_0)
        third_in = gate(upstream, to_x, to_y, out_sent, mixed_0, ngrad_0, kept_0)
    else:
        third_in = upstream
    third = heads_of(packed_1, third_in, 1, 0)
    rims_third = return_rims(third)
    if fast:
        to_x, to_y = reduce_second(normed, rest_0, from_x0, from_y0)
        end_x0, end_y0 = square(to_x, 1), square(to_y, 2)
        out_kept_0, out_sent = out_second(out_kept_0, out_got_0)
        out_got_0 = chips(out_sent, 2, n_vox)
        fourth_in = gate(upstream, to_x, to_y, out_sent)
    else:
        fourth_in = upstream
    fourth = heads_of(packed_1, fourth_in, 1, 1)
    rims_fourth = return_rims(fourth)

    att_1 = attended((third, fourth))
    grad_1 = gradients((third, fourth), (rims_third, rims_fourth))
    if fast:
        part_0 = kept_sum(kept_0, end_x0, end_y0, from_x0, from_y0)
        kept_z0, sent = groups_of(part_0, 0)
        got_z0 = chips(sent, 1, n_vox)
        to_x, to_y = reduce_first(normed, grad_1)
        from_x1, from_y1 = square(to_x, 1), square(to_y, 2)
        rest_1 = gate(grad_1, to_x, to_y)
    else:
        rest_1 = grad_1
    out_grad_1 = dot(att_1, chip_cotangent, ((0,), (0,)))
    mixed_part = mixed_0 + dot(att_1, out_rows(CHUNKS[1]))
    ngrad_part = ngrad_0 + dot(rest_1, weights_1, ((1,), (1,)))
    if fast:
        out_kept_1, out_sent = out_first(out_grad_1)
        out_got_1 = chips(out_sent, 1, n_vox)
        kept_1 = reduce_kept(normed, rest_1)
        kept_z0, sent = halves_of(kept_z0 + got_z0.astype(F32))
        qkv_sum_0 = kept_z0 + chips(sent, 2, n_vox).astype(F32)
        to_x, to_y = reduce_second(normed, rest_1, from_x1, from_y1)
        end_x1, end_y1 = square(to_x, 1), square(to_y, 2)
        out_kept_1, out_sent = out_second(out_kept_1, out_got_1)
        out_got_1 = chips(out_sent, 2, n_vox)
        out_sums = [out_kept_0 + out_got_0.astype(F32), out_kept_1 + out_got_1.astype(F32)]
        part_1 = kept_sum(kept_1, end_x1, end_y1, from_x1, from_y1)
        kept_z1, sent = groups_of(part_1, 1)
        kept_z1, sent = halves_of(kept_z1 + chips(sent, 1, n_vox).astype(F32))
        qkv_sums = [qkv_sum_0, kept_z1 + chips(sent, 2, n_vox).astype(F32)]
    else:
        out_sums = [out_grad_0, out_grad_1]
        qkv_sums = [dot(normed, grad, ((0,), (0,))) for grad in (grad_0, grad_1)]

    scale_parts = {}
    for p, result in zip(CHUNKS[0] + CHUNKS[1], (first, second, third, fourth)):
        scale_parts[p] = jnp.sum(result[6].reshape(8, 2, PAIR), axis=(0, 2))

    mixed_mine = lax.dynamic_slice_in_dim(mixed_part, core * own_rows, own_rows, 0)
    mixed_theirs = lax.dynamic_slice_in_dim(mixed_part, (1 - core) * own_rows, own_rows, 0)
    mixed = (
        own_tokens.astype(F32) + (mixed_mine + lax.ppermute(mixed_theirs, "vox", swap))
    ).astype(BF)

    ngrad_mine = lax.dynamic_slice_in_dim(ngrad_part, core * own_rows, own_rows, 0)
    ngrad_theirs = lax.dynamic_slice_in_dim(ngrad_part, (1 - core) * own_rows, own_rows, 0)
    normed_grad = ngrad_mine + lax.ppermute(ngrad_theirs, "vox", swap)
    if fast:
        held = jnp.split(normed_grad, 4, axis=1)
        normed_grad = jnp.concatenate(
            xor_blocks([held[ORDER.index(k)] for k in range(4)], scene), axis=1
        )

    own_wide = own_tokens.astype(F32)
    own_inverse = lax.rsqrt(jnp.mean(own_wide * own_wide, axis=1, keepdims=True) + EPS)
    gain_grad = jnp.sum(normed_grad * own_wide * own_inverse, axis=0)
    scaled_grad = normed_grad * gain
    token_grad = own_cotangent.astype(F32) + own_inverse * (
        scaled_grad
        - own_wide
        * own_inverse
        * own_inverse
        * jnp.mean(scaled_grad * own_wide, axis=1, keepdims=True)
    )

    scale_part = jnp.concatenate([scale_parts[p] for p in range(len(scale_parts))])
    scale_grad = spread_groups(scale_part, 0, group_heads, core)
    if fast:
        small = jnp.concatenate([gain_grad, scale_grad, jnp.zeros((112,), F32)]).reshape(9, 128)
        for step in (1, 2):
            small = small + square(small, step)
        for step in (1, 2, 4):
            small = small + lax.ppermute(small, "vox", [(i, i ^ step) for i in range(n_vox)])
        small = small.reshape(-1)
        summed_gain, summed_scale = small[:model_width], small[model_width : model_width + HEADS]
    else:
        summed_gain, summed_scale = lax.psum((gain_grad, scale_grad), ("vox", "fsdp"))

    if fast:
        by_pair = {}
        for pairs, total in zip(CHUNKS, out_sums):
            for i, p in enumerate(pairs):
                by_pair[p] = total[i * PAIR : (i + 1) * PAIR]
        turned = xor_blocks([by_pair[p] for p in range(4)], scene)
        out_sum = turned[0]
        for step in (1, 2, 3):
            out_sum = out_sum + square(turned[step].astype(BF), step).astype(F32)
        half = out_sum.shape[1] // 2
        first, second = out_sum[:, :half], out_sum[:, half:]
        out_other = lax.ppermute(jnp.where(core == 0, second, first), "vox", swap)
        summed_out = in_order(core, jnp.where(core == 0, first, second), out_other, 0)

        a0, a1 = qkv_sums[0][:, :PAIR], qkv_sums[0][:, PAIR:]
        b0, b1 = qkv_sums[1][:, :PAIR], qkv_sums[1][:, PAIR:]

        def by_chip(options):
            value = options[3]
            for k in range(3):
                value = jnp.where(chip == k, options[k], value)
            return value

        g0 = by_chip((a0, a0, b1, b0))
        g1 = by_chip((b0, a1, a0, b1))
        g2 = by_chip((b1, b0, a1, a1))
        got = lax.ppermute(jnp.where(core == 0, g2, g0), "vox", swap)
        summed_qkv = jnp.concatenate(
            [
                jnp.where(core == 0, g0, g1),
                got,
                jnp.where(core == 0, g1, g2),
            ],
            axis=1,
        )
    else:
        by_pair = {}
        cols = {}
        for pairs, out_total, qkv_total in zip(CHUNKS, out_sums, qkv_sums):
            for i, p in enumerate(pairs):
                by_pair[p] = out_total[i * PAIR : (i + 1) * PAIR]
                for j in range(3):
                    at = (2 * j + i) * PAIR
                    cols[4 * j + p] = qkv_total[:, at : at + PAIR]
        out_total = jnp.concatenate([by_pair[p] for p in range(4)], axis=0)
        qkv_total = jnp.concatenate([cols[k] for k in range(12)], axis=1)
        out_total = spread_groups(out_total, 0, unit, core)
        qkv_total = lax.psum_scatter(qkv_total, "fsdp", scatter_dimension=0, tiled=True)
        qkv_total = spread_groups(qkv_total, 1, unit, core)
        summed_qkv = lax.psum_scatter(qkv_total, "vox", scatter_dimension=1, tiled=True)
        out_total = lax.psum_scatter(out_total, "fsdp", scatter_dimension=0, tiled=True)
        summed_out = lax.psum_scatter(out_total, "vox", scatter_dimension=1, tiled=True)

    return (
        mixed[None],
        token_grad.astype(BF)[None],
        summed_qkv,
        summed_out,
        summed_gain,
        summed_scale,
    )


def solution(mesh):
    return jax.shard_map(
        on_device,
        mesh=mesh,
        in_specs=(
            P("fsdp", "vox", None),
            P(),
            P("fsdp", None),
            P("fsdp", None),
            P(),
            P("fsdp", "vox", None),
            P("fsdp", "vox"),
            P("fsdp", None),
            P("fsdp", "vox", None),
        ),
        out_specs=(
            P("fsdp", "vox", None),
            P("fsdp", "vox", None),
            P("fsdp", "vox"),
            P("fsdp", "vox"),
            P(),
            P(),
        ),
        check_vma=False,
    )
```

```python
import functools

import jax
import jax.numpy as jnp
from jax import lax
from jax.experimental import pallas as pl
from jax.experimental.pallas import tpu as pltpu
from jax.sharding import PartitionSpec as P

HEADS = 16
HD = 64
PAIR = 2 * HD
BLK = 64
WINDOW = 8
EPS = 1e-06
LOG2E = 1.4426950408889634
BF = jnp.bfloat16
F32 = jnp.float32


def dot(a, b, dims=((1,), (0,))):
    return lax.dot_general(a, b, (dims, ((), ())), preferred_element_type=F32)


def head_sums(x, same_head):
    high = x.astype(BF)
    low = (x - high.astype(F32)).astype(BF)
    return dot(high, same_head) + dot(low, same_head)


def unit_rows(x, same_head):
    length = jnp.sqrt(head_sums(x * x, same_head) + EPS)
    return x / length, length


def unit_back(unit, length, grad, same_head):
    return (grad - unit * head_sums(unit * grad, same_head)) / length


def attention_kernel(
    mult_ref, valid_ref, scale_ref, even_ref,
    q_ref, k_ref, v_ref, k1_ref, v1_ref, k2_ref, v2_ref, u_ref,
    att_ref, dq_ref, dk_ref, dv_ref, rim1_ref, rim2_ref, ds_ref,
    k_unit, k_len, k_low, k_turn, v_low, v_turn, mult, s_ref, g_ref, e_ref, w_low, c_low, dk, dv,
):
    rows = q_ref.shape[0]
    margin = k1_ref.shape[0]
    even = even_ref[0] == 1
    pool = rows + 2 * margin
    reach = margin // BLK
    steps = rows // PAIR
    span = WINDOW * BLK
    pair = pl.program_id(0)

    lane = lax.broadcasted_iota(jnp.int32, (BLK, PAIR), 1)
    row = lax.broadcasted_iota(jnp.int32, (BLK, PAIR), 0)
    head_a = lax.broadcasted_iota(jnp.int32, (PAIR, PAIR), 0) < HD
    head_b = lax.broadcasted_iota(jnp.int32, (PAIR, PAIR), 1) < HD
    same_head = jnp.where(head_a == head_b, 1.0, 0.0).astype(BF)
    first_lanes = head_b

    @pl.when(pair == 0)
    def _():
        for t in range(steps):
            for w in range(WINDOW):
                count = jnp.where(lane < BLK, mult_ref[2 * t, w], mult_ref[2 * t + 1, w])
                live = row < valid_ref[2 * t + w]
                mult[t, w * BLK : (w + 1) * BLK, :] = jnp.where(live, count, 0).astype(F32)

    def split_heads(x):
        return jnp.concatenate(
            [jnp.where(first_lanes, x, 0.0), jnp.where(first_lanes, 0.0, x)], axis=0
        ).astype(BF)

    def take(at, keys, values):
        unit, length = unit_rows(keys.astype(F32), same_head)
        place = slice(at, at + keys.shape[0])
        k_unit[place, :] = unit
        k_len[place, :] = length
        k_low[place, :] = unit.astype(BF)
        v_low[place, :] = values

    for part in range(0, margin, BLK):
        here = slice(part, part + BLK)
        k1, k2 = k1_ref[here, :].astype(F32), k2_ref[here, :].astype(F32)
        v1, v2 = v1_ref[here, :].astype(F32), v2_ref[here, :].astype(F32)
        take(part, jnp.where(even, k2, k1), jnp.where(even, v2, v1).astype(BF))
        take(margin + rows + part, jnp.where(even, k1, k2), jnp.where(even, v1, v2).astype(BF))
    for part in range(0, rows, PAIR):
        here = slice(part, part + PAIR)
        take(margin + part, k_ref[here, :], v_ref[here, :])
    for part in range(0, pool, 128):
        place = slice(part, part + 128)
        k_turn[:, place] = jnp.transpose(k_low[place, :].astype(F32)).astype(BF)
        v_turn[:, place] = jnp.transpose(v_low[place, :].astype(F32)).astype(BF)

    dk[...] = jnp.zeros_like(dk)
    dv[...] = jnp.zeros_like(dv)
    wide_lane = lax.broadcasted_iota(jnp.int32, (1, 2 * PAIR), 1)
    scale = jnp.where(wide_lane < PAIR, scale_ref[2 * pair], scale_ref[2 * pair + 1])
    ds = jnp.zeros((8, 2 * PAIR), F32)

    for t in range(steps):
        own = slice(t * PAIR, (t + 1) * PAIR)
        window = slice(t * PAIR, t * PAIR + span)
        q_unit, q_len = unit_rows(q_ref[own, :].astype(F32), same_head)
        q_split = split_heads(q_unit)
        live = jnp.concatenate(
            [row < valid_ref[2 * t + reach], row < valid_ref[2 * t + 1 + reach]], axis=0
        )
        u_split = split_heads(jnp.where(live, u_ref[own, :].astype(F32), 0.0))
        s_ref[...] = dot(k_low[window, :], q_split, ((1,), (1,)))
        g_ref[...] = dot(v_low[window, :], u_split, ((1,), (1,)))

        def mult_of(part):
            half = mult[t, part, :]
            return jnp.concatenate([half, half], axis=1)

        parts = [slice(i, i + 32) for i in range(0, span, 32)]
        peak = jnp.full((8, 2 * PAIR), -1e30, F32)
        stretch = scale * LOG2E
        for part in parts:
            raised = jnp.where(mult_of(part) > 0.0, s_ref[part, :] * stretch, -1e30)
            peak = jnp.maximum(peak, jnp.max(raised.reshape(4, 8, 2 * PAIR), axis=0))
        peak = jnp.max(peak, axis=0, keepdims=True)
        total = jnp.zeros((8, 2 * PAIR), F32)
        centre = jnp.zeros((8, 2 * PAIR), F32)
        for part in parts:
            count = mult_of(part)
            shifted = jnp.where(count > 0.0, s_ref[part, :] * stretch - peak, -1e30)
            e = jnp.exp2(shifted) * count
            e_ref[part, :] = e
            total = total + jnp.sum(e.reshape(4, 8, 2 * PAIR), axis=0)
            centre = centre + jnp.sum((e * g_ref[part, :]).reshape(4, 8, 2 * PAIR), axis=0)
        share = 1.0 / jnp.sum(total, axis=0, keepdims=True)
        centre = jnp.sum(centre, axis=0, keepdims=True) * share
        for part in parts:
            w = e_ref[part, :] * share
            w_low[part, :] = w.astype(BF)
            sg = w * (g_ref[part, :] - centre)
            ds = ds + jnp.sum((sg * s_ref[part, :]).reshape(4, 8, 2 * PAIR), axis=0)
            c_low[part, :] = (sg * scale).astype(BF)

        def by_query(turned):
            return jnp.transpose(
                jnp.concatenate([turned[:HD, :PAIR], turned[HD:, PAIR:]], axis=0)
            )

        mixed = by_query(dot(v_turn[:, window], w_low[...]))
        att_ref[own, :] = jnp.where(live, mixed, 0.0).astype(BF)
        q_grad = by_query(dot(k_turn[:, window], c_low[...]))
        dq_ref[own, :] = unit_back(q_unit, q_len, q_grad, same_head).astype(BF)
        dv[window, :] += dot(w_low[...], u_split)
        dk[window, :] += dot(c_low[...], q_split)

    def key_grad(part):
        place = slice(part, part + BLK)
        return unit_back(k_unit[place, :], k_len[place, :], dk[place, :], same_head)

    for part in range(0, rows, BLK):
        here = slice(part, part + BLK)
        dk_ref[here, :] = key_grad(margin + part)
        dv_ref[here, :] = dv[margin + part : margin + part + BLK, :]
    for part in range(0, margin, BLK):
        here = slice(part, part + BLK)
        far = margin + rows + part
        kb, ka = key_grad(part), key_grad(far)
        vb, va = dv[part : part + BLK, :], dv[far : far + BLK, :]
        rim1_ref[0, here, :] = jnp.where(even, ka, kb).astype(BF)
        rim1_ref[1, here, :] = jnp.where(even, va, vb).astype(BF)
        rim2_ref[0, here, :] = jnp.where(even, kb, ka).astype(BF)
        rim2_ref[1, here, :] = jnp.where(even, vb, va).astype(BF)
    ds_ref[0, :, :] = ds


def attention(packed, first, second, upstream, mult, valid, scales, even, pairs):
    rows, width3 = packed.shape
    width = width3 // 3
    margin = first.shape[0]
    pool = rows + 2 * margin
    count = len(pairs)
    stride = pairs[1] - pairs[0]
    steps = rows // PAIR
    span = WINDOW * BLK

    def at(offset):
        return lambda p, *_: (0, offset + p)

    return pl.pallas_call(
        attention_kernel,
        grid_spec=pltpu.PrefetchScalarGridSpec(
            num_scalar_prefetch=4,
            grid=(count,),
            in_specs=[
                pl.BlockSpec((rows, PAIR), at(0)),
                pl.BlockSpec((rows, PAIR), at(count)),
                pl.BlockSpec((rows, PAIR), at(2 * count)),
                pl.BlockSpec((margin, PAIR), at(0)),
                pl.BlockSpec((margin, PAIR), at(count)),
                pl.BlockSpec((margin, PAIR), at(0)),
                pl.BlockSpec((margin, PAIR), at(count)),
                pl.BlockSpec((rows, PAIR), lambda p, *_: (0, pairs[0] + stride * p)),
            ],
            out_specs=[
                pl.BlockSpec((rows, PAIR), at(0)),
                pl.BlockSpec((rows, PAIR), at(0)),
                pl.BlockSpec((rows, PAIR), at(0)),
                pl.BlockSpec((rows, PAIR), at(0)),
                pl.BlockSpec((2, margin, PAIR), lambda p, *_: (0, 0, p)),
                pl.BlockSpec((2, margin, PAIR), lambda p, *_: (0, 0, p)),
                pl.BlockSpec((1, 8, 2 * PAIR), lambda p, *_: (p, 0, 0)),
            ],
            scratch_shapes=[
                pltpu.VMEM((pool, PAIR), F32),
                pltpu.VMEM((pool, PAIR), F32),
                pltpu.VMEM((pool, PAIR), BF),
                pltpu.VMEM((PAIR, pool), BF),
                pltpu.VMEM((pool, PAIR), BF),
                pltpu.VMEM((PAIR, pool), BF),
                pltpu.VMEM((steps, span, PAIR), F32),
                pltpu.VMEM((span, 2 * PAIR), F32),
                pltpu.VMEM((span, 2 * PAIR), F32),
                pltpu.VMEM((span, 2 * PAIR), F32),
                pltpu.VMEM((span, 2 * PAIR), BF),
                pltpu.VMEM((span, 2 * PAIR), BF),
                pltpu.VMEM((pool, PAIR), F32),
                pltpu.VMEM((pool, PAIR), F32),
            ],
        ),
        out_shape=[
            jax.ShapeDtypeStruct((rows, width), BF),
            jax.ShapeDtypeStruct((rows, width), BF),
            jax.ShapeDtypeStruct((rows, width), F32),
            jax.ShapeDtypeStruct((rows, width), F32),
            jax.ShapeDtypeStruct((2, margin, width), BF),
            jax.ShapeDtypeStruct((2, margin, width), BF),
            jax.ShapeDtypeStruct((count, 8, 2 * PAIR), F32),
        ],
        compiler_params=pltpu.CompilerParams(vmem_limit_bytes=40 * 1024 * 1024),
        cost_estimate=pl.CostEstimate(
            flops=8 * 2 * 6 * count * steps * span * 256 * 128,
            bytes_accessed=rows * width * 20,
            transcendentals=count * steps * span * 256,
        ),
        name="block_attention",
    )(mult, valid, scales, even, packed, packed, packed, first, first, second, second, upstream)


def pick_kernel(core_ref, qkv_ref, out_ref, first_ref, second_ref):
    core = core_ref[0]
    for ref, pairs in zip((first_ref, second_ref), CHUNKS):
        at = 0
        for base in range(0, qkv_ref.shape[1], 8 * PAIR):
            for p in pairs:
                start = pl.multiple_of(base + 2 * p * PAIR + core * PAIR, PAIR)
                ref[:, at : at + PAIR] = qkv_ref[:, pl.ds(start, PAIR)]
                at += PAIR
    half = out_ref.shape[1] // 2
    rows = out_ref[pl.ds(pl.multiple_of(core * PAIR, PAIR), PAIR), :]
    first_ref[:PAIR, at:] = rows[:, :half]
    first_ref[PAIR:, at:] = rows[:, half:]


def pick_weights(w_qkv, w_out, core):
    height, columns = w_qkv.shape
    part = columns // 4
    wide = part + w_out.shape[1] // 2
    return pl.pallas_call(
        pick_kernel,
        grid_spec=pltpu.PrefetchScalarGridSpec(
            num_scalar_prefetch=1,
            grid=(1,),
            in_specs=[
                pl.BlockSpec(w_qkv.shape, lambda i, *_: (0, 0)),
                pl.BlockSpec(w_out.shape, lambda i, *_: (0, 0)),
            ],
            out_specs=[
                pl.BlockSpec((height, wide), lambda i, *_: (0, 0)),
                pl.BlockSpec((height, part), lambda i, *_: (0, 0)),
            ],
        ),
        out_shape=[
            jax.ShapeDtypeStruct((height, wide), BF),
            jax.ShapeDtypeStruct((height, part), BF),
        ],
        compiler_params=pltpu.CompilerParams(vmem_limit_bytes=16 * 1024 * 1024),
        name="pick_weights",
    )(jnp.reshape(core, (1,)).astype(jnp.int32), w_qkv, w_out)


def gate(value, *others):
    return lax.optimization_barrier((value,) + others)[0]


def pick_groups(array, axis, unit, core):
    size = array.shape[axis]
    picked = [
        jnp.where(
            core == 0,
            lax.slice_in_dim(array, at, at + unit, axis=axis),
            lax.slice_in_dim(array, at + unit, at + 2 * unit, axis=axis),
        )
        for at in range(0, size, 2 * unit)
    ]
    return jnp.concatenate(picked, axis=axis)


def spread_groups(array, axis, unit, core):
    groups = jnp.split(array, array.shape[axis] // unit, axis=axis)
    parts = []
    for group in groups:
        empty = jnp.zeros_like(group)
        parts += [jnp.where(core == 0, group, empty), jnp.where(core == 0, empty, group)]
    return jnp.concatenate(parts, axis=axis)


def in_order(core, own, other, axis):
    first = jnp.where(core == 0, own, other)
    second = jnp.where(core == 0, other, own)
    return jnp.concatenate([first, second], axis=axis)


def xor_blocks(blocks, index):
    odd = (index & 1) == 1
    high = (index & 2) == 2
    near = [jnp.where(odd, blocks[k ^ 1], blocks[k]) for k in range(4)]
    return [jnp.where(high, near[k ^ 2], near[k]) for k in range(4)]


ORDER = (1, 3, 2, 0)
CHUNKS = ((0, 3), (1, 2))


def square(value, step):
    return lax.ppermute(value, "fsdp", [(i, i ^ step) for i in range(4)])


def gather_near(shard):
    return square(shard, 1), square(shard, 2)


def gather_far(near, far):
    half = near.shape[0] // 2
    top = square(far[:half], 1)
    low = square(near[half:], 2)
    return jnp.concatenate([top, low], axis=0)


def chips(value, step, n_vox):
    return lax.ppermute(value, "vox", [(i, i ^ (2 * step)) for i in range(n_vox)])


def stacked(block):
    half = block.shape[1] // 2
    return jnp.concatenate([block[:, :half], block[:, half:]], axis=0)


def reduce_terms(normed, grad, place, side, extra=None):
    half = grad.shape[1] // 2
    size = normed.shape[1] // 4
    columns = grad[:, side * half : (side + 1) * half]
    value = dot(normed[:, place.start * size : place.stop * size], columns, ((0,), (0,)))
    if extra is None:
        return value
    more = jnp.concatenate([extra[k] for k in range(place.start, place.stop)], axis=0)
    half = more.shape[1] // 2
    return jnp.concatenate([value, more[:, side * half : (side + 1) * half]], axis=1)


def reduce_first(normed, grad, extra=None):
    return (
        reduce_terms(normed, grad, slice(0, 2), 0, extra).astype(BF),
        reduce_terms(normed, grad, slice(1, 3), 1, extra).astype(BF),
    )


def reduce_second(normed, grad, from_x, from_y, extra=None):
    size = normed.shape[1] // 4
    to_y = reduce_terms(normed, grad, slice(2, 3), 0, extra) + from_x[size:].astype(F32)
    to_x = reduce_terms(normed, grad, slice(0, 1), 1, extra) + from_y[:size].astype(F32)
    return to_x.astype(BF), to_y.astype(BF)


def reduce_kept(normed, grad, from_x, from_y, extra=None):
    size = normed.shape[1] // 4
    return (
        reduce_terms(normed, grad, slice(3, 4), 0, extra) + from_x[:size].astype(F32),
        reduce_terms(normed, grad, slice(3, 4), 1, extra) + from_y[size:].astype(F32),
    )


def on_device(
    tokens, gain, w_qkv, w_out, logit_scale, key_blocks, slot_count, valid_voxels, cotangent
):
    own_tokens = tokens[0]
    own_cotangent = cotangent[0]
    own_rows, model_width = own_tokens.shape
    rows = 2 * own_rows
    own_blocks = key_blocks.shape[1]
    blocks = 2 * own_blocks
    slot_total = key_blocks.shape[2]
    reach = own_blocks // 2
    margin = reach * BLK
    n_vox = lax.axis_size("vox")
    n_fsdp = lax.axis_size("fsdp")
    n_chip = n_vox // 2
    place = lax.axis_index("vox")
    scene = lax.axis_index("fsdp")
    core = place % 2
    chip = place // 2
    fast = n_vox == 8 and n_fsdp == 4
    unit = 128 if fast else 64
    swap = [(i, i ^ 1) for i in range(n_vox)]
    even, low = chip % 2 == 0, chip < 2
    even_flag = jnp.reshape(even, (1,)).astype(jnp.int32)
    near_chips = [(i, i ^ 2) for i in range(n_vox)]
    far_chips = []
    for i in range(n_vox):
        to = i // 2 + (1 if i // 2 % 2 else -1)
        far_chips.append((i, 2 * to + i % 2 if 0 <= to < n_chip else i))
    part_width = model_width // 2

    def columns_of(array, pairs):
        return jnp.concatenate(
            [
                array[:, base + p * PAIR : base + (p + 1) * PAIR]
                for base in range(0, array.shape[1], part_width)
                for p in pairs
            ],
            axis=1,
        )

    if fast:
        shard, shard_1 = pick_weights(w_qkv, w_out, core)
        near, far = gather_near(shard)
        diag = gather_far(near, far)
        weights_1 = lax.all_gather(gate(shard_1, near, far), "fsdp", axis=0, tiled=True)
        turned = xor_blocks(jnp.split(weights_1, 4, axis=0), scene)
        weights_1 = jnp.concatenate([turned[k] for k in ORDER], axis=0)
        wide = shard_1.shape[1]
        weights_0 = jnp.concatenate([block[:, :wide] for block in (near, diag, far, shard)], axis=0)
        out_blocks = [
            jnp.concatenate([block[:PAIR, wide:], block[PAIR:, wide:]], axis=1)
            for block in (shard, near, far, diag)
        ]
        out_half = jnp.concatenate(xor_blocks(out_blocks, scene), axis=0)
    else:
        core_qkv = pick_groups(w_qkv, 1, unit, core)
        core_out = pick_groups(w_out, 0, unit, core)
        weights_0, weights_1 = [
            lax.all_gather(columns_of(core_qkv, pairs), "fsdp", axis=0, tiled=True)
            for pairs in CHUNKS
        ]
        out_half = lax.all_gather(core_out, "fsdp", axis=0, tiled=True)

    other_tokens = lax.ppermute(own_tokens, "vox", swap)
    other_cotangent = lax.ppermute(own_cotangent, "vox", swap)
    lists = jnp.concatenate([key_blocks[0], slot_count[0][:, None]], axis=1)
    all_lists = in_order(
        core, lists, lax.ppermute(lists.astype(F32), "vox", swap).astype(jnp.int32), 0
    )
    chip_tokens = in_order(core, own_tokens, other_tokens, 0)
    chip_cotangent = in_order(core, own_cotangent, other_cotangent, 0)

    first_block = chip * blocks
    pool_blocks = blocks + 2 * reach
    window_id = (
        all_lists[:, :slot_total] - first_block + reach
        - 2 * (jnp.arange(blocks, dtype=jnp.int32) // 2)[:, None]
    )
    used = jnp.arange(slot_total, dtype=jnp.int32)[None, :] < all_lists[:, slot_total:]
    hits = jnp.logical_and(
        window_id[:, :, None] == jnp.arange(WINDOW, dtype=jnp.int32), used[:, :, None]
    )
    mult = jnp.sum(hits.astype(jnp.int32), axis=1)
    scene_total = valid_voxels.shape[1]
    pool_ids = first_block - reach + jnp.arange(pool_blocks, dtype=jnp.int32)
    valid = jnp.take(valid_voxels[0], jnp.clip(pool_ids, 0, scene_total - 1))
    group_heads = unit // HD
    scales = pick_groups(logit_scale, 0, group_heads, core)

    wide = chip_tokens.astype(F32)
    inverse = lax.rsqrt(jnp.mean(wide * wide, axis=1, keepdims=True) + EPS)
    normed = (wide * inverse * gain).astype(BF)
    if fast:
        turned = xor_blocks(jnp.split(normed, 4, axis=1), scene)
        normed = jnp.concatenate([turned[k] for k in ORDER], axis=1)

    def pairings(first, second):
        return lax.ppermute(first, "vox", near_chips), lax.ppermute(second, "vox", far_chips)

    def project(weight):
        packed = dot(normed, weight).astype(BF)
        width = packed.shape[1] // 3
        top, bottom = packed[:margin, width:], packed[rows - margin :, width:]
        return (packed,) + pairings(jnp.where(even, bottom, top), jnp.where(even, top, bottom))

    def heads_of(inputs, upstream, pairs):
        chunk_scales = jnp.concatenate([scales[2 * p : 2 * p + 2] for p in pairs])
        return attention(*inputs, upstream, mult, valid, chunk_scales, even_flag, pairs)

    def with_rims(grad, first, second):
        first, second = first.astype(F32), second.astype(F32)
        return jnp.concatenate(
            [
                grad[:margin] + jnp.where(even, second, first),
                grad[margin : rows - margin],
                grad[rows - margin :] + jnp.where(even, first, second),
            ],
            axis=0,
        ).astype(BF)

    def gradients(result, rims):
        return jnp.concatenate(
            [result[1]]
            + [with_rims(result[2 + i], rims[0][i], rims[1][i]) for i in range(2)],
            axis=1,
        )

    def out_rows(pairs):
        return jnp.concatenate([out_half[p * PAIR : (p + 1) * PAIR] for p in pairs], axis=0)

    def groups_of(left, right, chunk):
        half = 3 * PAIR
        groups = [left[:, k * PAIR : (k + 1) * PAIR] for k in range(3)]
        groups += [right[:, k * PAIR : (k + 1) * PAIR] for k in range(3)]
        sets = ((0, 3, 4), (1, 2, 5)) if chunk == 0 else ((0, 1, 3), (2, 4, 5))
        evens = jnp.concatenate([groups[k] for k in sets[0]] + [left[:, half:]], axis=1)
        odds = jnp.concatenate([groups[k] for k in sets[1]] + [right[:, half:]], axis=1)
        return jnp.where(even, evens, odds), jnp.where(even, odds, evens).astype(BF)

    def halves_of(kept):
        left, right = kept[:, : 2 * PAIR], kept[:, PAIR : 3 * PAIR]
        if kept.shape[1] > 3 * PAIR:
            more = kept[:, 3 * PAIR :]
            cut = more.shape[0] // 2
            left = jnp.concatenate([left, more[:cut]], axis=0)
            right = jnp.concatenate([right, more[cut:]], axis=0)
        return jnp.where(low, left, right), jnp.where(low, right, left).astype(BF)

    packed_0 = project(weights_0)
    upstream = dot(chip_cotangent, out_half, ((1,), (1,))).astype(BF)
    first = heads_of(packed_0, upstream, CHUNKS[0])
    rims_0 = pairings(first[4], first[5])
    packed_1 = project(gate(weights_1, first[4], first[5]) if fast else weights_1)
    out_grad_0 = dot(first[0], chip_cotangent, ((0,), (0,)))
    mixed_0 = dot(first[0], out_rows(CHUNKS[0]))
    grad_0 = gradients(first, rims_0)
    if fast:
        to_x, to_y = reduce_first(normed, grad_0)
        from_x0, from_y0 = square(to_x, 1), square(to_y, 2)
        second_in = gate(upstream, to_x, to_y, out_grad_0, mixed_0)
    else:
        second_in = upstream
    second = heads_of(packed_1, second_in, CHUNKS[1])
    rims_1 = pairings(second[4], second[5])
    grad_1 = gradients(second, rims_1)
    out_grad_1 = dot(second[0], chip_cotangent, ((0,), (0,)))
    mixed_part = mixed_0 + dot(second[0], out_rows(CHUNKS[1]))
    if fast:
        grad_0 = gate(grad_0, second[4], second[5])
        to_x, to_y = reduce_second(normed, grad_0, from_x0, from_y0)
        end_x, end_y = square(to_x, 1), square(to_y, 2)
        left, right = reduce_kept(normed, grad_0, from_x0, from_y0)
        blocks_of = {}
        for pairs, value in zip(CHUNKS, (out_grad_0, out_grad_1)):
            for i, p in enumerate(pairs):
                blocks_of[p] = value[i * PAIR : (i + 1) * PAIR]
        turned = xor_blocks([blocks_of[p] for p in range(4)], scene)
        extra = [stacked(turned[k]) for k in ORDER]
        to_x, to_y = reduce_first(normed, grad_1, extra)
        from_x1, from_y1 = square(to_x, 1), square(to_y, 2)
        left, right = left + end_y.astype(F32), right + end_x.astype(F32)
        left, right, grad_0, grad_1, mixed_part, _, _ = lax.optimization_barrier(
            (left, right, grad_0, grad_1, mixed_part, to_x, to_y)
        )
        kept_0, sent = groups_of(left, right, 0)
        got = chips(sent, 1, n_vox)
        ngrad_part = dot(grad_0, weights_0, ((1,), (1,))) + dot(grad_1, weights_1, ((1,), (1,)))
        to_x, to_y = reduce_second(normed, grad_1, from_x1, from_y1, extra)
        end_x, end_y = square(to_x, 1), square(to_y, 2)
        left, right = reduce_kept(normed, grad_1, from_x1, from_y1, extra)
        kept_0, sent = halves_of(gate(kept_0 + got.astype(F32), to_x, to_y))
        qkv_sum_0 = kept_0 + chips(sent, 2, n_vox).astype(F32)
        kept_1, sent = groups_of(left + end_y.astype(F32), right + end_x.astype(F32), 1)
        kept_1, sent = halves_of(kept_1 + chips(sent, 1, n_vox).astype(F32))
        kept_1 = kept_1 + chips(sent, 2, n_vox).astype(F32)
        height = normed.shape[1] // 4
        qkv_sums = [qkv_sum_0, kept_1[:height]]
        out_sum = kept_1[height:]
    else:
        out_sums = [out_grad_0, out_grad_1]
        qkv_sums = [dot(normed, grad, ((0,), (0,))) for grad in (grad_0, grad_1)]
        ngrad_part = dot(grad_0, weights_0, ((1,), (1,))) + dot(grad_1, weights_1, ((1,), (1,)))

    scale_parts = {}
    for pairs, result in zip(CHUNKS, (first, second)):
        sums = jnp.sum(result[6].reshape(2, 8, 2, PAIR), axis=(1, 3))
        for i, p in enumerate(pairs):
            scale_parts[p] = sums[i]

    mixed_mine = lax.dynamic_slice_in_dim(mixed_part, core * own_rows, own_rows, 0)
    mixed_theirs = lax.dynamic_slice_in_dim(mixed_part, (1 - core) * own_rows, own_rows, 0)
    mixed = (
        own_tokens.astype(F32) + (mixed_mine + lax.ppermute(mixed_theirs, "vox", swap))
    ).astype(BF)

    ngrad_mine = lax.dynamic_slice_in_dim(ngrad_part, core * own_rows, own_rows, 0)
    ngrad_theirs = lax.dynamic_slice_in_dim(ngrad_part, (1 - core) * own_rows, own_rows, 0)
    normed_grad = ngrad_mine + lax.ppermute(ngrad_theirs, "vox", swap)
    if fast:
        held = jnp.split(normed_grad, 4, axis=1)
        normed_grad = jnp.concatenate(
            xor_blocks([held[ORDER.index(k)] for k in range(4)], scene), axis=1
        )

    own_wide = own_tokens.astype(F32)
    own_inverse = lax.rsqrt(jnp.mean(own_wide * own_wide, axis=1, keepdims=True) + EPS)
    gain_grad = jnp.sum(normed_grad * own_wide * own_inverse, axis=0)
    scaled_grad = normed_grad * gain
    token_grad = own_cotangent.astype(F32) + own_inverse * (
        scaled_grad
        - own_wide
        * own_inverse
        * own_inverse
        * jnp.mean(scaled_grad * own_wide, axis=1, keepdims=True)
    )

    scale_part = jnp.concatenate([scale_parts[p] for p in range(len(scale_parts))])
    scale_grad = spread_groups(scale_part, 0, group_heads, core)
    if fast:
        small = jnp.concatenate([gain_grad, scale_grad, jnp.zeros((112,), F32)]).reshape(9, 128)
        every = lax.all_gather(small, ("vox", "fsdp"), axis=0, tiled=False)
        small = jnp.sum(every, axis=0)
        small = small.reshape(-1)
        summed_gain, summed_scale = small[:model_width], small[model_width : model_width + HEADS]
    else:
        summed_gain, summed_scale = lax.psum((gain_grad, scale_grad), ("vox", "fsdp"))

    if fast:
        half = out_sum.shape[1] // 2
        first, second = out_sum[:, :half], out_sum[:, half:]
        out_other = lax.ppermute(jnp.where(core == 0, second, first), "vox", swap)
        summed_out = in_order(core, jnp.where(core == 0, first, second), out_other, 0)

        a0, a1 = qkv_sums[0][:, :PAIR], qkv_sums[0][:, PAIR:]
        b0, b1 = qkv_sums[1][:, :PAIR], qkv_sums[1][:, PAIR:]

        def by_chip(options):
            value = options[3]
            for k in range(3):
                value = jnp.where(chip == k, options[k], value)
            return value

        g0 = by_chip((a0, a0, b1, b0))
        g1 = by_chip((b0, a1, a0, b1))
        g2 = by_chip((b1, b0, a1, a1))
        got = lax.ppermute(jnp.where(core == 0, g2, g0), "vox", swap)
        summed_qkv = jnp.concatenate(
            [
                jnp.where(core == 0, g0, g1),
                got,
                jnp.where(core == 0, g1, g2),
            ],
            axis=1,
        )
    else:
        by_pair = {}
        cols = {}
        for pairs, out_total, qkv_total in zip(CHUNKS, out_sums, qkv_sums):
            for i, p in enumerate(pairs):
                by_pair[p] = out_total[i * PAIR : (i + 1) * PAIR]
                for j in range(3):
                    at = (2 * j + i) * PAIR
                    cols[4 * j + p] = qkv_total[:, at : at + PAIR]
        out_total = jnp.concatenate([by_pair[p] for p in range(4)], axis=0)
        qkv_total = jnp.concatenate([cols[k] for k in range(12)], axis=1)
        out_total = spread_groups(out_total, 0, unit, core)
        qkv_total = lax.psum_scatter(qkv_total, "fsdp", scatter_dimension=0, tiled=True)
        qkv_total = spread_groups(qkv_total, 1, unit, core)
        summed_qkv = lax.psum_scatter(qkv_total, "vox", scatter_dimension=1, tiled=True)
        out_total = lax.psum_scatter(out_total, "fsdp", scatter_dimension=0, tiled=True)
        summed_out = lax.psum_scatter(out_total, "vox", scatter_dimension=1, tiled=True)

    return (
        mixed[None],
        token_grad.astype(BF)[None],
        summed_qkv,
        summed_out,
        summed_gain,
        summed_scale,
    )


def solution(mesh):
    return jax.shard_map(
        on_device,
        mesh=mesh,
        in_specs=(
            P("fsdp", "vox", None),
            P(),
            P("fsdp", None),
            P("fsdp", None),
            P(),
            P("fsdp", "vox", None),
            P("fsdp", "vox"),
            P("fsdp", None),
            P("fsdp", "vox", None),
        ),
        out_specs=(
            P("fsdp", "vox", None),
            P("fsdp", "vox", None),
            P("fsdp", "vox"),
            P("fsdp", "vox"),
            P(),
            P(),
        ),
        check_vma=False,
    )
```

```python
import functools

import jax
import jax.numpy as jnp
from jax import lax
from jax.experimental import pallas as pl
from jax.experimental.pallas import tpu as pltpu
from jax.sharding import PartitionSpec as P

HEADS = 16
HD = 64
PAIR = 2 * HD
BLK = 64
WINDOW = 8
EPS = 1e-06
LOG2E = 1.4426950408889634
BF = jnp.bfloat16
F32 = jnp.float32


def dot(a, b, dims=((1,), (0,))):
    return lax.dot_general(a, b, (dims, ((), ())), preferred_element_type=F32)


def head_sums(x, same_head):
    high = x.astype(BF)
    low = (x - high.astype(F32)).astype(BF)
    return dot(high, same_head) + dot(low, same_head)


def unit_rows(x, same_head):
    length = jnp.sqrt(head_sums(x * x, same_head) + EPS)
    return x / length, length


def unit_back(unit, length, grad, same_head):
    return (grad - unit * head_sums(unit * grad, same_head)) / length


def attention_kernel(
    mult_ref, valid_ref, scale_ref, even_ref,
    q_ref, k_ref, v_ref, k1_ref, v1_ref, k2_ref, v2_ref, u_ref,
    att_ref, dq_ref, dk_ref, dv_ref, rim1_ref, rim2_ref, ds_ref,
    k_unit, k_len, k_low, k_turn, v_low, v_turn, bias, scores, grads, raised, w_lows, c_lows, dk, dv,
):
    rows = q_ref.shape[0]
    margin = k1_ref.shape[0]
    even = even_ref[0] == 1
    pool = rows + 2 * margin
    reach = margin // BLK
    steps = rows // PAIR
    span = WINDOW * BLK
    pair = pl.program_id(0)

    lane = lax.broadcasted_iota(jnp.int32, (BLK, PAIR), 1)
    row = lax.broadcasted_iota(jnp.int32, (BLK, PAIR), 0)
    head_a = lax.broadcasted_iota(jnp.int32, (PAIR, PAIR), 0) < HD
    head_b = lax.broadcasted_iota(jnp.int32, (PAIR, PAIR), 1) < HD
    same_head = jnp.where(head_a == head_b, 1.0, 0.0).astype(BF)
    first_lanes = head_b

    @pl.when(pair == 0)
    def _():
        for t in range(steps):
            for w in range(WINDOW):
                count = jnp.where(lane < BLK, mult_ref[2 * t, w], mult_ref[2 * t + 1, w])
                live = row < valid_ref[2 * t + w]
                seen = jnp.where(live, count, 0).astype(F32)
                bias[t, w * BLK : (w + 1) * BLK, :] = jnp.where(
                    seen > 0.0, jnp.log2(jnp.maximum(seen, 1.0)), -1e30
                )

    def split_heads(x):
        return jnp.concatenate(
            [jnp.where(first_lanes, x, 0.0), jnp.where(first_lanes, 0.0, x)], axis=0
        ).astype(BF)

    def take(at, keys, values):
        unit, length = unit_rows(keys.astype(F32), same_head)
        place = slice(at, at + keys.shape[0])
        k_unit[place, :] = unit
        k_len[place, :] = length
        k_low[place, :] = unit.astype(BF)
        v_low[place, :] = values

    for part in range(0, margin, BLK):
        here = slice(part, part + BLK)
        k1, k2 = k1_ref[here, :].astype(F32), k2_ref[here, :].astype(F32)
        v1, v2 = v1_ref[here, :].astype(F32), v2_ref[here, :].astype(F32)
        take(part, jnp.where(even, k2, k1), jnp.where(even, v2, v1).astype(BF))
        take(margin + rows + part, jnp.where(even, k1, k2), jnp.where(even, v1, v2).astype(BF))
    for part in range(0, rows, PAIR):
        here = slice(part, part + PAIR)
        take(margin + part, k_ref[here, :], v_ref[here, :])
    for part in range(0, pool, 128):
        place = slice(part, part + 128)
        k_turn[:, place] = jnp.transpose(k_low[place, :].astype(F32)).astype(BF)
        v_turn[:, place] = jnp.transpose(v_low[place, :].astype(F32)).astype(BF)

    dk[...] = jnp.zeros_like(dk)
    dv[...] = jnp.zeros_like(dv)
    wide_lane = lax.broadcasted_iota(jnp.int32, (1, 2 * PAIR), 1)
    scale = jnp.where(wide_lane < PAIR, scale_ref[2 * pair], scale_ref[2 * pair + 1])
    ds = jnp.zeros((8, 2 * PAIR), F32)

    def window_of(t):
        return slice(t * PAIR, t * PAIR + span)

    def begin(t):
        own, window = slice(t * PAIR, (t + 1) * PAIR), window_of(t)
        q_unit, q_len = unit_rows(q_ref[own, :].astype(F32), same_head)
        q_split = split_heads(q_unit)
        live = jnp.concatenate(
            [row < valid_ref[2 * t + reach], row < valid_ref[2 * t + 1 + reach]], axis=0
        )
        u_split = split_heads(jnp.where(live, u_ref[own, :].astype(F32), 0.0))
        scores[t % 2] = dot(k_low[window, :], q_split, ((1,), (1,)))
        grads[t % 2] = dot(v_low[window, :], u_split, ((1,), (1,)))
        return q_unit, q_len, q_split, live, u_split

    stretch = scale * LOG2E
    parts = [slice(i, i + 32) for i in range(0, span, 32)]

    def fold(x):
        return x.reshape(4, 8, 2 * PAIR)

    following = begin(0)
    for t in range(steps):
        own, window = slice(t * PAIR, (t + 1) * PAIR), window_of(t)
        q_unit, q_len, q_split, live, u_split = following
        s_ref, g_ref, e_ref = scores.at[t % 2], grads.at[t % 2], raised.at[t % 2]
        w_low, c_low = w_lows.at[t % 2], c_lows.at[t % 2]
        if t + 1 < steps:
            following = begin(t + 1)

        peak = jnp.full((8, 2 * PAIR), -1e30, F32)
        for part in parts:
            half = bias[t, part, :]
            x = s_ref[part, :] * stretch + jnp.concatenate([half, half], axis=1)
            e_ref[part, :] = x
            peak = jnp.maximum(peak, jnp.max(fold(x), axis=0))
        peak = jnp.max(peak, axis=0, keepdims=True)
        total = jnp.zeros((8, 2 * PAIR), F32)
        centre = jnp.zeros((8, 2 * PAIR), F32)
        for part in parts:
            e = jnp.exp2(e_ref[part, :] - peak)
            e_ref[part, :] = e
            total = total + jnp.sum(fold(e), axis=0)
            centre = centre + jnp.sum(fold(e * g_ref[part, :]), axis=0)
        share = 1.0 / jnp.sum(total, axis=0, keepdims=True)
        centre = jnp.sum(centre, axis=0, keepdims=True) * share
        for part in parts:
            w = e_ref[part, :] * share
            w_low[part, :] = w.astype(BF)
            sg = w * (g_ref[part, :] - centre)
            ds = ds + jnp.sum(fold(sg * s_ref[part, :]), axis=0)
            c_low[part, :] = (sg * scale).astype(BF)

        def by_query(turned):
            return jnp.transpose(
                jnp.concatenate([turned[:HD, :PAIR], turned[HD:, PAIR:]], axis=0)
            )

        mixed = by_query(dot(v_turn[:, window], w_low[...]))
        att_ref[own, :] = jnp.where(live, mixed, 0.0).astype(BF)
        q_grad = by_query(dot(k_turn[:, window], c_low[...]))
        dq_ref[own, :] = unit_back(q_unit, q_len, q_grad, same_head).astype(BF)
        dv[window, :] += dot(w_low[...], u_split)
        dk[window, :] += dot(c_low[...], q_split)

    def key_grad(part):
        place = slice(part, part + BLK)
        return unit_back(k_unit[place, :], k_len[place, :], dk[place, :], same_head)

    for part in range(0, rows, BLK):
        here = slice(part, part + BLK)
        dk_ref[here, :] = key_grad(margin + part)
        dv_ref[here, :] = dv[margin + part : margin + part + BLK, :]
    for part in range(0, margin, BLK):
        here = slice(part, part + BLK)
        far = margin + rows + part
        kb, ka = key_grad(part), key_grad(far)
        vb, va = dv[part : part + BLK, :], dv[far : far + BLK, :]
        rim1_ref[0, here, :] = jnp.where(even, ka, kb).astype(BF)
        rim1_ref[1, here, :] = jnp.where(even, va, vb).astype(BF)
        rim2_ref[0, here, :] = jnp.where(even, kb, ka).astype(BF)
        rim2_ref[1, here, :] = jnp.where(even, vb, va).astype(BF)
    ds_ref[0, :, :] = ds


def attention(packed, first, second, upstream, mult, valid, scales, even, pairs, begin=0, count=2):
    rows = packed.shape[0]
    width = count * PAIR
    margin = first.shape[0]
    pool = rows + 2 * margin
    held = len(pairs)
    stride = pairs[1] - pairs[0]
    steps = rows // PAIR
    span = WINDOW * BLK

    def at(offset):
        return lambda p, *_: (0, offset + p)

    return pl.pallas_call(
        attention_kernel,
        grid_spec=pltpu.PrefetchScalarGridSpec(
            num_scalar_prefetch=4,
            grid=(count,),
            in_specs=[
                pl.BlockSpec((rows, PAIR), at(begin)),
                pl.BlockSpec((rows, PAIR), at(held + begin)),
                pl.BlockSpec((rows, PAIR), at(2 * held + begin)),
                pl.BlockSpec((margin, PAIR), at(begin)),
                pl.BlockSpec((margin, PAIR), at(held + begin)),
                pl.BlockSpec((margin, PAIR), at(begin)),
                pl.BlockSpec((margin, PAIR), at(held + begin)),
                pl.BlockSpec((rows, PAIR), lambda p, *_: (0, pairs[begin] + stride * p)),
            ],
            out_specs=[
                pl.BlockSpec((rows, PAIR), at(0)),
                pl.BlockSpec((rows, PAIR), at(0)),
                pl.BlockSpec((rows, PAIR), at(0)),
                pl.BlockSpec((rows, PAIR), at(0)),
                pl.BlockSpec((2, margin, PAIR), lambda p, *_: (0, 0, p)),
                pl.BlockSpec((2, margin, PAIR), lambda p, *_: (0, 0, p)),
                pl.BlockSpec((1, 8, 2 * PAIR), lambda p, *_: (p, 0, 0)),
            ],
            scratch_shapes=[
                pltpu.VMEM((pool, PAIR), F32),
                pltpu.VMEM((pool, PAIR), F32),
                pltpu.VMEM((pool, PAIR), BF),
                pltpu.VMEM((PAIR, pool), BF),
                pltpu.VMEM((pool, PAIR), BF),
                pltpu.VMEM((PAIR, pool), BF),
                pltpu.VMEM((steps, span, PAIR), F32),
                pltpu.VMEM((2, span, 2 * PAIR), F32),
                pltpu.VMEM((2, span, 2 * PAIR), F32),
                pltpu.VMEM((2, span, 2 * PAIR), F32),
                pltpu.VMEM((2, span, 2 * PAIR), BF),
                pltpu.VMEM((2, span, 2 * PAIR), BF),
                pltpu.VMEM((pool, PAIR), F32),
                pltpu.VMEM((pool, PAIR), F32),
            ],
        ),
        out_shape=[
            jax.ShapeDtypeStruct((rows, width), BF),
            jax.ShapeDtypeStruct((rows, width), BF),
            jax.ShapeDtypeStruct((rows, width), F32),
            jax.ShapeDtypeStruct((rows, width), F32),
            jax.ShapeDtypeStruct((2, margin, width), BF),
            jax.ShapeDtypeStruct((2, margin, width), BF),
            jax.ShapeDtypeStruct((count, 8, 2 * PAIR), F32),
        ],
        compiler_params=pltpu.CompilerParams(vmem_limit_bytes=40 * 1024 * 1024),
        cost_estimate=pl.CostEstimate(
            flops=8 * 2 * 6 * count * steps * span * 256 * 128,
            bytes_accessed=rows * width * 20,
            transcendentals=count * steps * span * 256,
        ),
        name="block_attention",
    )(mult, valid, scales, even, packed, packed, packed, first, first, second, second, upstream)


def pick_kernel(core_ref, qkv_ref, out_ref, first_ref, second_ref):
    core = core_ref[0]
    for ref, pairs in zip((first_ref, second_ref), CHUNKS):
        at = 0
        for base in range(0, qkv_ref.shape[1], 8 * PAIR):
            for p in pairs:
                start = pl.multiple_of(base + 2 * p * PAIR + core * PAIR, PAIR)
                ref[:, at : at + PAIR] = qkv_ref[:, pl.ds(start, PAIR)]
                at += PAIR
    half = out_ref.shape[1] // 2
    rows = out_ref[pl.ds(pl.multiple_of(core * PAIR, PAIR), PAIR), :]
    first_ref[:PAIR, at:] = rows[:, :half]
    first_ref[PAIR:, at:] = rows[:, half:]


def pick_weights(w_qkv, w_out, core):
    height, columns = w_qkv.shape
    part = columns // 4
    wide = part + w_out.shape[1] // 2
    return pl.pallas_call(
        pick_kernel,
        grid_spec=pltpu.PrefetchScalarGridSpec(
            num_scalar_prefetch=1,
            grid=(1,),
            in_specs=[
                pl.BlockSpec(w_qkv.shape, lambda i, *_: (0, 0)),
                pl.BlockSpec(w_out.shape, lambda i, *_: (0, 0)),
            ],
            out_specs=[
                pl.BlockSpec((height, wide), lambda i, *_: (0, 0)),
                pl.BlockSpec((height, part), lambda i, *_: (0, 0)),
            ],
        ),
        out_shape=[
            jax.ShapeDtypeStruct((height, wide), BF),
            jax.ShapeDtypeStruct((height, part), BF),
        ],
        compiler_params=pltpu.CompilerParams(vmem_limit_bytes=16 * 1024 * 1024),
        name="pick_weights",
    )(jnp.reshape(core, (1,)).astype(jnp.int32), w_qkv, w_out)


def gate(value, *others):
    return lax.optimization_barrier((value,) + others)[0]


def pick_groups(array, axis, unit, core):
    size = array.shape[axis]
    picked = [
        jnp.where(
            core == 0,
            lax.slice_in_dim(array, at, at + unit, axis=axis),
            lax.slice_in_dim(array, at + unit, at + 2 * unit, axis=axis),
        )
        for at in range(0, size, 2 * unit)
    ]
    return jnp.concatenate(picked, axis=axis)


def spread_groups(array, axis, unit, core):
    groups = jnp.split(array, array.shape[axis] // unit, axis=axis)
    parts = []
    for group in groups:
        empty = jnp.zeros_like(group)
        parts += [jnp.where(core == 0, group, empty), jnp.where(core == 0, empty, group)]
    return jnp.concatenate(parts, axis=axis)


def in_order(core, own, other, axis):
    first = jnp.where(core == 0, own, other)
    second = jnp.where(core == 0, other, own)
    return jnp.concatenate([first, second], axis=axis)


def xor_blocks(blocks, index):
    odd = (index & 1) == 1
    high = (index & 2) == 2
    near = [jnp.where(odd, blocks[k ^ 1], blocks[k]) for k in range(4)]
    return [jnp.where(high, near[k ^ 2], near[k]) for k in range(4)]


ORDER = (1, 3, 2, 0)
CHUNKS = ((0, 3), (1, 2))


def square(value, step):
    return lax.ppermute(value, "fsdp", [(i, i ^ step) for i in range(4)])


def gather_near(shard):
    return square(shard, 1), square(shard, 2)


def gather_far(near, far):
    half = near.shape[0] // 2
    top = square(far[:half], 1)
    low = square(near[half:], 2)
    return jnp.concatenate([top, low], axis=0)


def chips(value, step, n_vox):
    return lax.ppermute(value, "vox", [(i, i ^ (2 * step)) for i in range(n_vox)])


def stacked(block):
    half = block.shape[1] // 2
    return jnp.concatenate([block[:, :half], block[:, half:]], axis=0)


def reduce_terms(normed, columns, place, extra=None):
    size = normed.shape[1] // 4
    value = dot(normed[:, place.start * size : place.stop * size], columns, ((0,), (0,)))
    if extra is None:
        return value
    more = jnp.concatenate([extra[k] for k in range(place.start, place.stop)], axis=0)
    return jnp.concatenate([value, more], axis=1)


def reduce_first(normed, left, right, extra=(None, None)):
    return (
        reduce_terms(normed, left, slice(0, 2), extra[0]).astype(BF),
        reduce_terms(normed, right, slice(1, 3), extra[1]).astype(BF),
    )


def reduce_second(normed, left, right, from_x, from_y, extra=(None, None)):
    size = normed.shape[1] // 4
    to_y = reduce_terms(normed, left, slice(2, 3), extra[0]) + from_x[size:].astype(F32)
    to_x = reduce_terms(normed, right, slice(0, 1), extra[1]) + from_y[:size].astype(F32)
    return to_x.astype(BF), to_y.astype(BF)


def reduce_kept(normed, left, right, from_x, from_y, extra=(None, None)):
    size = normed.shape[1] // 4
    return (
        reduce_terms(normed, left, slice(3, 4), extra[0]) + from_x[:size].astype(F32),
        reduce_terms(normed, right, slice(3, 4), extra[1]) + from_y[size:].astype(F32),
    )


def on_device(
    tokens, gain, w_qkv, w_out, logit_scale, key_blocks, slot_count, valid_voxels, cotangent
):
    own_tokens = tokens[0]
    own_cotangent = cotangent[0]
    own_rows, model_width = own_tokens.shape
    rows = 2 * own_rows
    own_blocks = key_blocks.shape[1]
    blocks = 2 * own_blocks
    slot_total = key_blocks.shape[2]
    reach = own_blocks // 2
    margin = reach * BLK
    n_vox = lax.axis_size("vox")
    n_fsdp = lax.axis_size("fsdp")
    n_chip = n_vox // 2
    place = lax.axis_index("vox")
    scene = lax.axis_index("fsdp")
    core = place % 2
    chip = place // 2
    fast = n_vox == 8 and n_fsdp == 4
    unit = 128 if fast else 64
    swap = [(i, i ^ 1) for i in range(n_vox)]
    even, low = chip % 2 == 0, chip < 2
    even_flag = jnp.reshape(even, (1,)).astype(jnp.int32)
    near_chips = [(i, i ^ 2) for i in range(n_vox)]
    far_chips = []
    for i in range(n_vox):
        to = i // 2 + (1 if i // 2 % 2 else -1)
        far_chips.append((i, 2 * to + i % 2 if 0 <= to < n_chip else i))
    part_width = model_width // 2

    def columns_of(array, pairs):
        return jnp.concatenate(
            [
                array[:, base + p * PAIR : base + (p + 1) * PAIR]
                for base in range(0, array.shape[1], part_width)
                for p in pairs
            ],
            axis=1,
        )

    if fast:
        shard, shard_1 = pick_weights(w_qkv, w_out, core)
        near, far = gather_near(shard)
        diag = gather_far(near, far)
        weights_1 = lax.all_gather(shard_1, "fsdp", axis=0, tiled=True)
        turned = xor_blocks(jnp.split(weights_1, 4, axis=0), scene)
        weights_1 = jnp.concatenate([turned[k] for k in ORDER], axis=0)
        wide = shard_1.shape[1]
        weights_0 = jnp.concatenate([block[:, :wide] for block in (near, diag, far, shard)], axis=0)
        out_blocks = [
            jnp.concatenate([block[:PAIR, wide:], block[PAIR:, wide:]], axis=1)
            for block in (shard, near, far, diag)
        ]
        out_half = jnp.concatenate(xor_blocks(out_blocks, scene), axis=0)
    else:
        core_qkv = pick_groups(w_qkv, 1, unit, core)
        core_out = pick_groups(w_out, 0, unit, core)
        weights_0, weights_1 = [
            lax.all_gather(columns_of(core_qkv, pairs), "fsdp", axis=0, tiled=True)
            for pairs in CHUNKS
        ]
        out_half = lax.all_gather(core_out, "fsdp", axis=0, tiled=True)

    other_tokens = lax.ppermute(own_tokens, "vox", swap)
    other_cotangent = lax.ppermute(own_cotangent, "vox", swap)
    lists = jnp.concatenate([key_blocks[0], slot_count[0][:, None]], axis=1)
    all_lists = in_order(
        core, lists, lax.ppermute(lists.astype(F32), "vox", swap).astype(jnp.int32), 0
    )
    chip_tokens = in_order(core, own_tokens, other_tokens, 0)
    chip_cotangent = in_order(core, own_cotangent, other_cotangent, 0)

    first_block = chip * blocks
    pool_blocks = blocks + 2 * reach
    window_id = (
        all_lists[:, :slot_total] - first_block + reach
        - 2 * (jnp.arange(blocks, dtype=jnp.int32) // 2)[:, None]
    )
    used = jnp.arange(slot_total, dtype=jnp.int32)[None, :] < all_lists[:, slot_total:]
    hits = jnp.logical_and(
        window_id[:, :, None] == jnp.arange(WINDOW, dtype=jnp.int32), used[:, :, None]
    )
    mult = jnp.sum(hits.astype(jnp.int32), axis=1)
    scene_total = valid_voxels.shape[1]
    pool_ids = first_block - reach + jnp.arange(pool_blocks, dtype=jnp.int32)
    valid = jnp.take(valid_voxels[0], jnp.clip(pool_ids, 0, scene_total - 1))
    group_heads = unit // HD
    scales = pick_groups(logit_scale, 0, group_heads, core)

    wide = chip_tokens.astype(F32)
    inverse = lax.rsqrt(jnp.mean(wide * wide, axis=1, keepdims=True) + EPS)
    normed = (wide * inverse * gain).astype(BF)
    if fast:
        turned = xor_blocks(jnp.split(normed, 4, axis=1), scene)
        normed = jnp.concatenate([turned[k] for k in ORDER], axis=1)

    def pairings(first, second):
        return lax.ppermute(first, "vox", near_chips), lax.ppermute(second, "vox", far_chips)

    def project(weight):
        packed = dot(normed, weight).astype(BF)
        width = packed.shape[1] // 3
        top, bottom = packed[:margin, width:], packed[rows - margin :, width:]
        return (packed,) + pairings(jnp.where(even, bottom, top), jnp.where(even, top, bottom))

    def heads_of(inputs, upstream, pairs, begin=0, count=2):
        used = pairs[begin : begin + count]
        chunk_scales = jnp.concatenate([scales[2 * p : 2 * p + 2] for p in used])
        return attention(
            *inputs, upstream, mult, valid, chunk_scales, even_flag, pairs, begin, count
        )

    def with_rims(grad, first, second):
        first, second = first.astype(F32), second.astype(F32)
        return jnp.concatenate(
            [
                grad[:margin] + jnp.where(even, second, first),
                grad[margin : rows - margin],
                grad[rows - margin :] + jnp.where(even, first, second),
            ],
            axis=0,
        ).astype(BF)

    def key_value_grads(keys, values, rims):
        return [with_rims(g, rims[0][i], rims[1][i]) for i, g in enumerate((keys, values))]

    def out_rows(pairs):
        return jnp.concatenate([out_half[p * PAIR : (p + 1) * PAIR] for p in pairs], axis=0)

    def groups_of(left, right, chunk):
        half = 3 * PAIR
        groups = [left[:, k * PAIR : (k + 1) * PAIR] for k in range(3)]
        groups += [right[:, k * PAIR : (k + 1) * PAIR] for k in range(3)]
        sets = ((0, 3, 4), (1, 2, 5)) if chunk == 0 else ((0, 3, 2), (1, 4, 5))
        evens = jnp.concatenate([groups[k] for k in sets[0]] + [left[:, half:]], axis=1)
        odds = jnp.concatenate([groups[k] for k in sets[1]] + [right[:, half:]], axis=1)
        return jnp.where(even, evens, odds), jnp.where(even, odds, evens).astype(BF)

    def halves_of(kept):
        left, right = kept[:, : 2 * PAIR], kept[:, PAIR : 3 * PAIR]
        if kept.shape[1] > 3 * PAIR:
            more = kept[:, 3 * PAIR :]
            cut = more.shape[0] // 2
            left = jnp.concatenate([left, more[:cut]], axis=0)
            right = jnp.concatenate([right, more[cut:]], axis=0)
        return jnp.where(low, left, right), jnp.where(low, right, left).astype(BF)

    packed_0 = project(weights_0)
    upstream = dot(chip_cotangent, out_half, ((1,), (1,))).astype(BF)
    packed_1 = project(weights_1)
    first = heads_of(packed_0, gate(upstream, packed_1[1], packed_1[2]), CHUNKS[0])
    rims_0 = pairings(first[4], first[5])
    third = heads_of(packed_1, gate(upstream, first[4], first[5]), CHUNKS[1], 0, 1)
    rims_0 = [gate(rim, third[6]) for rim in rims_0]
    key_0, value_0 = key_value_grads(first[2], first[3], rims_0)
    grad_0 = jnp.concatenate([first[1], key_0, value_0], axis=1)
    cut = grad_0.shape[1] // 2
    left_0, right_0 = grad_0[:, :cut], grad_0[:, cut:]
    if fast:
        to_x, to_y = reduce_first(normed, left_0, right_0)
        from_x0, from_y0 = square(to_x, 1), square(to_y, 2)
        fourth_in = gate(upstream, to_x, to_y)
    else:
        fourth_in = upstream
    fourth = heads_of(packed_1, fourth_in, CHUNKS[1], 1, 1)
    rims_1 = pairings(*[jnp.concatenate([third[i], fourth[i]], axis=2) for i in (4, 5)])

    att_0 = gate(first[0], fourth[6])
    att_1 = jnp.concatenate([third[0], fourth[0]], axis=1)
    out_grads = [dot(att, chip_cotangent, ((0,), (0,))) for att in (att_0, att_1)]
    if fast:
        blocks_of = {}
        for pairs, value in zip(CHUNKS, out_grads):
            for i, p in enumerate(pairs):
                blocks_of[p] = value[i * PAIR : (i + 1) * PAIR].astype(BF)
        turned = [stacked(b) for b in xor_blocks([blocks_of[p] for p in range(4)], scene)]
        quarter = model_width // 4
        extra = [[turned[k][:, at : at + quarter] for k in ORDER] for at in (0, quarter)]
        to_x, to_y = reduce_first(normed, third[1], fourth[1], extra)
        early_x, early_y = square(to_x, 1), square(to_y, 2)
        left_0, right_0, att_0, att_1 = lax.optimization_barrier(
            (left_0, right_0, att_0, att_1, to_x, to_y)
        )[:4]
        to_x, to_y = reduce_second(normed, left_0, right_0, from_x0, from_y0)
        end_x0, end_y0 = square(to_x, 1), square(to_y, 2)
    mixed_part = dot(att_0, out_rows(CHUNKS[0])) + dot(att_1, out_rows(CHUNKS[1]))

    key_1, value_1 = key_value_grads(
        *[jnp.concatenate([third[i], fourth[i]], axis=1) for i in (2, 3)], rims_1
    )
    grad_1 = jnp.concatenate([third[1], fourth[1], key_1, value_1], axis=1)
    if fast:
        to_x, to_y = reduce_first(normed, key_1, value_1)
        late_x, late_y = square(to_x, 1), square(to_y, 2)
        grad_0, grad_1, from_x0, from_y0, end_x0, end_y0 = lax.optimization_barrier(
            (grad_0, grad_1, from_x0, from_y0, end_x0, end_y0, to_x, to_y)
        )[:6]

    ngrad_part = dot(grad_0, weights_0, ((1,), (1,))) + dot(grad_1, weights_1, ((1,), (1,)))
    mixed_mine = lax.dynamic_slice_in_dim(mixed_part, core * own_rows, own_rows, 0)
    mixed_theirs = lax.dynamic_slice_in_dim(mixed_part, (1 - core) * own_rows, own_rows, 0)
    mixed = (
        own_tokens.astype(F32) + (mixed_mine + lax.ppermute(mixed_theirs, "vox", swap))
    ).astype(BF)

    ngrad_mine = lax.dynamic_slice_in_dim(ngrad_part, core * own_rows, own_rows, 0)
    ngrad_theirs = lax.dynamic_slice_in_dim(ngrad_part, (1 - core) * own_rows, own_rows, 0)
    normed_grad = ngrad_mine + lax.ppermute(ngrad_theirs, "vox", swap)
    if fast:
        held = jnp.split(normed_grad, 4, axis=1)
        normed_grad = jnp.concatenate(
            xor_blocks([held[ORDER.index(k)] for k in range(4)], scene), axis=1
        )

    own_wide = own_tokens.astype(F32)
    own_inverse = lax.rsqrt(jnp.mean(own_wide * own_wide, axis=1, keepdims=True) + EPS)
    gain_grad = jnp.sum(normed_grad * own_wide * own_inverse, axis=0)
    scaled_grad = normed_grad * gain
    token_grad = (
        own_cotangent.astype(F32)
        + own_inverse
        * (
            scaled_grad
            - own_wide
            * own_inverse
            * own_inverse
            * jnp.mean(scaled_grad * own_wide, axis=1, keepdims=True)
        )
    ).astype(BF)

    scale_parts = {}
    for pairs, sums in zip(CHUNKS, (first[6], jnp.concatenate([third[6], fourth[6]], axis=0))):
        sums = jnp.sum(sums.reshape(2, 8, 2, PAIR), axis=(1, 3))
        for i, p in enumerate(pairs):
            scale_parts[p] = sums[i]
    scale_part = jnp.concatenate([scale_parts[p] for p in range(len(scale_parts))])
    scale_grad = spread_groups(scale_part, 0, group_heads, core)

    if fast:
        small = jnp.concatenate([gain_grad, scale_grad, jnp.zeros((112,), F32)]).reshape(9, 128)
        kept_0, sent = groups_of(
            *[
                a + b.astype(F32)
                for a, b in zip(
                    reduce_kept(normed, left_0, right_0, from_x0, from_y0), (end_y0, end_x0)
                )
            ],
            0,
        )
        got_0 = chips(sent, 1, n_vox)
        late_x, late_y = lax.optimization_barrier((late_x, late_y, small))[:2]
        small = small + square(small, 1)
        from_x1, from_y1 = [
            jnp.concatenate([early[:, :PAIR], late, early[:, PAIR:]], axis=1)
            for early, late in ((early_x, late_x), (early_y, late_y))
        ]
        left_1 = jnp.concatenate([third[1], key_1], axis=1)
        right_1 = jnp.concatenate([fourth[1], value_1], axis=1)
        to_x, to_y = reduce_second(normed, left_1, right_1, from_x1, from_y1, extra)
        end_x, end_y = square(to_x, 1), square(to_y, 2)
        got_0, small, from_x1, from_y1 = lax.optimization_barrier(
            (got_0, small, from_x1, from_y1, to_x, to_y)
        )[:4]
        small = small + square(small, 2)
        kept_0, sent = halves_of(kept_0 + got_0.astype(F32))
        got_0 = chips(sent, 2, n_vox)
        left, right = reduce_kept(normed, left_1, right_1, from_x1, from_y1, extra)
        end_x, end_y = lax.optimization_barrier((end_x, end_y, token_grad, mixed))[:2]
        kept_1, sent = groups_of(left + end_y.astype(F32), right + end_x.astype(F32), 1)
        got_1 = chips(sent, 1, n_vox)
        small = gate(small, sent)
        small = small + lax.ppermute(small, "vox", swap)
        small = small + chips(small, 1, n_vox)
        kept_1, sent = halves_of(kept_1 + got_1.astype(F32))
        got_1 = chips(sent, 2, n_vox)
        small = gate(small, sent)
        small = small + chips(small, 2, n_vox)
        small = small.reshape(-1)
        summed_gain, summed_scale = small[:model_width], small[model_width : model_width + HEADS]
        kept_1 = kept_1 + got_1.astype(F32)
        height = model_width // 4
        qkv_sums = [kept_0 + got_0.astype(F32), kept_1[:height]]
        out_sum = kept_1[height:]
    else:
        out_sums = out_grads
        qkv_sums = [dot(normed, grad, ((0,), (0,))) for grad in (grad_0, grad_1)]
        summed_gain, summed_scale = lax.psum((gain_grad, scale_grad), ("vox", "fsdp"))

    if fast:
        half = out_sum.shape[1] // 2
        first, second = out_sum[:, :half], out_sum[:, half:]
        out_other = lax.ppermute(jnp.where(core == 0, second, first), "vox", swap)
        summed_out = in_order(core, jnp.where(core == 0, first, second), out_other, 0)

        a0, a1 = qkv_sums[0][:, :PAIR], qkv_sums[0][:, PAIR:]
        b0, b1 = qkv_sums[1][:, :PAIR], qkv_sums[1][:, PAIR:]

        def by_chip(options):
            value = options[3]
            for k in range(3):
                value = jnp.where(chip == k, options[k], value)
            return value

        g0 = by_chip((a0, a0, b1, b0))
        g1 = by_chip((b0, a1, a0, b1))
        g2 = by_chip((b1, b0, a1, a1))
        got = lax.ppermute(jnp.where(core == 0, g2, g0), "vox", swap)
        summed_qkv = jnp.concatenate(
            [
                jnp.where(core == 0, g0, g1),
                got,
                jnp.where(core == 0, g1, g2),
            ],
            axis=1,
        )
    else:
        by_pair = {}
        cols = {}
        for pairs, out_total, qkv_total in zip(CHUNKS, out_sums, qkv_sums):
            for i, p in enumerate(pairs):
                by_pair[p] = out_total[i * PAIR : (i + 1) * PAIR]
                for j in range(3):
                    at = (2 * j + i) * PAIR
                    cols[4 * j + p] = qkv_total[:, at : at + PAIR]
        out_total = jnp.concatenate([by_pair[p] for p in range(4)], axis=0)
        qkv_total = jnp.concatenate([cols[k] for k in range(12)], axis=1)
        out_total = spread_groups(out_total, 0, unit, core)
        qkv_total = lax.psum_scatter(qkv_total, "fsdp", scatter_dimension=0, tiled=True)
        qkv_total = spread_groups(qkv_total, 1, unit, core)
        summed_qkv = lax.psum_scatter(qkv_total, "vox", scatter_dimension=1, tiled=True)
        out_total = lax.psum_scatter(out_total, "fsdp", scatter_dimension=0, tiled=True)
        summed_out = lax.psum_scatter(out_total, "vox", scatter_dimension=1, tiled=True)

    return (
        mixed[None],
        token_grad[None],
        summed_qkv,
        summed_out,
        summed_gain,
        summed_scale,
    )


def solution(mesh):
    return jax.shard_map(
        on_device,
        mesh=mesh,
        in_specs=(
            P("fsdp", "vox", None),
            P(),
            P("fsdp", None),
            P("fsdp", None),
            P(),
            P("fsdp", "vox", None),
            P("fsdp", "vox"),
            P("fsdp", None),
            P("fsdp", "vox", None),
        ),
        out_specs=(
            P("fsdp", "vox", None),
            P("fsdp", "vox", None),
            P("fsdp", "vox"),
            P("fsdp", "vox"),
            P(),
            P(),
        ),
        check_vma=False,
    )
```

```python
import functools

import jax
import jax.numpy as jnp
from jax import lax
from jax.experimental import pallas as pl
from jax.experimental.pallas import tpu as pltpu
from jax.sharding import PartitionSpec as P

HEADS = 16
HD = 64
PAIR = 2 * HD
BLK = 64
WINDOW = 8
EPS = 1e-06
LOG2E = 1.4426950408889634
BF = jnp.bfloat16
F32 = jnp.float32


def dot(a, b, dims=((1,), (0,))):
    return lax.dot_general(a, b, (dims, ((), ())), preferred_element_type=F32)


def head_sums(x, same_head):
    high = x.astype(BF)
    low = (x - high.astype(F32)).astype(BF)
    return dot(high, same_head) + dot(low, same_head)


def unit_rows(x, same_head):
    length = jnp.sqrt(head_sums(x * x, same_head) + EPS)
    return x / length, length


def unit_back(unit, length, grad, same_head):
    return (grad - unit * head_sums(unit * grad, same_head)) / length


def attention_kernel(
    mult_ref, valid_ref, scale_ref, even_ref,
    q_ref, k_ref, v_ref, k1_ref, v1_ref, k2_ref, v2_ref, u_ref,
    att_ref, dq_ref, dk_ref, dv_ref, rim1_ref, rim2_ref, ds_ref, turn_ref,
    k_unit, k_len, k_low, k_turn, v_low, v_turn, bias, scores, grads, raised, w_lows, c_lows, dk, dv,
):
    rows = q_ref.shape[0]
    margin = k1_ref.shape[0]
    even = even_ref[0] == 1
    pool = rows + 2 * margin
    reach = margin // BLK
    steps = rows // PAIR
    span = WINDOW * BLK
    pair = pl.program_id(0)

    lane = lax.broadcasted_iota(jnp.int32, (BLK, PAIR), 1)
    row = lax.broadcasted_iota(jnp.int32, (BLK, PAIR), 0)
    head_a = lax.broadcasted_iota(jnp.int32, (PAIR, PAIR), 0) < HD
    head_b = lax.broadcasted_iota(jnp.int32, (PAIR, PAIR), 1) < HD
    same_head = jnp.where(head_a == head_b, 1.0, 0.0).astype(BF)
    first_lanes = head_b

    @pl.when(pair == 0)
    def _():
        for t in range(steps):
            for w in range(WINDOW):
                count = jnp.where(lane < BLK, mult_ref[2 * t, w], mult_ref[2 * t + 1, w])
                live = row < valid_ref[2 * t + w]
                seen = jnp.where(live, count, 0).astype(F32)
                bias[t, w * BLK : (w + 1) * BLK, :] = jnp.where(
                    seen > 0.0, jnp.log2(jnp.maximum(seen, 1.0)), -1e30
                )

    def split_heads(x):
        return jnp.concatenate(
            [jnp.where(first_lanes, x, 0.0), jnp.where(first_lanes, 0.0, x)], axis=0
        ).astype(BF)

    def take(at, keys, values):
        unit, length = unit_rows(keys.astype(F32), same_head)
        place = slice(at, at + keys.shape[0])
        k_unit[place, :] = unit
        k_len[place, :] = length
        k_low[place, :] = unit.astype(BF)
        v_low[place, :] = values

    for part in range(0, margin, BLK):
        here = slice(part, part + BLK)
        k1, k2 = k1_ref[here, :].astype(F32), k2_ref[here, :].astype(F32)
        v1, v2 = v1_ref[here, :].astype(F32), v2_ref[here, :].astype(F32)
        take(part, jnp.where(even, k2, k1), jnp.where(even, v2, v1).astype(BF))
        take(margin + rows + part, jnp.where(even, k1, k2), jnp.where(even, v1, v2).astype(BF))
    for part in range(0, rows, PAIR):
        here = slice(part, part + PAIR)
        take(margin + part, k_ref[here, :], v_ref[here, :])
    for part in range(0, pool, 128):
        place = slice(part, part + 128)
        k_turn[:, place] = jnp.transpose(k_low[place, :].astype(F32)).astype(BF)
        v_turn[:, place] = jnp.transpose(v_low[place, :].astype(F32)).astype(BF)

    dk[...] = jnp.zeros_like(dk)
    dv[...] = jnp.zeros_like(dv)
    wide_lane = lax.broadcasted_iota(jnp.int32, (1, 2 * PAIR), 1)
    scale = jnp.where(wide_lane < PAIR, scale_ref[2 * pair], scale_ref[2 * pair + 1])
    ds = jnp.zeros((8, 2 * PAIR), F32)

    def window_of(t):
        return slice(t * PAIR, t * PAIR + span)

    def begin(t):
        own, window = slice(t * PAIR, (t + 1) * PAIR), window_of(t)
        q_unit, q_len = unit_rows(q_ref[own, :].astype(F32), same_head)
        q_split = split_heads(q_unit)
        live = jnp.concatenate(
            [row < valid_ref[2 * t + reach], row < valid_ref[2 * t + 1 + reach]], axis=0
        )
        u_split = split_heads(jnp.where(live, u_ref[own, :].astype(F32), 0.0))
        scores[t % 2] = dot(k_low[window, :], q_split, ((1,), (1,)))
        grads[t % 2] = dot(v_low[window, :], u_split, ((1,), (1,)))
        return q_unit, q_len, q_split, live, u_split

    stretch = scale * LOG2E
    parts = [slice(i, i + 32) for i in range(0, span, 32)]

    def fold(x):
        return x.reshape(4, 8, 2 * PAIR)

    following = begin(0)
    for t in range(steps):
        own, window = slice(t * PAIR, (t + 1) * PAIR), window_of(t)
        q_unit, q_len, q_split, live, u_split = following
        s_ref, g_ref, e_ref = scores.at[t % 2], grads.at[t % 2], raised.at[t % 2]
        w_low, c_low = w_lows.at[t % 2], c_lows.at[t % 2]
        if t + 1 < steps:
            following = begin(t + 1)

        peak = jnp.full((8, 2 * PAIR), -1e30, F32)
        for part in parts:
            half = bias[t, part, :]
            x = s_ref[part, :] * stretch + jnp.concatenate([half, half], axis=1)
            e_ref[part, :] = x
            peak = jnp.maximum(peak, jnp.max(fold(x), axis=0))
        peak = jnp.max(peak, axis=0, keepdims=True)
        total = jnp.zeros((8, 2 * PAIR), F32)
        centre = jnp.zeros((8, 2 * PAIR), F32)
        for part in parts:
            e = jnp.exp2(e_ref[part, :] - peak)
            e_ref[part, :] = e
            total = total + jnp.sum(fold(e), axis=0)
            centre = centre + jnp.sum(fold(e * g_ref[part, :]), axis=0)
        share = 1.0 / jnp.sum(total, axis=0, keepdims=True)
        centre = jnp.sum(centre, axis=0, keepdims=True) * share
        for part in parts:
            w = e_ref[part, :] * share
            w_low[part, :] = w.astype(BF)
            sg = w * (g_ref[part, :] - centre)
            ds = ds + jnp.sum(fold(sg * s_ref[part, :]), axis=0)
            c_low[part, :] = (sg * scale).astype(BF)

        def own_heads(turned):
            return jnp.concatenate([turned[:HD, :PAIR], turned[HD:, PAIR:]], axis=0)

        mixed = own_heads(dot(v_turn[:, window], w_low[...]))
        att_ref[own, :] = jnp.where(live, jnp.transpose(mixed), 0.0).astype(BF)
        row_lane = lax.broadcasted_iota(jnp.int32, (PAIR, PAIR), 1)
        limit = jnp.where(
            row_lane < BLK, valid_ref[2 * t + reach], valid_ref[2 * t + 1 + reach] + BLK
        )
        turn_ref[:, own] = jnp.where(row_lane < limit, mixed, 0.0).astype(BF)
        q_grad = jnp.transpose(own_heads(dot(k_turn[:, window], c_low[...])))
        dq_ref[own, :] = unit_back(q_unit, q_len, q_grad, same_head).astype(BF)
        dv[window, :] += dot(w_low[...], u_split)
        dk[window, :] += dot(c_low[...], q_split)

    def key_grad(part):
        place = slice(part, part + BLK)
        return unit_back(k_unit[place, :], k_len[place, :], dk[place, :], same_head)

    for part in range(0, rows, BLK):
        here = slice(part, part + BLK)
        dk_ref[here, :] = key_grad(margin + part)
        dv_ref[here, :] = dv[margin + part : margin + part + BLK, :]
    for part in range(0, margin, BLK):
        here = slice(part, part + BLK)
        far = margin + rows + part
        kb, ka = key_grad(part), key_grad(far)
        vb, va = dv[part : part + BLK, :], dv[far : far + BLK, :]
        rim1_ref[0, here, :] = jnp.where(even, ka, kb).astype(BF)
        rim1_ref[1, here, :] = jnp.where(even, va, vb).astype(BF)
        rim2_ref[0, here, :] = jnp.where(even, kb, ka).astype(BF)
        rim2_ref[1, here, :] = jnp.where(even, vb, va).astype(BF)
    ds_ref[0, :, :] = ds


def attention(packed, first, second, upstream, mult, valid, scales, even, pairs, begin=0, count=2, base=0):
    rows = packed.shape[0]
    width = count * PAIR
    margin = first.shape[0]
    pool = rows + 2 * margin
    held = len(pairs)
    stride = pairs[1] - pairs[0]
    steps = rows // PAIR
    span = WINDOW * BLK

    def at(offset):
        return lambda p, *_: (0, offset + p)

    return pl.pallas_call(
        attention_kernel,
        grid_spec=pltpu.PrefetchScalarGridSpec(
            num_scalar_prefetch=4,
            grid=(count,),
            in_specs=[
                pl.BlockSpec((rows, PAIR), at(begin)),
                pl.BlockSpec((rows, PAIR), at(held + begin)),
                pl.BlockSpec((rows, PAIR), at(2 * held + begin)),
                pl.BlockSpec((margin, PAIR), at(base + begin)),
                pl.BlockSpec((margin, PAIR), at(base + held + begin)),
                pl.BlockSpec((margin, PAIR), at(base + begin)),
                pl.BlockSpec((margin, PAIR), at(base + held + begin)),
                pl.BlockSpec((rows, PAIR), lambda p, *_: (0, pairs[begin] + stride * p)),
            ],
            out_specs=[
                pl.BlockSpec((rows, PAIR), at(0)),
                pl.BlockSpec((rows, PAIR), at(0)),
                pl.BlockSpec((rows, PAIR), at(0)),
                pl.BlockSpec((rows, PAIR), at(0)),
                pl.BlockSpec((2, margin, PAIR), lambda p, *_: (0, 0, p)),
                pl.BlockSpec((2, margin, PAIR), lambda p, *_: (0, 0, p)),
                pl.BlockSpec((1, 8, 2 * PAIR), lambda p, *_: (p, 0, 0)),
                pl.BlockSpec((PAIR, rows), lambda p, *_: (p, 0)),
            ],
            scratch_shapes=[
                pltpu.VMEM((pool, PAIR), F32),
                pltpu.VMEM((pool, PAIR), F32),
                pltpu.VMEM((pool, PAIR), BF),
                pltpu.VMEM((PAIR, pool), BF),
                pltpu.VMEM((pool, PAIR), BF),
                pltpu.VMEM((PAIR, pool), BF),
                pltpu.VMEM((steps, span, PAIR), F32),
                pltpu.VMEM((2, span, 2 * PAIR), F32),
                pltpu.VMEM((2, span, 2 * PAIR), F32),
                pltpu.VMEM((2, span, 2 * PAIR), F32),
                pltpu.VMEM((2, span, 2 * PAIR), BF),
                pltpu.VMEM((2, span, 2 * PAIR), BF),
                pltpu.VMEM((pool, PAIR), F32),
                pltpu.VMEM((pool, PAIR), F32),
            ],
        ),
        out_shape=[
            jax.ShapeDtypeStruct((rows, width), BF),
            jax.ShapeDtypeStruct((rows, width), BF),
            jax.ShapeDtypeStruct((rows, width), F32),
            jax.ShapeDtypeStruct((rows, width), F32),
            jax.ShapeDtypeStruct((2, margin, width), BF),
            jax.ShapeDtypeStruct((2, margin, width), BF),
            jax.ShapeDtypeStruct((count, 8, 2 * PAIR), F32),
            jax.ShapeDtypeStruct((width, rows), BF),
        ],
        compiler_params=pltpu.CompilerParams(vmem_limit_bytes=40 * 1024 * 1024),
        cost_estimate=pl.CostEstimate(
            flops=8 * 2 * 6 * count * steps * span * 256 * 128,
            bytes_accessed=rows * width * 20,
            transcendentals=count * steps * span * 256,
        ),
        name="block_attention",
    )(mult, valid, scales, even, packed, packed, packed, first, first, second, second, upstream)


def pick_kernel(core_ref, qkv_ref, out_ref, picked_ref):
    core = core_ref[0]
    at = 0
    for pairs in CHUNKS:
        for base in range(0, qkv_ref.shape[1], 8 * PAIR):
            for p in pairs:
                start = pl.multiple_of(base + 2 * p * PAIR + core * PAIR, PAIR)
                picked_ref[:, at : at + PAIR] = qkv_ref[:, pl.ds(start, PAIR)]
                at += PAIR
    half = out_ref.shape[1] // 2
    rows = out_ref[pl.ds(pl.multiple_of(core * PAIR, PAIR), PAIR), :]
    picked_ref[:PAIR, at:] = rows[:, :half]
    picked_ref[PAIR:, at:] = rows[:, half:]


def whole(shape):
    return pl.BlockSpec(shape, lambda *_: (0,) * len(shape))


def small_kernel(kernel, name, scalars, arrays, outs, scratch=()):
    return pl.pallas_call(
        kernel,
        grid_spec=pltpu.PrefetchScalarGridSpec(
            num_scalar_prefetch=len(scalars),
            grid=(1,),
            in_specs=[whole(a.shape) for a in arrays],
            out_specs=[whole(shape) for shape, _ in outs],
            scratch_shapes=list(scratch),
        ),
        out_shape=[jax.ShapeDtypeStruct(shape, kind) for shape, kind in outs],
        compiler_params=pltpu.CompilerParams(vmem_limit_bytes=40 * 1024 * 1024),
        name=name,
    )(*scalars, *arrays)


def pick_weights(w_qkv, w_out, core_flag):
    height, columns = w_qkv.shape
    wide = columns // 2 + w_out.shape[1] // 2
    return small_kernel(
        pick_kernel, "pick_weights", [core_flag], [w_qkv, w_out], [((height, wide), BF)]
    )[0]


def rim_kernel(even_ref, *refs):
    t_ref, rim1_ref, rim2_ref = refs[:3]
    even = even_ref[0] == 1
    margin = rim1_ref.shape[1]
    size = t_ref.shape[0] // 4

    def added(index, grad):
        rows = grad.shape[0]
        one, two = rim1_ref[index].astype(F32), rim2_ref[index].astype(F32)
        return jnp.concatenate(
            [
                grad[:margin] + jnp.where(even, two, one),
                grad[margin : rows - margin],
                grad[rows - margin :] + jnp.where(even, one, two),
            ],
            axis=0,
        ).astype(BF)

    if len(refs) == 10:
        q_ref, dk_ref, dv_ref, left_ref, right_ref, x_ref, y_ref = refs[3:]
        keys, values = added(0, dk_ref[...]), added(1, dv_ref[...])
        left_ref[:, : 2 * PAIR] = q_ref[...]
        left_ref[:, 2 * PAIR :] = keys[:, :PAIR]
        right_ref[:, :PAIR] = keys[:, PAIR:]
        right_ref[:, PAIR:] = values
    else:
        ka_ref, kb_ref, va_ref, vb_ref, left_ref, right_ref, x_ref, y_ref = refs[3:]
        left_ref[...] = added(0, jnp.concatenate([ka_ref[...], kb_ref[...]], axis=1))
        right_ref[...] = added(1, jnp.concatenate([va_ref[...], vb_ref[...]], axis=1))
    x_ref[...] = dot(t_ref[: 2 * size, :], left_ref[...]).astype(BF)
    y_ref[...] = dot(t_ref[size : 3 * size, :], right_ref[...]).astype(BF)


def leave_kernel(
    scene_ref, t_ref, a0_ref, a1_ref, a2_ref, cot_ref, q1_ref, q2_ref, left_ref, right_ref, fx_ref, fy_ref,
    x_ref, y_ref, kl_ref, kr_ref, e_ref, o_ref, at_ref,
):
    size = t_ref.shape[0] // 4
    quarter = cot_ref.shape[1] // 4
    at_ref[0] = a0_ref[:PAIR, :]
    at_ref[3] = a0_ref[PAIR:, :]
    at_ref[1] = a1_ref[...]
    at_ref[2] = a2_ref[...]
    x_ref[: 2 * size, :PAIR] = dot(t_ref[: 2 * size, :], q1_ref[...]).astype(BF)
    y_ref[: 2 * size, :PAIR] = dot(t_ref[size : 3 * size, :], q2_ref[...]).astype(BF)
    for i, k in enumerate(ORDER):
        grad = dot(at_ref[jnp.bitwise_xor(scene_ref[0], k)], cot_ref[...])
        evens = jnp.concatenate(
            [grad[:, :quarter], grad[:, 2 * quarter : 3 * quarter]], axis=0
        )
        odds = jnp.concatenate(
            [grad[:, quarter : 2 * quarter], grad[:, 3 * quarter :]], axis=0
        )
        if i < 2:
            x_ref[i * size : (i + 1) * size, PAIR:] = evens.astype(BF)
        else:
            e_ref[i - 2] = evens
        if i in (1, 2):
            y_ref[(i - 1) * size : i * size, PAIR:] = odds.astype(BF)
        else:
            o_ref[i // 3] = odds
    left, right = left_ref[...], right_ref[...]
    y_ref[2 * size :, :] = (
        dot(t_ref[2 * size : 3 * size, :], left) + fx_ref[size:, :].astype(F32)
    ).astype(BF)
    x_ref[2 * size :, :] = (dot(t_ref[:size, :], right) + fy_ref[:size, :].astype(F32)).astype(BF)
    kl_ref[...] = dot(t_ref[3 * size :, :], left) + fx_ref[:size, :].astype(F32)
    kr_ref[...] = dot(t_ref[3 * size :, :], right) + fy_ref[size:, :].astype(F32)


def second_kernel(
    t_ref, q1_ref, q2_ref, key_ref, value_ref, ex_ref, ey_ref, lx_ref, ly_ref, e_ref, o_ref,
    x_ref, y_ref, kl_ref, kr_ref,
):
    size = t_ref.shape[0] // 4

    def term(place, query_ref, other_ref, extra, early_ref, late_ref, half):
        block = t_ref[place * size : (place + 1) * size, :]
        here = slice(half * size, (half + 1) * size)
        early, late = early_ref[here, :].astype(F32), late_ref[here, :].astype(F32)
        return jnp.concatenate(
            [
                dot(block, query_ref[...]) + early[:, :PAIR],
                dot(block, other_ref[...]) + late,
                extra + early[:, PAIR:],
            ],
            axis=1,
        )

    y_ref[...] = term(2, q1_ref, key_ref, e_ref[0], ex_ref, lx_ref, 1).astype(BF)
    x_ref[...] = term(0, q2_ref, value_ref, o_ref[0], ey_ref, ly_ref, 0).astype(BF)
    kl_ref[...] = term(3, q1_ref, key_ref, e_ref[1], ex_ref, lx_ref, 0)
    kr_ref[...] = term(3, q2_ref, value_ref, o_ref[1], ey_ref, ly_ref, 1)


def gate(value, *others):
    return lax.optimization_barrier((value,) + others)[0]


def pick_groups(array, axis, unit, core):
    size = array.shape[axis]
    picked = [
        jnp.where(
            core == 0,
            lax.slice_in_dim(array, at, at + unit, axis=axis),
            lax.slice_in_dim(array, at + unit, at + 2 * unit, axis=axis),
        )
        for at in range(0, size, 2 * unit)
    ]
    return jnp.concatenate(picked, axis=axis)


def spread_groups(array, axis, unit, core):
    groups = jnp.split(array, array.shape[axis] // unit, axis=axis)
    parts = []
    for group in groups:
        empty = jnp.zeros_like(group)
        parts += [jnp.where(core == 0, group, empty), jnp.where(core == 0, empty, group)]
    return jnp.concatenate(parts, axis=axis)


def in_order(core, own, other, axis):
    first = jnp.where(core == 0, own, other)
    second = jnp.where(core == 0, other, own)
    return jnp.concatenate([first, second], axis=axis)


def xor_blocks(blocks, index):
    odd = (index & 1) == 1
    high = (index & 2) == 2
    near = [jnp.where(odd, blocks[k ^ 1], blocks[k]) for k in range(4)]
    return [jnp.where(high, near[k ^ 2], near[k]) for k in range(4)]


ORDER = (1, 3, 2, 0)
CHUNKS = ((0, 3), (1, 2))


def square(value, step):
    return lax.ppermute(value, "fsdp", [(i, i ^ step) for i in range(4)])


def gather_near(shard):
    return square(shard, 1), square(shard, 2)


def gather_far(near, far):
    half = near.shape[0] // 2
    top = square(far[:half], 1)
    low = square(near[half:], 2)
    return jnp.concatenate([top, low], axis=0)


def chips(value, step, n_vox):
    return lax.ppermute(value, "vox", [(i, i ^ (2 * step)) for i in range(n_vox)])


def on_device(
    tokens, gain, w_qkv, w_out, logit_scale, key_blocks, slot_count, valid_voxels, cotangent
):
    own_tokens = tokens[0]
    own_cotangent = cotangent[0]
    own_rows, model_width = own_tokens.shape
    rows = 2 * own_rows
    own_blocks = key_blocks.shape[1]
    blocks = 2 * own_blocks
    slot_total = key_blocks.shape[2]
    reach = own_blocks // 2
    margin = reach * BLK
    n_vox = lax.axis_size("vox")
    n_fsdp = lax.axis_size("fsdp")
    n_chip = n_vox // 2
    place = lax.axis_index("vox")
    scene = lax.axis_index("fsdp")
    core = place % 2
    chip = place // 2
    fast = n_vox == 8 and n_fsdp == 4
    unit = 128 if fast else 64
    swap = [(i, i ^ 1) for i in range(n_vox)]
    even, low = chip % 2 == 0, chip < 2
    even_flag, core_flag, scene_flag = [
        jnp.reshape(x, (1,)).astype(jnp.int32) for x in (even, core, scene)
    ]
    near_chips = [(i, i ^ 2) for i in range(n_vox)]
    far_chips = []
    for i in range(n_vox):
        to = i // 2 + (1 if i // 2 % 2 else -1)
        far_chips.append((i, 2 * to + i % 2 if 0 <= to < n_chip else i))
    part_width = model_width // 2

    def columns_of(array, pairs):
        return jnp.concatenate(
            [
                array[:, base + p * PAIR : base + (p + 1) * PAIR]
                for base in range(0, array.shape[1], part_width)
                for p in pairs
            ],
            axis=1,
        )

    if fast:
        shard = pick_weights(w_qkv, w_out, core_flag)
        near, far = gather_near(shard)
        diag = gather_far(near, far)
        wide = 3 * part_width // 2
        weights_0, weights_1 = [
            jnp.concatenate([block[:, at : at + wide] for block in (near, diag, far, shard)], axis=0)
            for at in (0, wide)
        ]
        wide = 2 * wide
        out_blocks = [
            jnp.concatenate([block[:PAIR, wide:], block[PAIR:, wide:]], axis=1)
            for block in (shard, near, far, diag)
        ]
        out_half = jnp.concatenate(xor_blocks(out_blocks, scene), axis=0)
    else:
        core_qkv = pick_groups(w_qkv, 1, unit, core)
        core_out = pick_groups(w_out, 0, unit, core)
        weights_0, weights_1 = [
            lax.all_gather(columns_of(core_qkv, pairs), "fsdp", axis=0, tiled=True)
            for pairs in CHUNKS
        ]
        out_half = lax.all_gather(core_out, "fsdp", axis=0, tiled=True)

    other_tokens = lax.ppermute(own_tokens, "vox", swap)
    other_cotangent = lax.ppermute(own_cotangent, "vox", swap)
    lists = jnp.concatenate([key_blocks[0], slot_count[0][:, None]], axis=1)
    all_lists = in_order(
        core, lists, lax.ppermute(lists.astype(F32), "vox", swap).astype(jnp.int32), 0
    )
    chip_tokens = in_order(core, own_tokens, other_tokens, 0)
    chip_cotangent = in_order(core, own_cotangent, other_cotangent, 0)

    first_block = chip * blocks
    pool_blocks = blocks + 2 * reach
    window_id = (
        all_lists[:, :slot_total] - first_block + reach
        - 2 * (jnp.arange(blocks, dtype=jnp.int32) // 2)[:, None]
    )
    used = jnp.arange(slot_total, dtype=jnp.int32)[None, :] < all_lists[:, slot_total:]
    hits = jnp.logical_and(
        window_id[:, :, None] == jnp.arange(WINDOW, dtype=jnp.int32), used[:, :, None]
    )
    mult = jnp.sum(hits.astype(jnp.int32), axis=1)
    scene_total = valid_voxels.shape[1]
    pool_ids = first_block - reach + jnp.arange(pool_blocks, dtype=jnp.int32)
    valid = jnp.take(valid_voxels[0], jnp.clip(pool_ids, 0, scene_total - 1))
    group_heads = unit // HD
    scales = pick_groups(logit_scale, 0, group_heads, core)

    wide = chip_tokens.astype(F32)
    inverse = lax.rsqrt(jnp.mean(wide * wide, axis=1, keepdims=True) + EPS)
    normed = (wide * inverse * gain).astype(BF)
    if fast:
        turned = xor_blocks(jnp.split(normed, 4, axis=1), scene)
        normed = jnp.concatenate([turned[k] for k in ORDER], axis=1)
        normed_t = jnp.transpose(normed)

    def pairings(first, second):
        return lax.ppermute(first, "vox", near_chips), lax.ppermute(second, "vox", far_chips)

    def heads_of(packed, upstream, chunk, begin=0, count=2):
        pairs = CHUNKS[chunk]
        used = pairs[begin : begin + count]
        chunk_scales = jnp.concatenate([scales[2 * p : 2 * p + 2] for p in used])
        return attention(
            packed, *halos, upstream, mult, valid, chunk_scales, even_flag, pairs, begin, count,
            4 * chunk,
        )

    def with_rims(grad, first, second):
        first, second = first.astype(F32), second.astype(F32)
        return jnp.concatenate(
            [
                grad[:margin] + jnp.where(even, second, first),
                grad[margin : rows - margin],
                grad[rows - margin :] + jnp.where(even, first, second),
            ],
            axis=0,
        ).astype(BF)

    def key_value_grads(keys, values, rims):
        return [with_rims(g, rims[0][i], rims[1][i]) for i, g in enumerate((keys, values))]

    def out_rows(pairs):
        return jnp.concatenate([out_half[p * PAIR : (p + 1) * PAIR] for p in pairs], axis=0)

    def groups_of(left, right, chunk):
        half = 3 * PAIR
        groups = [left[:, k * PAIR : (k + 1) * PAIR] for k in range(3)]
        groups += [right[:, k * PAIR : (k + 1) * PAIR] for k in range(3)]
        sets = ((0, 3, 4), (1, 2, 5)) if chunk == 0 else ((0, 3, 2), (1, 4, 5))
        evens = jnp.concatenate([groups[k] for k in sets[0]] + [left[:, half:]], axis=1)
        odds = jnp.concatenate([groups[k] for k in sets[1]] + [right[:, half:]], axis=1)
        return jnp.where(even, evens, odds), jnp.where(even, odds, evens).astype(BF)

    def halves_of(kept):
        left, right = kept[:, : 2 * PAIR], kept[:, PAIR : 3 * PAIR]
        if kept.shape[1] > 3 * PAIR:
            more = kept[:, 3 * PAIR :]
            cut = more.shape[0] // 2
            left = jnp.concatenate([left, more[:cut]], axis=0)
            right = jnp.concatenate([right, more[cut:]], axis=0)
        return jnp.where(low, left, right), jnp.where(low, right, left).astype(BF)

    packed_0, packed_1 = [dot(normed, weight).astype(BF) for weight in (weights_0, weights_1)]
    query_width = part_width // 2
    top, bottom = [
        jnp.concatenate([packed[at, query_width:] for packed in (packed_0, packed_1)], axis=1)
        for at in (slice(0, margin), slice(rows - margin, rows))
    ]
    halos = pairings(jnp.where(even, bottom, top), jnp.where(even, top, bottom))
    upstream = dot(chip_cotangent, out_half, ((1,), (1,))).astype(BF)
    first = heads_of(packed_0, upstream, 0)
    rims_0 = pairings(first[4], first[5])
    third = heads_of(packed_1, gate(upstream, first[4], first[5]), 1, 0, 1)
    rims_0 = [gate(rim, third[6]) for rim in rims_0]
    half = 3 * query_width // 2
    if fast:
        left_0, right_0, to_x, to_y = small_kernel(
            rim_kernel, "rims_first", [even_flag],
            [normed_t, *rims_0, first[1], first[2], first[3]],
            [((rows, half), BF)] * 2 + [((model_width // 2, half), BF)] * 2,
        )
        from_x0, from_y0 = square(to_x, 1), square(to_y, 2)
        fourth_in = gate(upstream, to_x, to_y)
    else:
        key_0, value_0 = key_value_grads(first[2], first[3], rims_0)
        grad_0 = jnp.concatenate([first[1], key_0, value_0], axis=1)
        fourth_in = upstream
    fourth = heads_of(packed_1, fourth_in, 1, 1, 1)
    rims_1 = pairings(*[jnp.concatenate([third[i], fourth[i]], axis=2) for i in (4, 5)])

    att_0 = gate(first[0], fourth[6])
    att_1 = jnp.concatenate([third[0], fourth[0]], axis=1)
    if fast:
        quarter = model_width // 4
        to_x, to_y, left, right, evens, odds = small_kernel(
            leave_kernel, "leave_early", [scene_flag],
            [normed_t, first[7], third[7], fourth[7], chip_cotangent, third[1], fourth[1],
             left_0, right_0, from_x0, from_y0],
            [((3 * quarter, half), BF)] * 2
            + [((quarter, half), F32)] * 2
            + [((2, quarter, quarter), F32)] * 2,
            [pltpu.VMEM((4, PAIR, rows), BF)],
        )
        early_x, early_y = square(to_x, 1), square(to_y, 2)
        att_0, att_1 = lax.optimization_barrier((att_0, att_1, to_x, to_y))[:2]
    mixed_part = dot(att_0, out_rows(CHUNKS[0])) + dot(att_1, out_rows(CHUNKS[1]))

    if fast:
        key_1, value_1, to_x, to_y = small_kernel(
            rim_kernel, "rims_second", [even_flag],
            [normed_t, *rims_1, third[2], fourth[2], third[3], fourth[3]],
            [((rows, query_width), BF)] * 2 + [((model_width // 2, query_width), BF)] * 2,
        )
        late_x, late_y = square(to_x, 1), square(to_y, 2)
        left_0, early_x, early_y = lax.optimization_barrier(
            (left_0, early_x, early_y, to_x, to_y)
        )[:3]
        grad_0 = jnp.concatenate([left_0, right_0], axis=1)
    else:
        key_1, value_1 = key_value_grads(
            *[jnp.concatenate([third[i], fourth[i]], axis=1) for i in (2, 3)], rims_1
        )
    grad_1 = jnp.concatenate([third[1], fourth[1], key_1, value_1], axis=1)

    ngrad_part = dot(grad_0, weights_0, ((1,), (1,))) + dot(grad_1, weights_1, ((1,), (1,)))
    mixed_mine = lax.dynamic_slice_in_dim(mixed_part, core * own_rows, own_rows, 0)
    mixed_theirs = lax.dynamic_slice_in_dim(mixed_part, (1 - core) * own_rows, own_rows, 0)
    mixed = (
        own_tokens.astype(F32) + (mixed_mine + lax.ppermute(mixed_theirs, "vox", swap))
    ).astype(BF)

    ngrad_mine = lax.dynamic_slice_in_dim(ngrad_part, core * own_rows, own_rows, 0)
    ngrad_theirs = lax.dynamic_slice_in_dim(ngrad_part, (1 - core) * own_rows, own_rows, 0)
    normed_grad = ngrad_mine + lax.ppermute(ngrad_theirs, "vox", swap)
    if fast:
        held = jnp.split(normed_grad, 4, axis=1)
        normed_grad = jnp.concatenate(
            xor_blocks([held[ORDER.index(k)] for k in range(4)], scene), axis=1
        )

    own_wide = own_tokens.astype(F32)
    own_inverse = lax.rsqrt(jnp.mean(own_wide * own_wide, axis=1, keepdims=True) + EPS)
    gain_grad = jnp.sum(normed_grad * own_wide * own_inverse, axis=0)
    scaled_grad = normed_grad * gain
    token_grad = (
        own_cotangent.astype(F32)
        + own_inverse
        * (
            scaled_grad
            - own_wide
            * own_inverse
            * own_inverse
            * jnp.mean(scaled_grad * own_wide, axis=1, keepdims=True)
        )
    ).astype(BF)

    scale_parts = {}
    for pairs, sums in zip(CHUNKS, (first[6], jnp.concatenate([third[6], fourth[6]], axis=0))):
        sums = jnp.sum(sums.reshape(2, 8, 2, PAIR), axis=(1, 3))
        for i, p in enumerate(pairs):
            scale_parts[p] = sums[i]
    scale_part = jnp.concatenate([scale_parts[p] for p in range(len(scale_parts))])
    scale_grad = spread_groups(scale_part, 0, group_heads, core)

    if fast:
        small = jnp.concatenate([gain_grad, scale_grad, jnp.zeros((112,), F32)]).reshape(9, 128)
        height = model_width // 4
        kept_0, sent = groups_of(
            left + early_y[2 * height :].astype(F32), right + early_x[2 * height :].astype(F32), 0
        )
        got_0 = chips(sent, 1, n_vox)
        late_x, late_y = lax.optimization_barrier((late_x, late_y, small))[:2]
        small = small + square(small, 1)
        to_x, to_y, left, right = small_kernel(
            second_kernel, "second_exchange", [],
            [normed_t, third[1], fourth[1], key_1, value_1, early_x, early_y, late_x, late_y, evens, odds],
            [((height, half + quarter), BF)] * 2 + [((height, half + quarter), F32)] * 2,
        )
        end_x, end_y = square(to_x, 1), square(to_y, 2)
        got_0, small = lax.optimization_barrier((got_0, small, to_x, to_y))[:2]
        small = small + square(small, 2)
        kept_0, sent = halves_of(kept_0 + got_0.astype(F32))
        got_0 = chips(sent, 2, n_vox)
        end_x, end_y = lax.optimization_barrier((end_x, end_y, token_grad, mixed))[:2]
        kept_1, sent = groups_of(left + end_y.astype(F32), right + end_x.astype(F32), 1)
        got_1 = chips(sent, 1, n_vox)
        small = gate(small, sent)
        small = small + lax.ppermute(small, "vox", swap)
        small = small + chips(small, 1, n_vox)
        kept_1, sent = halves_of(kept_1 + got_1.astype(F32))
        got_1 = chips(sent, 2, n_vox)
        small = gate(small, sent)
        small = small + chips(small, 2, n_vox)
        small = small.reshape(-1)
        summed_gain, summed_scale = small[:model_width], small[model_width : model_width + HEADS]
        kept_1 = kept_1 + got_1.astype(F32)
        qkv_sums = [kept_0 + got_0.astype(F32), kept_1[:height]]
        out_sum = kept_1[height:]
    else:
        out_sums = [dot(att, chip_cotangent, ((0,), (0,))) for att in (att_0, att_1)]
        qkv_sums = [dot(normed, grad, ((0,), (0,))) for grad in (grad_0, grad_1)]
        summed_gain, summed_scale = lax.psum((gain_grad, scale_grad), ("vox", "fsdp"))

    if fast:
        half = out_sum.shape[1] // 2
        first, second = out_sum[:, :half], out_sum[:, half:]
        out_other = lax.ppermute(jnp.where(core == 0, second, first), "vox", swap)
        summed_out = in_order(core, jnp.where(core == 0, first, second), out_other, 0)

        a0, a1 = qkv_sums[0][:, :PAIR], qkv_sums[0][:, PAIR:]
        b0, b1 = qkv_sums[1][:, :PAIR], qkv_sums[1][:, PAIR:]

        def by_chip(options):
            value = options[3]
            for k in range(3):
                value = jnp.where(chip == k, options[k], value)
            return value

        g0 = by_chip((a0, a0, b1, b0))
        g1 = by_chip((b0, a1, a0, b1))
        g2 = by_chip((b1, b0, a1, a1))
        got = lax.ppermute(jnp.where(core == 0, g2, g0), "vox", swap)
        summed_qkv = jnp.concatenate(
            [
                jnp.where(core == 0, g0, g1),
                got,
                jnp.where(core == 0, g1, g2),
            ],
            axis=1,
        )
    else:
        by_pair = {}
        cols = {}
        for pairs, out_total, qkv_total in zip(CHUNKS, out_sums, qkv_sums):
            for i, p in enumerate(pairs):
                by_pair[p] = out_total[i * PAIR : (i + 1) * PAIR]
                for j in range(3):
                    at = (2 * j + i) * PAIR
                    cols[4 * j + p] = qkv_total[:, at : at + PAIR]
        out_total = jnp.concatenate([by_pair[p] for p in range(4)], axis=0)
        qkv_total = jnp.concatenate([cols[k] for k in range(12)], axis=1)
        out_total = spread_groups(out_total, 0, unit, core)
        qkv_total = lax.psum_scatter(qkv_total, "fsdp", scatter_dimension=0, tiled=True)
        qkv_total = spread_groups(qkv_total, 1, unit, core)
        summed_qkv = lax.psum_scatter(qkv_total, "vox", scatter_dimension=1, tiled=True)
        out_total = lax.psum_scatter(out_total, "fsdp", scatter_dimension=0, tiled=True)
        summed_out = lax.psum_scatter(out_total, "vox", scatter_dimension=1, tiled=True)

    return (
        mixed[None],
        token_grad[None],
        summed_qkv,
        summed_out,
        summed_gain,
        summed_scale,
    )


def solution(mesh):
    return jax.shard_map(
        on_device,
        mesh=mesh,
        in_specs=(
            P("fsdp", "vox", None),
            P(),
            P("fsdp", None),
            P("fsdp", None),
            P(),
            P("fsdp", "vox", None),
            P("fsdp", "vox"),
            P("fsdp", None),
            P("fsdp", "vox", None),
        ),
        out_specs=(
            P("fsdp", "vox", None),
            P("fsdp", "vox", None),
            P("fsdp", "vox"),
            P("fsdp", "vox"),
            P(),
            P(),
        ),
        check_vma=False,
    )
```

```python
import functools

import jax
import jax.numpy as jnp
from jax import lax
from jax.experimental import pallas as pl
from jax.experimental.pallas import tpu as pltpu
from jax.sharding import PartitionSpec as P

HEADS = 16
HD = 64
PAIR = 2 * HD
BLK = 64
WINDOW = 8
EPS = 1e-06
LOG2E = 1.4426950408889634
BF = jnp.bfloat16
F32 = jnp.float32


def dot(a, b, dims=((1,), (0,))):
    return lax.dot_general(a, b, (dims, ((), ())), preferred_element_type=F32)


def head_sums(x, same_head):
    high = x.astype(BF)
    low = (x - high.astype(F32)).astype(BF)
    return dot(high, same_head) + dot(low, same_head)


def unit_rows(x, same_head):
    length = jnp.sqrt(head_sums(x * x, same_head) + EPS)
    return x / length, length


def unit_back(unit, length, grad, same_head):
    return (grad - unit * head_sums(unit * grad, same_head)) / length


def attention_kernel(
    mult_ref, valid_ref, scale_ref, even_ref,
    q_ref, k_ref, v_ref, k1_ref, v1_ref, k2_ref, v2_ref, u_ref,
    *refs,
):
    carried, refs = (refs[:3], refs[3:]) if len(refs) > 22 else ((), refs)
    att_ref, dq_ref, dk_ref, dv_ref, rim1_ref, rim2_ref, ds_ref, turn_ref = refs[:8]
    k_unit, k_len, k_low, k_turn, v_low, v_turn, bias = refs[8:15]
    scores, grads, raised, w_lows, c_lows, dk, dv = refs[15:]
    held = slice(PAIR, 2 * PAIR) if carried else slice(0, PAIR)
    if carried:
        att_ref[:, :PAIR] = carried[0][...]
        rim1_ref[:, :, :PAIR] = carried[1][...]
        rim2_ref[:, :, :PAIR] = carried[2][...]
    rows = q_ref.shape[0]
    margin = k1_ref.shape[0]
    even = even_ref[0] == 1
    pool = rows + 2 * margin
    reach = margin // BLK
    steps = rows // PAIR
    span = WINDOW * BLK
    pair = pl.program_id(0)

    lane = lax.broadcasted_iota(jnp.int32, (BLK, PAIR), 1)
    row = lax.broadcasted_iota(jnp.int32, (BLK, PAIR), 0)
    head_a = lax.broadcasted_iota(jnp.int32, (PAIR, PAIR), 0) < HD
    head_b = lax.broadcasted_iota(jnp.int32, (PAIR, PAIR), 1) < HD
    same_head = jnp.where(head_a == head_b, 1.0, 0.0).astype(BF)
    first_lanes = head_b

    @pl.when(pair == 0)
    def _():
        for t in range(steps):
            for w in range(WINDOW):
                count = jnp.where(lane < BLK, mult_ref[2 * t, w], mult_ref[2 * t + 1, w])
                live = row < valid_ref[2 * t + w]
                seen = jnp.where(live, count, 0).astype(F32)
                bias[t, w * BLK : (w + 1) * BLK, :] = jnp.where(
                    seen > 0.0, jnp.log2(jnp.maximum(seen, 1.0)), -1e30
                )

    def split_heads(x):
        return jnp.concatenate(
            [jnp.where(first_lanes, x, 0.0), jnp.where(first_lanes, 0.0, x)], axis=0
        ).astype(BF)

    def take(at, keys, values):
        unit, length = unit_rows(keys.astype(F32), same_head)
        place = slice(at, at + keys.shape[0])
        k_unit[place, :] = unit
        k_len[place, :] = length
        k_low[place, :] = unit.astype(BF)
        v_low[place, :] = values

    for part in range(0, margin, BLK):
        here = slice(part, part + BLK)
        k1, k2 = k1_ref[here, :].astype(F32), k2_ref[here, :].astype(F32)
        v1, v2 = v1_ref[here, :].astype(F32), v2_ref[here, :].astype(F32)
        take(part, jnp.where(even, k2, k1), jnp.where(even, v2, v1).astype(BF))
        take(margin + rows + part, jnp.where(even, k1, k2), jnp.where(even, v1, v2).astype(BF))
    for part in range(0, rows, PAIR):
        here = slice(part, part + PAIR)
        take(margin + part, k_ref[here, :], v_ref[here, :])
    for part in range(0, pool, 128):
        place = slice(part, part + 128)
        k_turn[:, place] = jnp.transpose(k_low[place, :].astype(F32)).astype(BF)
        v_turn[:, place] = jnp.transpose(v_low[place, :].astype(F32)).astype(BF)

    dk[...] = jnp.zeros_like(dk)
    dv[...] = jnp.zeros_like(dv)
    wide_lane = lax.broadcasted_iota(jnp.int32, (1, 2 * PAIR), 1)
    scale = jnp.where(wide_lane < PAIR, scale_ref[2 * pair], scale_ref[2 * pair + 1])
    ds = jnp.zeros((8, 2 * PAIR), F32)

    def window_of(t):
        return slice(t * PAIR, t * PAIR + span)

    def begin(t):
        own, window = slice(t * PAIR, (t + 1) * PAIR), window_of(t)
        q_unit, q_len = unit_rows(q_ref[own, :].astype(F32), same_head)
        q_split = split_heads(q_unit)
        live = jnp.concatenate(
            [row < valid_ref[2 * t + reach], row < valid_ref[2 * t + 1 + reach]], axis=0
        )
        u_split = split_heads(jnp.where(live, u_ref[own, :].astype(F32), 0.0))
        scores[t % 2] = dot(k_low[window, :], q_split, ((1,), (1,)))
        grads[t % 2] = dot(v_low[window, :], u_split, ((1,), (1,)))
        return q_unit, q_len, q_split, live, u_split

    stretch = scale * LOG2E
    parts = [slice(i, i + 32) for i in range(0, span, 32)]

    def fold(x):
        return x.reshape(4, 8, 2 * PAIR)

    following = begin(0)
    for t in range(steps):
        own, window = slice(t * PAIR, (t + 1) * PAIR), window_of(t)
        q_unit, q_len, q_split, live, u_split = following
        s_ref, g_ref, e_ref = scores.at[t % 2], grads.at[t % 2], raised.at[t % 2]
        w_low, c_low = w_lows.at[t % 2], c_lows.at[t % 2]
        if t + 1 < steps:
            following = begin(t + 1)

        peak = jnp.full((8, 2 * PAIR), -1e30, F32)
        for part in parts:
            half = bias[t, part, :]
            x = s_ref[part, :] * stretch + jnp.concatenate([half, half], axis=1)
            e_ref[part, :] = x
            peak = jnp.maximum(peak, jnp.max(fold(x), axis=0))
        peak = jnp.max(peak, axis=0, keepdims=True)
        total = jnp.zeros((8, 2 * PAIR), F32)
        centre = jnp.zeros((8, 2 * PAIR), F32)
        for part in parts:
            e = jnp.exp2(e_ref[part, :] - peak)
            e_ref[part, :] = e
            total = total + jnp.sum(fold(e), axis=0)
            centre = centre + jnp.sum(fold(e * g_ref[part, :]), axis=0)
        share = 1.0 / jnp.sum(total, axis=0, keepdims=True)
        centre = jnp.sum(centre, axis=0, keepdims=True) * share
        for part in parts:
            w = e_ref[part, :] * share
            w_low[part, :] = w.astype(BF)
            sg = w * (g_ref[part, :] - centre)
            ds = ds + jnp.sum(fold(sg * s_ref[part, :]), axis=0)
            c_low[part, :] = (sg * scale).astype(BF)

        def own_heads(turned):
            return jnp.concatenate([turned[:HD, :PAIR], turned[HD:, PAIR:]], axis=0)

        mixed = own_heads(dot(v_turn[:, window], w_low[...]))
        att_ref[own, held] = jnp.where(live, jnp.transpose(mixed), 0.0).astype(BF)
        row_lane = lax.broadcasted_iota(jnp.int32, (PAIR, PAIR), 1)
        limit = jnp.where(
            row_lane < BLK, valid_ref[2 * t + reach], valid_ref[2 * t + 1 + reach] + BLK
        )
        turn_ref[:, own] = jnp.where(row_lane < limit, mixed, 0.0).astype(BF)
        q_grad = jnp.transpose(own_heads(dot(k_turn[:, window], c_low[...])))
        dq_ref[own, :] = unit_back(q_unit, q_len, q_grad, same_head).astype(BF)
        dv[window, :] += dot(w_low[...], u_split)
        dk[window, :] += dot(c_low[...], q_split)

    def key_grad(part):
        place = slice(part, part + BLK)
        return unit_back(k_unit[place, :], k_len[place, :], dk[place, :], same_head)

    for part in range(0, rows, BLK):
        here = slice(part, part + BLK)
        dk_ref[here, :] = key_grad(margin + part)
        dv_ref[here, :] = dv[margin + part : margin + part + BLK, :]
    for part in range(0, margin, BLK):
        here = slice(part, part + BLK)
        far = margin + rows + part
        kb, ka = key_grad(part), key_grad(far)
        vb, va = dv[part : part + BLK, :], dv[far : far + BLK, :]
        rim1_ref[0, here, held] = jnp.where(even, ka, kb).astype(BF)
        rim1_ref[1, here, held] = jnp.where(even, va, vb).astype(BF)
        rim2_ref[0, here, held] = jnp.where(even, kb, ka).astype(BF)
        rim2_ref[1, here, held] = jnp.where(even, vb, va).astype(BF)
    ds_ref[0, :, :] = ds


def attention(packed, first, second, upstream, mult, valid, scales, even, pairs, begin=0, count=2, base=0, carried=()):
    rows = packed.shape[0]
    width = count * PAIR
    both = width + (PAIR if carried else 0)
    margin = first.shape[0]
    pool = rows + 2 * margin
    held = len(pairs)
    stride = pairs[1] - pairs[0]
    steps = rows // PAIR
    span = WINDOW * BLK

    def at(offset):
        return lambda p, *_: (0, offset + p)

    return pl.pallas_call(
        attention_kernel,
        grid_spec=pltpu.PrefetchScalarGridSpec(
            num_scalar_prefetch=4,
            grid=(count,),
            in_specs=[
                pl.BlockSpec((rows, PAIR), at(begin)),
                pl.BlockSpec((rows, PAIR), at(held + begin)),
                pl.BlockSpec((rows, PAIR), at(2 * held + begin)),
                pl.BlockSpec((margin, PAIR), at(base + begin)),
                pl.BlockSpec((margin, PAIR), at(base + held + begin)),
                pl.BlockSpec((margin, PAIR), at(base + begin)),
                pl.BlockSpec((margin, PAIR), at(base + held + begin)),
                pl.BlockSpec((rows, PAIR), lambda p, *_: (0, pairs[begin] + stride * p)),
            ]
            + [whole(array.shape) for array in carried],
            out_specs=[
                pl.BlockSpec((rows, both // count), at(0)),
                pl.BlockSpec((rows, PAIR), at(0)),
                pl.BlockSpec((rows, PAIR), at(0)),
                pl.BlockSpec((rows, PAIR), at(0)),
                pl.BlockSpec((2, margin, both // count), lambda p, *_: (0, 0, p)),
                pl.BlockSpec((2, margin, both // count), lambda p, *_: (0, 0, p)),
                pl.BlockSpec((1, 8, 2 * PAIR), lambda p, *_: (p, 0, 0)),
                pl.BlockSpec((PAIR, rows), lambda p, *_: (p, 0)),
            ],
            scratch_shapes=[
                pltpu.VMEM((pool, PAIR), F32),
                pltpu.VMEM((pool, PAIR), F32),
                pltpu.VMEM((pool, PAIR), BF),
                pltpu.VMEM((PAIR, pool), BF),
                pltpu.VMEM((pool, PAIR), BF),
                pltpu.VMEM((PAIR, pool), BF),
                pltpu.VMEM((steps, span, PAIR), F32),
                pltpu.VMEM((2, span, 2 * PAIR), F32),
                pltpu.VMEM((2, span, 2 * PAIR), F32),
                pltpu.VMEM((2, span, 2 * PAIR), F32),
                pltpu.VMEM((2, span, 2 * PAIR), BF),
                pltpu.VMEM((2, span, 2 * PAIR), BF),
                pltpu.VMEM((pool, PAIR), F32),
                pltpu.VMEM((pool, PAIR), F32),
            ],
        ),
        out_shape=[
            jax.ShapeDtypeStruct((rows, both), BF),
            jax.ShapeDtypeStruct((rows, width), BF),
            jax.ShapeDtypeStruct((rows, width), F32),
            jax.ShapeDtypeStruct((rows, width), F32),
            jax.ShapeDtypeStruct((2, margin, both), BF),
            jax.ShapeDtypeStruct((2, margin, both), BF),
            jax.ShapeDtypeStruct((count, 8, 2 * PAIR), F32),
            jax.ShapeDtypeStruct((width, rows), BF),
        ],
        compiler_params=pltpu.CompilerParams(vmem_limit_bytes=24 * 1024 * 1024),
        cost_estimate=pl.CostEstimate(
            flops=8 * 2 * 6 * count * steps * span * 256 * 128,
            bytes_accessed=rows * width * 20,
            transcendentals=count * steps * span * 256,
        ),
        name="block_attention",
    )(
        mult, valid, scales, even,
        packed, packed, packed, first, first, second, second, upstream, *carried,
    )


def pick_kernel(core_ref, qkv_ref, out_ref, top_ref, low_ref):
    core = core_ref[0]
    at = 0
    for pairs in CHUNKS:
        for base in range(0, qkv_ref.shape[1], 8 * PAIR):
            for p in pairs:
                start = pl.multiple_of(base + 2 * p * PAIR + core * PAIR, PAIR)
                top_ref[:, at : at + PAIR] = qkv_ref[:PAIR, pl.ds(start, PAIR)]
                low_ref[:, at : at + PAIR] = qkv_ref[PAIR:, pl.ds(start, PAIR)]
                at += PAIR
    half = out_ref.shape[1] // 2
    rows = out_ref[pl.ds(pl.multiple_of(core * PAIR, PAIR), PAIR), :]
    top_ref[:, at:] = rows[:, :half]
    low_ref[:, at:] = rows[:, half:]


def whole(shape):
    return pl.BlockSpec(shape, lambda *_: (0,) * len(shape))


def small_kernel(kernel, name, scalars, arrays, outs, scratch=()):
    return pl.pallas_call(
        kernel,
        grid_spec=pltpu.PrefetchScalarGridSpec(
            num_scalar_prefetch=len(scalars),
            grid=(1,),
            in_specs=[whole(a.shape) for a in arrays],
            out_specs=[whole(shape) for shape, _ in outs],
            scratch_shapes=list(scratch),
        ),
        out_shape=[jax.ShapeDtypeStruct(shape, kind) for shape, kind in outs],
        compiler_params=pltpu.CompilerParams(vmem_limit_bytes=24 * 1024 * 1024),
        name=name,
    )(*scalars, *arrays)


def pick_weights(w_qkv, w_out, core_flag):
    height, columns = w_qkv.shape
    wide = columns // 2 + w_out.shape[1] // 2
    return small_kernel(
        pick_kernel, "pick_weights", [core_flag], [w_qkv, w_out], [((height // 2, wide), BF)] * 2
    )


def turn_kernel(x_ref, turned_ref):
    for i in range(0, x_ref.shape[0], PAIR):
        for j in range(0, x_ref.shape[1], PAIR):
            tile = x_ref[i : i + PAIR, j : j + PAIR].astype(F32)
            turned_ref[j : j + PAIR, i : i + PAIR] = jnp.transpose(tile).astype(BF)


def rim_kernel(even_ref, *refs):
    t_ref, rim1_ref, rim2_ref = refs[:3]
    even = even_ref[0] == 1
    margin = rim1_ref.shape[1]
    size = t_ref.shape[0] // 4

    def added(index, grad):
        rows = grad.shape[0]
        one, two = rim1_ref[index].astype(F32), rim2_ref[index].astype(F32)
        return jnp.concatenate(
            [
                grad[:margin] + jnp.where(even, two, one),
                grad[margin : rows - margin],
                grad[rows - margin :] + jnp.where(even, one, two),
            ],
            axis=0,
        ).astype(BF)

    if len(refs) == 10:
        q_ref, dk_ref, dv_ref, left_ref, right_ref, x_ref, y_ref = refs[3:]
        keys, values = added(0, dk_ref[...]), added(1, dv_ref[...])
        left_ref[:, : 2 * PAIR] = q_ref[...]
        left_ref[:, 2 * PAIR :] = keys[:, :PAIR]
        right_ref[:, :PAIR] = keys[:, PAIR:]
        right_ref[:, PAIR:] = values
    else:
        ka_ref, kb_ref, va_ref, vb_ref, left_ref, right_ref, x_ref, y_ref = refs[3:]
        left_ref[...] = added(0, jnp.concatenate([ka_ref[...], kb_ref[...]], axis=1))
        right_ref[...] = added(1, jnp.concatenate([va_ref[...], vb_ref[...]], axis=1))
    x_ref[...] = dot(t_ref[: 2 * size, :], left_ref[...]).astype(BF)
    y_ref[...] = dot(t_ref[size : 3 * size, :], right_ref[...]).astype(BF)


def leave_kernel(
    scene_ref, t_ref, a0_ref, a1_ref, a2_ref, cot_ref, q1_ref, q2_ref, left_ref, right_ref, fx_ref, fy_ref,
    x_ref, y_ref, kl_ref, kr_ref, e_ref, o_ref, at_ref,
):
    size = t_ref.shape[0] // 4
    quarter = cot_ref.shape[1] // 4
    at_ref[0] = a0_ref[:PAIR, :]
    at_ref[3] = a0_ref[PAIR:, :]
    at_ref[1] = a1_ref[...]
    at_ref[2] = a2_ref[...]
    x_ref[: 2 * size, :PAIR] = dot(t_ref[: 2 * size, :], q1_ref[...]).astype(BF)
    y_ref[: 2 * size, :PAIR] = dot(t_ref[size : 3 * size, :], q2_ref[...]).astype(BF)
    for i, k in enumerate(ORDER):
        grad = dot(at_ref[jnp.bitwise_xor(scene_ref[0], k)], cot_ref[...])
        evens = jnp.concatenate(
            [grad[:, :quarter], grad[:, 2 * quarter : 3 * quarter]], axis=0
        )
        odds = jnp.concatenate(
            [grad[:, quarter : 2 * quarter], grad[:, 3 * quarter :]], axis=0
        )
        if i < 2:
            x_ref[i * size : (i + 1) * size, PAIR:] = evens.astype(BF)
        else:
            e_ref[i - 2] = evens
        if i in (1, 2):
            y_ref[(i - 1) * size : i * size, PAIR:] = odds.astype(BF)
        else:
            o_ref[i // 3] = odds
    left, right = left_ref[...], right_ref[...]
    y_ref[2 * size :, :] = (
        dot(t_ref[2 * size : 3 * size, :], left) + fx_ref[size:, :].astype(F32)
    ).astype(BF)
    x_ref[2 * size :, :] = (dot(t_ref[:size, :], right) + fy_ref[:size, :].astype(F32)).astype(BF)
    kl_ref[...] = dot(t_ref[3 * size :, :], left) + fx_ref[:size, :].astype(F32)
    kr_ref[...] = dot(t_ref[3 * size :, :], right) + fy_ref[size:, :].astype(F32)


def second_kernel(
    t_ref, q1_ref, q2_ref, key_ref, value_ref, ex_ref, ey_ref, lx_ref, ly_ref, e_ref, o_ref,
    x_ref, y_ref, kl_ref, kr_ref,
):
    size = t_ref.shape[0] // 4

    def term(place, query_ref, other_ref, extra, early_ref, late_ref, half):
        block = t_ref[place * size : (place + 1) * size, :]
        here = slice(half * size, (half + 1) * size)
        early, late = early_ref[here, :].astype(F32), late_ref[here, :].astype(F32)
        return jnp.concatenate(
            [
                dot(block, query_ref[...]) + early[:, :PAIR],
                dot(block, other_ref[...]) + late,
                extra + early[:, PAIR:],
            ],
            axis=1,
        )

    y_ref[...] = term(2, q1_ref, key_ref, e_ref[0], ex_ref, lx_ref, 1).astype(BF)
    x_ref[...] = term(0, q2_ref, value_ref, o_ref[0], ey_ref, ly_ref, 0).astype(BF)
    kl_ref[...] = term(3, q1_ref, key_ref, e_ref[1], ex_ref, lx_ref, 0)
    kr_ref[...] = term(3, q2_ref, value_ref, o_ref[1], ey_ref, ly_ref, 1)


def gate(value, *others):
    return lax.optimization_barrier((value,) + others)[0]


def pick_groups(array, axis, unit, core):
    size = array.shape[axis]
    picked = [
        jnp.where(
            core == 0,
            lax.slice_in_dim(array, at, at + unit, axis=axis),
            lax.slice_in_dim(array, at + unit, at + 2 * unit, axis=axis),
        )
        for at in range(0, size, 2 * unit)
    ]
    return jnp.concatenate(picked, axis=axis)


def spread_groups(array, axis, unit, core):
    groups = jnp.split(array, array.shape[axis] // unit, axis=axis)
    parts = []
    for group in groups:
        empty = jnp.zeros_like(group)
        parts += [jnp.where(core == 0, group, empty), jnp.where(core == 0, empty, group)]
    return jnp.concatenate(parts, axis=axis)


def in_order(core, own, other, axis):
    first = jnp.where(core == 0, own, other)
    second = jnp.where(core == 0, other, own)
    return jnp.concatenate([first, second], axis=axis)


def xor_blocks(blocks, index):
    odd = (index & 1) == 1
    high = (index & 2) == 2
    near = [jnp.where(odd, blocks[k ^ 1], blocks[k]) for k in range(4)]
    return [jnp.where(high, near[k ^ 2], near[k]) for k in range(4)]


ORDER = (1, 3, 2, 0)
CHUNKS = ((0, 3), (1, 2))


def square(value, step):
    return lax.ppermute(value, "fsdp", [(i, i ^ step) for i in range(4)])


def chips(value, step, n_vox):
    return lax.ppermute(value, "vox", [(i, i ^ (2 * step)) for i in range(n_vox)])


def on_device(
    tokens, gain, w_qkv, w_out, logit_scale, key_blocks, slot_count, valid_voxels, cotangent
):
    own_tokens = tokens[0]
    own_cotangent = cotangent[0]
    own_rows, model_width = own_tokens.shape
    rows = 2 * own_rows
    own_blocks = key_blocks.shape[1]
    blocks = 2 * own_blocks
    slot_total = key_blocks.shape[2]
    reach = own_blocks // 2
    margin = reach * BLK
    n_vox = lax.axis_size("vox")
    n_fsdp = lax.axis_size("fsdp")
    n_chip = n_vox // 2
    place = lax.axis_index("vox")
    scene = lax.axis_index("fsdp")
    core = place % 2
    chip = place // 2
    fast = n_vox == 8 and n_fsdp == 4
    unit = 128 if fast else 64
    swap = [(i, i ^ 1) for i in range(n_vox)]
    even, low = chip % 2 == 0, chip < 2
    even_flag, core_flag, scene_flag = [
        jnp.reshape(x, (1,)).astype(jnp.int32) for x in (even, core, scene)
    ]
    near_chips = [(i, i ^ 2) for i in range(n_vox)]
    far_chips = []
    for i in range(n_vox):
        to = i // 2 + (1 if i // 2 % 2 else -1)
        far_chips.append((i, 2 * to + i % 2 if 0 <= to < n_chip else i))
    part_width = model_width // 2

    def columns_of(array, pairs):
        return jnp.concatenate(
            [
                array[:, base + p * PAIR : base + (p + 1) * PAIR]
                for base in range(0, array.shape[1], part_width)
                for p in pairs
            ],
            axis=1,
        )

    if fast:
        top, low_half = pick_weights(w_qkv, w_out, core_flag)
        far_top, near_low = square(top, 2), square(low_half, 1)
        near_top, far_low = square(top, 1), square(low_half, 2)
        diag_top, diag_low = square(far_top, 1), square(near_low, 2)
        near, diag = (near_top, near_low), (diag_top, diag_low)
        far, shard = (far_top, far_low), (top, low_half)
        wide = 3 * part_width // 2
        weights_0, weights_1 = [
            jnp.concatenate(
                [block[:, at : at + wide] for both in (near, diag, far, shard) for block in both],
                axis=0,
            )
            for at in (0, wide)
        ]
        wide = 2 * wide
        out_blocks = [
            jnp.concatenate([block[0][:, wide:], block[1][:, wide:]], axis=1)
            for block in (shard, near, far, diag)
        ]
        out_half = jnp.concatenate(xor_blocks(out_blocks, scene), axis=0)
    else:
        core_qkv = pick_groups(w_qkv, 1, unit, core)
        core_out = pick_groups(w_out, 0, unit, core)
        weights_0, weights_1 = [
            lax.all_gather(columns_of(core_qkv, pairs), "fsdp", axis=0, tiled=True)
            for pairs in CHUNKS
        ]
        out_half = lax.all_gather(core_out, "fsdp", axis=0, tiled=True)

    other_tokens = lax.ppermute(own_tokens, "vox", swap)
    other_cotangent = lax.ppermute(own_cotangent, "vox", swap)
    lists = jnp.concatenate([key_blocks[0], slot_count[0][:, None]], axis=1)
    all_lists = in_order(
        core, lists, lax.ppermute(lists.astype(F32), "vox", swap).astype(jnp.int32), 0
    )
    chip_tokens = in_order(core, own_tokens, other_tokens, 0)
    chip_cotangent = in_order(core, own_cotangent, other_cotangent, 0)

    first_block = chip * blocks
    pool_blocks = blocks + 2 * reach
    window_id = (
        all_lists[:, :slot_total] - first_block + reach
        - 2 * (jnp.arange(blocks, dtype=jnp.int32) // 2)[:, None]
    )
    used = jnp.arange(slot_total, dtype=jnp.int32)[None, :] < all_lists[:, slot_total:]
    hits = jnp.logical_and(
        window_id[:, :, None] == jnp.arange(WINDOW, dtype=jnp.int32), used[:, :, None]
    )
    mult = jnp.sum(hits.astype(jnp.int32), axis=1)
    scene_total = valid_voxels.shape[1]
    pool_ids = first_block - reach + jnp.arange(pool_blocks, dtype=jnp.int32)
    valid = jnp.take(valid_voxels[0], jnp.clip(pool_ids, 0, scene_total - 1))
    group_heads = unit // HD
    scales = pick_groups(logit_scale, 0, group_heads, core)

    wide = chip_tokens.astype(F32)
    inverse = lax.rsqrt(jnp.mean(wide * wide, axis=1, keepdims=True) + EPS)
    normed = (wide * inverse * gain).astype(BF)
    if fast:
        turned = xor_blocks(jnp.split(normed, 4, axis=1), scene)
        normed = jnp.concatenate([turned[k] for k in ORDER], axis=1)
        normed_t = small_kernel(turn_kernel, "turn", [], [normed], [(normed.shape[::-1], BF)])[0]

    def pairings(first, second):
        return lax.ppermute(first, "vox", near_chips), lax.ppermute(second, "vox", far_chips)

    def heads_of(packed, upstream, chunk, begin=0, count=2, carried=()):
        pairs = CHUNKS[chunk]
        used = pairs[begin : begin + count]
        chunk_scales = jnp.concatenate([scales[2 * p : 2 * p + 2] for p in used])
        return attention(
            packed, *halos, upstream, mult, valid, chunk_scales, even_flag, pairs, begin, count,
            4 * chunk, carried,
        )

    def with_rims(grad, first, second):
        first, second = first.astype(F32), second.astype(F32)
        return jnp.concatenate(
            [
                grad[:margin] + jnp.where(even, second, first),
                grad[margin : rows - margin],
                grad[rows - margin :] + jnp.where(even, first, second),
            ],
            axis=0,
        ).astype(BF)

    def key_value_grads(keys, values, rims):
        return [with_rims(g, rims[0][i], rims[1][i]) for i, g in enumerate((keys, values))]

    def out_rows(pairs):
        return jnp.concatenate([out_half[p * PAIR : (p + 1) * PAIR] for p in pairs], axis=0)

    def groups_of(left, right, chunk):
        half = 3 * PAIR
        groups = [left[:, k * PAIR : (k + 1) * PAIR] for k in range(3)]
        groups += [right[:, k * PAIR : (k + 1) * PAIR] for k in range(3)]
        sets = ((0, 3, 4), (1, 2, 5)) if chunk == 0 else ((0, 3, 2), (1, 4, 5))
        evens = jnp.concatenate([groups[k] for k in sets[0]] + [left[:, half:]], axis=1)
        odds = jnp.concatenate([groups[k] for k in sets[1]] + [right[:, half:]], axis=1)
        return jnp.where(even, evens, odds), jnp.where(even, odds, evens).astype(BF)

    def halves_of(kept):
        left, right = kept[:, : 2 * PAIR], kept[:, PAIR : 3 * PAIR]
        if kept.shape[1] > 3 * PAIR:
            more = kept[:, 3 * PAIR :]
            cut = more.shape[0] // 2
            left = jnp.concatenate([left, more[:cut]], axis=0)
            right = jnp.concatenate([right, more[cut:]], axis=0)
        return jnp.where(low, left, right), jnp.where(low, right, left).astype(BF)

    packed_0, packed_1 = [dot(normed, weight).astype(BF) for weight in (weights_0, weights_1)]
    query_width = part_width // 2
    top, bottom = [
        jnp.concatenate([packed[at, query_width:] for packed in (packed_0, packed_1)], axis=1)
        for at in (slice(0, margin), slice(rows - margin, rows))
    ]
    halos = pairings(jnp.where(even, bottom, top), jnp.where(even, top, bottom))
    upstream = dot(chip_cotangent, out_half, ((1,), (1,))).astype(BF)
    first = heads_of(packed_0, upstream, 0)
    rims_0 = pairings(first[4], first[5])
    third = heads_of(packed_1, gate(upstream, first[4], first[5]), 1, 0, 1)
    rims_0 = [gate(rim, third[6]) for rim in rims_0]
    half = 3 * query_width // 2
    if fast:
        left_0, right_0, to_x, to_y = small_kernel(
            rim_kernel, "rims_first", [even_flag],
            [normed_t, *rims_0, first[1], first[2], first[3]],
            [((rows, half), BF)] * 2 + [((model_width // 2, half), BF)] * 2,
        )
        from_x0, from_y0 = square(to_x, 1), square(to_y, 2)
        fourth_in = gate(upstream, to_x, to_y)
    else:
        key_0, value_0 = key_value_grads(first[2], first[3], rims_0)
        grad_0 = jnp.concatenate([first[1], key_0, value_0], axis=1)
        fourth_in = upstream
    fourth = heads_of(packed_1, fourth_in, 1, 1, 1, (third[0], third[4], third[5]))
    rims_1 = pairings(fourth[4], fourth[5])

    att_0 = gate(first[0], fourth[6])
    att_1 = fourth[0]
    if fast:
        quarter = model_width // 4
        to_x, to_y, left, right, evens, odds = small_kernel(
            leave_kernel, "leave_early", [scene_flag],
            [normed_t, first[7], third[7], fourth[7], chip_cotangent, third[1], fourth[1],
             left_0, right_0, from_x0, from_y0],
            [((3 * quarter, half), BF)] * 2
            + [((quarter, half), F32)] * 2
            + [((2, quarter, quarter), F32)] * 2,
            [pltpu.VMEM((4, PAIR, rows), BF)],
        )
        early_x, early_y = square(to_x, 1), square(to_y, 2)
        rims_1 = lax.optimization_barrier((*rims_1, to_x, to_y))[:2]

    if fast:
        key_1, value_1, to_x, to_y = small_kernel(
            rim_kernel, "rims_second", [even_flag],
            [normed_t, *rims_1, third[2], fourth[2], third[3], fourth[3]],
            [((rows, query_width), BF)] * 2 + [((model_width // 2, query_width), BF)] * 2,
        )
        late_x, late_y = square(to_x, 1), square(to_y, 2)
        early_x, early_y, att_0, att_1 = lax.optimization_barrier(
            (early_x, early_y, att_0, att_1, to_x, to_y)
        )[:4]
        height = model_width // 4
        kept_0, sent = groups_of(
            left + early_y[2 * height :].astype(F32), right + early_x[2 * height :].astype(F32), 0
        )
        got_0 = chips(sent, 1, n_vox)
        to_x, to_y, left, right = small_kernel(
            second_kernel, "second_exchange", [],
            [normed_t, third[1], fourth[1], key_1, value_1, early_x, early_y, late_x, late_y, evens, odds],
            [((height, half + quarter), BF)] * 2 + [((height, half + quarter), F32)] * 2,
        )
        end_x, end_y = square(to_x, 1), square(to_y, 2)
        left_0, key_1, scale_first, got_0 = lax.optimization_barrier(
            (left_0, key_1, first[6], got_0, to_x, to_y)
        )[:4]
        grad_0 = jnp.concatenate([left_0, right_0], axis=1)
    else:
        key_1, value_1 = key_value_grads(
            *[jnp.concatenate([third[i], fourth[i]], axis=1) for i in (2, 3)], rims_1
        )
        scale_first = first[6]
    mixed_part = dot(att_0, out_rows(CHUNKS[0])) + dot(att_1, out_rows(CHUNKS[1]))
    grad_1 = jnp.concatenate([third[1], fourth[1], key_1, value_1], axis=1)

    ngrad_part = dot(grad_0, weights_0, ((1,), (1,))) + dot(grad_1, weights_1, ((1,), (1,)))
    mixed_mine = lax.dynamic_slice_in_dim(mixed_part, core * own_rows, own_rows, 0)
    mixed_theirs = lax.dynamic_slice_in_dim(mixed_part, (1 - core) * own_rows, own_rows, 0)
    mixed = (
        own_tokens.astype(F32) + (mixed_mine + lax.ppermute(mixed_theirs, "vox", swap))
    ).astype(BF)

    ngrad_mine = lax.dynamic_slice_in_dim(ngrad_part, core * own_rows, own_rows, 0)
    ngrad_theirs = lax.dynamic_slice_in_dim(ngrad_part, (1 - core) * own_rows, own_rows, 0)
    normed_grad = ngrad_mine + lax.ppermute(ngrad_theirs, "vox", swap)
    if fast:
        held = jnp.split(normed_grad, 4, axis=1)
        normed_grad = jnp.concatenate(
            xor_blocks([held[ORDER.index(k)] for k in range(4)], scene), axis=1
        )

    own_wide = own_tokens.astype(F32)
    own_inverse = lax.rsqrt(jnp.mean(own_wide * own_wide, axis=1, keepdims=True) + EPS)
    gain_grad = jnp.sum(normed_grad * own_wide * own_inverse, axis=0)
    scaled_grad = normed_grad * gain
    token_grad = (
        own_cotangent.astype(F32)
        + own_inverse
        * (
            scaled_grad
            - own_wide
            * own_inverse
            * own_inverse
            * jnp.mean(scaled_grad * own_wide, axis=1, keepdims=True)
        )
    ).astype(BF)

    scale_parts = {}
    for pairs, sums in zip(
        CHUNKS, (scale_first, jnp.concatenate([third[6], fourth[6]], axis=0))
    ):
        sums = jnp.sum(sums.reshape(2, 8, 2, PAIR), axis=(1, 3))
        for i, p in enumerate(pairs):
            scale_parts[p] = sums[i]
    scale_part = jnp.concatenate([scale_parts[p] for p in range(len(scale_parts))])
    scale_grad = spread_groups(scale_part, 0, group_heads, core)

    if fast:
        small = jnp.concatenate([gain_grad, scale_grad, jnp.zeros((112,), F32)]).reshape(9, 128)
        small = small + square(small, 1)
        small = small + square(small, 2)
        kept_0, sent = halves_of(kept_0 + got_0.astype(F32))
        got_0 = chips(sent, 2, n_vox)
        kept_1, sent = groups_of(left + end_y.astype(F32), right + end_x.astype(F32), 1)
        got_1 = chips(sent, 1, n_vox)
        small = small + lax.ppermute(small, "vox", swap)
        small = small + chips(small, 1, n_vox)
        kept_1, sent = halves_of(kept_1 + got_1.astype(F32))
        got_1 = chips(sent, 2, n_vox)
        small = small + chips(small, 2, n_vox)
        small = small.reshape(-1)
        summed_gain, summed_scale = small[:model_width], small[model_width : model_width + HEADS]
        kept_1 = kept_1 + got_1.astype(F32)
        qkv_sums = [kept_0 + got_0.astype(F32), kept_1[:height]]
        out_sum = kept_1[height:]
    else:
        out_sums = [dot(att, chip_cotangent, ((0,), (0,))) for att in (att_0, att_1)]
        qkv_sums = [dot(normed, grad, ((0,), (0,))) for grad in (grad_0, grad_1)]
        summed_gain, summed_scale = lax.psum((gain_grad, scale_grad), ("vox", "fsdp"))

    if fast:
        half = out_sum.shape[1] // 2
        first, second = out_sum[:, :half], out_sum[:, half:]
        out_other = lax.ppermute(jnp.where(core == 0, second, first), "vox", swap)
        summed_out = in_order(core, jnp.where(core == 0, first, second), out_other, 0)

        a0, a1 = qkv_sums[0][:, :PAIR], qkv_sums[0][:, PAIR:]
        b0, b1 = qkv_sums[1][:, :PAIR], qkv_sums[1][:, PAIR:]

        def by_chip(options):
            value = options[3]
            for k in range(3):
                value = jnp.where(chip == k, options[k], value)
            return value

        g0 = by_chip((a0, a0, b1, b0))
        g1 = by_chip((b0, a1, a0, b1))
        g2 = by_chip((b1, b0, a1, a1))
        got = lax.ppermute(jnp.where(core == 0, g2, g0), "vox", swap)
        summed_qkv = jnp.concatenate(
            [
                jnp.where(core == 0, g0, g1),
                got,
                jnp.where(core == 0, g1, g2),
            ],
            axis=1,
        )
    else:
        by_pair = {}
        cols = {}
        for pairs, out_total, qkv_total in zip(CHUNKS, out_sums, qkv_sums):
            for i, p in enumerate(pairs):
                by_pair[p] = out_total[i * PAIR : (i + 1) * PAIR]
                for j in range(3):
                    at = (2 * j + i) * PAIR
                    cols[4 * j + p] = qkv_total[:, at : at + PAIR]
        out_total = jnp.concatenate([by_pair[p] for p in range(4)], axis=0)
        qkv_total = jnp.concatenate([cols[k] for k in range(12)], axis=1)
        out_total = spread_groups(out_total, 0, unit, core)
        qkv_total = lax.psum_scatter(qkv_total, "fsdp", scatter_dimension=0, tiled=True)
        qkv_total = spread_groups(qkv_total, 1, unit, core)
        summed_qkv = lax.psum_scatter(qkv_total, "vox", scatter_dimension=1, tiled=True)
        out_total = lax.psum_scatter(out_total, "fsdp", scatter_dimension=0, tiled=True)
        summed_out = lax.psum_scatter(out_total, "vox", scatter_dimension=1, tiled=True)

    return (
        mixed[None],
        token_grad[None],
        summed_qkv,
        summed_out,
        summed_gain,
        summed_scale,
    )


def solution(mesh):
    return jax.shard_map(
        on_device,
        mesh=mesh,
        in_specs=(
            P("fsdp", "vox", None),
            P(),
            P("fsdp", None),
            P("fsdp", None),
            P(),
            P("fsdp", "vox", None),
            P("fsdp", "vox"),
            P("fsdp", None),
            P("fsdp", "vox", None),
        ),
        out_specs=(
            P("fsdp", "vox", None),
            P("fsdp", "vox", None),
            P("fsdp", "vox"),
            P("fsdp", "vox"),
            P(),
            P(),
        ),
        check_vma=False,
    )
```

```python
import functools

import jax
import jax.numpy as jnp
from jax import lax
from jax.experimental import pallas as pl
from jax.experimental.pallas import tpu as pltpu
from jax.sharding import PartitionSpec as P

HEADS = 16
HD = 64
PAIR = 2 * HD
BLK = 64
WINDOW = 8
EPS = 1e-06
LOG2E = 1.4426950408889634
BF = jnp.bfloat16
F32 = jnp.float32


def dot(a, b, dims=((1,), (0,))):
    return lax.dot_general(a, b, (dims, ((), ())), preferred_element_type=F32)


def head_sums(x, same_head):
    high = x.astype(BF)
    low = (x - high.astype(F32)).astype(BF)
    return dot(high, same_head) + dot(low, same_head)


def unit_rows(x, same_head):
    length = jnp.sqrt(head_sums(x * x, same_head) + EPS)
    return x / length, length


def unit_back(unit, length, grad, same_head):
    return (grad - unit * head_sums(unit * grad, same_head)) / length


def attention_kernel(
    mult_ref, valid_ref, scale_ref, even_ref,
    q_ref, k_ref, v_ref, k1_ref, v1_ref, k2_ref, v2_ref, u_ref,
    *refs,
):
    carried, refs = (refs[:3], refs[3:]) if len(refs) > 22 else ((), refs)
    att_ref, dq_ref, dk_ref, dv_ref, rim1_ref, rim2_ref, ds_ref, turn_ref = refs[:8]
    k_unit, k_len, k_low, k_turn, v_low, v_turn, bias = refs[8:15]
    scores, grads, raised, w_lows, c_lows, dk, dv = refs[15:]
    held = slice(PAIR, 2 * PAIR) if carried else slice(0, PAIR)
    if carried:
        att_ref[:, :PAIR] = carried[0][...]
        rim1_ref[:, :, :PAIR] = carried[1][...]
        rim2_ref[:, :, :PAIR] = carried[2][...]
    rows = q_ref.shape[0]
    margin = k1_ref.shape[0]
    even = even_ref[0] == 1
    pool = rows + 2 * margin
    reach = margin // BLK
    steps = rows // PAIR
    span = WINDOW * BLK
    pair = pl.program_id(0)

    lane = lax.broadcasted_iota(jnp.int32, (BLK, PAIR), 1)
    row = lax.broadcasted_iota(jnp.int32, (BLK, PAIR), 0)
    head_a = lax.broadcasted_iota(jnp.int32, (PAIR, PAIR), 0) < HD
    head_b = lax.broadcasted_iota(jnp.int32, (PAIR, PAIR), 1) < HD
    same_head = jnp.where(head_a == head_b, 1.0, 0.0).astype(BF)
    first_lanes = head_b

    @pl.when(pair == 0)
    def _():
        for t in range(steps):
            for w in range(WINDOW):
                count = jnp.where(lane < BLK, mult_ref[2 * t, w], mult_ref[2 * t + 1, w])
                live = row < valid_ref[2 * t + w]
                seen = jnp.where(live, count, 0).astype(F32)
                bias[t, w * BLK : (w + 1) * BLK, :] = jnp.where(
                    seen > 0.0, jnp.log2(jnp.maximum(seen, 1.0)), -1e30
                )

    def split_heads(x):
        return jnp.concatenate(
            [jnp.where(first_lanes, x, 0.0), jnp.where(first_lanes, 0.0, x)], axis=0
        ).astype(BF)

    def take(at, keys, values):
        unit, length = unit_rows(keys.astype(F32), same_head)
        place = slice(at, at + keys.shape[0])
        k_unit[place, :] = unit
        k_len[place, :] = length
        k_low[place, :] = unit.astype(BF)
        v_low[place, :] = values

    for part in range(0, margin, BLK):
        here = slice(part, part + BLK)
        k1, k2 = k1_ref[here, :].astype(F32), k2_ref[here, :].astype(F32)
        v1, v2 = v1_ref[here, :].astype(F32), v2_ref[here, :].astype(F32)
        take(part, jnp.where(even, k2, k1), jnp.where(even, v2, v1).astype(BF))
        take(margin + rows + part, jnp.where(even, k1, k2), jnp.where(even, v1, v2).astype(BF))
    for part in range(0, rows, PAIR):
        here = slice(part, part + PAIR)
        take(margin + part, k_ref[here, :], v_ref[here, :])
    for part in range(0, pool, 128):
        place = slice(part, part + 128)
        k_turn[:, place] = jnp.transpose(k_low[place, :].astype(F32)).astype(BF)
        v_turn[:, place] = jnp.transpose(v_low[place, :].astype(F32)).astype(BF)

    dk[...] = jnp.zeros_like(dk)
    dv[...] = jnp.zeros_like(dv)
    wide_lane = lax.broadcasted_iota(jnp.int32, (1, 2 * PAIR), 1)
    scale = jnp.where(wide_lane < PAIR, scale_ref[2 * pair], scale_ref[2 * pair + 1])
    ds = jnp.zeros((8, 2 * PAIR), F32)

    def window_of(t):
        return slice(t * PAIR, t * PAIR + span)

    def begin(t):
        own, window = slice(t * PAIR, (t + 1) * PAIR), window_of(t)
        q_unit, q_len = unit_rows(q_ref[own, :].astype(F32), same_head)
        q_split = split_heads(q_unit)
        live = jnp.concatenate(
            [row < valid_ref[2 * t + reach], row < valid_ref[2 * t + 1 + reach]], axis=0
        )
        u_split = split_heads(jnp.where(live, u_ref[own, :].astype(F32), 0.0))
        scores[t % 2] = dot(k_low[window, :], q_split, ((1,), (1,)))
        grads[t % 2] = dot(v_low[window, :], u_split, ((1,), (1,)))
        return q_unit, q_len, q_split, live, u_split

    stretch = scale * LOG2E
    parts = [slice(i, i + 32) for i in range(0, span, 32)]

    def fold(x):
        return x.reshape(4, 8, 2 * PAIR)

    following = begin(0)
    for t in range(steps):
        own, window = slice(t * PAIR, (t + 1) * PAIR), window_of(t)
        q_unit, q_len, q_split, live, u_split = following
        s_ref, g_ref, e_ref = scores.at[t % 2], grads.at[t % 2], raised.at[t % 2]
        w_low, c_low = w_lows.at[t % 2], c_lows.at[t % 2]
        if t + 1 < steps:
            following = begin(t + 1)

        peak = jnp.full((8, 2 * PAIR), -1e30, F32)
        for part in parts:
            half = bias[t, part, :]
            x = s_ref[part, :] * stretch + jnp.concatenate([half, half], axis=1)
            e_ref[part, :] = x
            peak = jnp.maximum(peak, jnp.max(fold(x), axis=0))
        peak = jnp.max(peak, axis=0, keepdims=True)
        total = jnp.zeros((8, 2 * PAIR), F32)
        centre = jnp.zeros((8, 2 * PAIR), F32)
        for part in parts:
            e = jnp.exp2(e_ref[part, :] - peak)
            e_ref[part, :] = e
            total = total + jnp.sum(fold(e), axis=0)
            centre = centre + jnp.sum(fold(e * g_ref[part, :]), axis=0)
        share = 1.0 / jnp.sum(total, axis=0, keepdims=True)
        centre = jnp.sum(centre, axis=0, keepdims=True) * share
        for part in parts:
            w = e_ref[part, :] * share
            w_low[part, :] = w.astype(BF)
            sg = w * (g_ref[part, :] - centre)
            ds = ds + jnp.sum(fold(sg * s_ref[part, :]), axis=0)
            c_low[part, :] = (sg * scale).astype(BF)

        def own_heads(turned):
            return jnp.concatenate([turned[:HD, :PAIR], turned[HD:, PAIR:]], axis=0)

        mixed = own_heads(dot(v_turn[:, window], w_low[...]))
        att_ref[own, held] = jnp.where(live, jnp.transpose(mixed), 0.0).astype(BF)
        row_lane = lax.broadcasted_iota(jnp.int32, (PAIR, PAIR), 1)
        limit = jnp.where(
            row_lane < BLK, valid_ref[2 * t + reach], valid_ref[2 * t + 1 + reach] + BLK
        )
        turn_ref[:, own] = jnp.where(row_lane < limit, mixed, 0.0).astype(BF)
        q_grad = jnp.transpose(own_heads(dot(k_turn[:, window], c_low[...])))
        dq_ref[own, :] = unit_back(q_unit, q_len, q_grad, same_head).astype(BF)
        dv[window, :] += dot(w_low[...], u_split)
        dk[window, :] += dot(c_low[...], q_split)

    def key_grad(part):
        place = slice(part, part + BLK)
        return unit_back(k_unit[place, :], k_len[place, :], dk[place, :], same_head)

    for part in range(0, rows, BLK):
        here = slice(part, part + BLK)
        dk_ref[here, :] = key_grad(margin + part)
        dv_ref[here, :] = dv[margin + part : margin + part + BLK, :]
    for part in range(0, margin, BLK):
        here = slice(part, part + BLK)
        far = margin + rows + part
        kb, ka = key_grad(part), key_grad(far)
        vb, va = dv[part : part + BLK, :], dv[far : far + BLK, :]
        rim1_ref[0, here, held] = jnp.where(even, ka, kb).astype(BF)
        rim1_ref[1, here, held] = jnp.where(even, va, vb).astype(BF)
        rim2_ref[0, here, held] = jnp.where(even, kb, ka).astype(BF)
        rim2_ref[1, here, held] = jnp.where(even, vb, va).astype(BF)
    ds_ref[0, :, :] = ds


def attention(packed, first, second, upstream, mult, valid, scales, even, pairs, begin=0, count=2, base=0, carried=()):
    rows = packed.shape[0]
    width = count * PAIR
    both = width + (PAIR if carried else 0)
    margin = first.shape[0]
    pool = rows + 2 * margin
    held = len(pairs)
    stride = pairs[1] - pairs[0]
    steps = rows // PAIR
    span = WINDOW * BLK

    def at(offset):
        return lambda p, *_: (0, offset + p)

    return pl.pallas_call(
        attention_kernel,
        grid_spec=pltpu.PrefetchScalarGridSpec(
            num_scalar_prefetch=4,
            grid=(count,),
            in_specs=[
                pl.BlockSpec((rows, PAIR), at(begin)),
                pl.BlockSpec((rows, PAIR), at(held + begin)),
                pl.BlockSpec((rows, PAIR), at(2 * held + begin)),
                pl.BlockSpec((margin, PAIR), at(base + begin)),
                pl.BlockSpec((margin, PAIR), at(base + held + begin)),
                pl.BlockSpec((margin, PAIR), at(base + begin)),
                pl.BlockSpec((margin, PAIR), at(base + held + begin)),
                pl.BlockSpec((rows, PAIR), lambda p, *_: (0, pairs[begin] + stride * p)),
            ]
            + [whole(array.shape) for array in carried],
            out_specs=[
                pl.BlockSpec((rows, both // count), at(0)),
                pl.BlockSpec((rows, PAIR), at(0)),
                pl.BlockSpec((rows, PAIR), at(0)),
                pl.BlockSpec((rows, PAIR), at(0)),
                pl.BlockSpec((2, margin, both // count), lambda p, *_: (0, 0, p)),
                pl.BlockSpec((2, margin, both // count), lambda p, *_: (0, 0, p)),
                pl.BlockSpec((1, 8, 2 * PAIR), lambda p, *_: (p, 0, 0)),
                pl.BlockSpec((PAIR, rows), lambda p, *_: (p, 0)),
            ],
            scratch_shapes=[
                pltpu.VMEM((pool, PAIR), F32),
                pltpu.VMEM((pool, PAIR), F32),
                pltpu.VMEM((pool, PAIR), BF),
                pltpu.VMEM((PAIR, pool), BF),
                pltpu.VMEM((pool, PAIR), BF),
                pltpu.VMEM((PAIR, pool), BF),
                pltpu.VMEM((steps, span, PAIR), F32),
                pltpu.VMEM((2, span, 2 * PAIR), F32),
                pltpu.VMEM((2, span, 2 * PAIR), F32),
                pltpu.VMEM((2, span, 2 * PAIR), F32),
                pltpu.VMEM((2, span, 2 * PAIR), BF),
                pltpu.VMEM((2, span, 2 * PAIR), BF),
                pltpu.VMEM((pool, PAIR), F32),
                pltpu.VMEM((pool, PAIR), F32),
            ],
        ),
        out_shape=[
            jax.ShapeDtypeStruct((rows, both), BF),
            jax.ShapeDtypeStruct((rows, width), BF),
            jax.ShapeDtypeStruct((rows, width), F32),
            jax.ShapeDtypeStruct((rows, width), F32),
            jax.ShapeDtypeStruct((2, margin, both), BF),
            jax.ShapeDtypeStruct((2, margin, both), BF),
            jax.ShapeDtypeStruct((count, 8, 2 * PAIR), F32),
            jax.ShapeDtypeStruct((width, rows), BF),
        ],
        compiler_params=pltpu.CompilerParams(vmem_limit_bytes=24 * 1024 * 1024),
        cost_estimate=pl.CostEstimate(
            flops=8 * 2 * 6 * count * steps * span * 256 * 128,
            bytes_accessed=rows * width * 20,
            transcendentals=count * steps * span * 256,
        ),
        name="block_attention",
    )(
        mult, valid, scales, even,
        packed, packed, packed, first, first, second, second, upstream, *carried,
    )


def pick_kernel(core_ref, qkv_ref, out_ref, top_ref, low_ref):
    core = core_ref[0]
    at = 0
    for pairs in CHUNKS:
        for base in range(0, qkv_ref.shape[1], 8 * PAIR):
            for p in pairs:
                start = pl.multiple_of(base + 2 * p * PAIR + core * PAIR, PAIR)
                top_ref[:, at : at + PAIR] = qkv_ref[:PAIR, pl.ds(start, PAIR)]
                low_ref[:, at : at + PAIR] = qkv_ref[PAIR:, pl.ds(start, PAIR)]
                at += PAIR
    half = out_ref.shape[1] // 2
    rows = out_ref[pl.ds(pl.multiple_of(core * PAIR, PAIR), PAIR), :]
    top_ref[:, at:] = rows[:, :half]
    low_ref[:, at:] = rows[:, half:]


def whole(shape):
    return pl.BlockSpec(shape, lambda *_: (0,) * len(shape))


def small_kernel(kernel, name, scalars, arrays, outs, scratch=()):
    return pl.pallas_call(
        kernel,
        grid_spec=pltpu.PrefetchScalarGridSpec(
            num_scalar_prefetch=len(scalars),
            grid=(1,),
            in_specs=[whole(a.shape) for a in arrays],
            out_specs=[whole(shape) for shape, _ in outs],
            scratch_shapes=list(scratch),
        ),
        out_shape=[jax.ShapeDtypeStruct(shape, kind) for shape, kind in outs],
        compiler_params=pltpu.CompilerParams(vmem_limit_bytes=24 * 1024 * 1024),
        name=name,
    )(*scalars, *arrays)


def pick_weights(w_qkv, w_out, core_flag):
    height, columns = w_qkv.shape
    wide = columns // 2 + w_out.shape[1] // 2
    return small_kernel(
        pick_kernel, "pick_weights", [core_flag], [w_qkv, w_out], [((height // 2, wide), BF)] * 2
    )


def turn_kernel(x_ref, turned_ref):
    for i in range(0, x_ref.shape[0], PAIR):
        for j in range(0, x_ref.shape[1], PAIR):
            tile = x_ref[i : i + PAIR, j : j + PAIR].astype(F32)
            turned_ref[j : j + PAIR, i : i + PAIR] = jnp.transpose(tile).astype(BF)


def rim_kernel(even_ref, *refs):
    t_ref, rim1_ref, rim2_ref = refs[:3]
    even = even_ref[0] == 1
    margin = rim1_ref.shape[1]
    size = t_ref.shape[0] // 4

    def added(index, grad):
        rows = grad.shape[0]
        one, two = rim1_ref[index].astype(F32), rim2_ref[index].astype(F32)
        return jnp.concatenate(
            [
                grad[:margin] + jnp.where(even, two, one),
                grad[margin : rows - margin],
                grad[rows - margin :] + jnp.where(even, one, two),
            ],
            axis=0,
        ).astype(BF)

    if len(refs) == 10:
        q_ref, dk_ref, dv_ref, left_ref, right_ref, x_ref, y_ref = refs[3:]
        keys, values = added(0, dk_ref[...]), added(1, dv_ref[...])
        left_ref[:, : 2 * PAIR] = q_ref[...]
        left_ref[:, 2 * PAIR :] = keys[:, :PAIR]
        right_ref[:, :PAIR] = keys[:, PAIR:]
        right_ref[:, PAIR:] = values
    else:
        ka_ref, kb_ref, va_ref, vb_ref, left_ref, right_ref, x_ref, y_ref = refs[3:]
        left_ref[...] = added(0, jnp.concatenate([ka_ref[...], kb_ref[...]], axis=1))
        right_ref[...] = added(1, jnp.concatenate([va_ref[...], vb_ref[...]], axis=1))
    x_ref[...] = dot(t_ref[: 2 * size, :], left_ref[...]).astype(BF)
    y_ref[...] = dot(t_ref[size : 3 * size, :], right_ref[...]).astype(BF)


def leave_kernel(
    scene_ref, t_ref, a0_ref, a1_ref, a2_ref, cot_ref, q1_ref, q2_ref, left_ref, right_ref, fx_ref, fy_ref,
    x_ref, y_ref, kl_ref, kr_ref, e_ref, o_ref, at_ref,
):
    size = t_ref.shape[0] // 4
    quarter = cot_ref.shape[1] // 4
    at_ref[0] = a0_ref[:PAIR, :]
    at_ref[3] = a0_ref[PAIR:, :]
    at_ref[1] = a1_ref[...]
    at_ref[2] = a2_ref[...]
    x_ref[: 2 * size, :PAIR] = dot(t_ref[: 2 * size, :], q1_ref[...]).astype(BF)
    y_ref[: 2 * size, :PAIR] = dot(t_ref[size : 3 * size, :], q2_ref[...]).astype(BF)
    for i, k in enumerate(ORDER):
        grad = dot(at_ref[jnp.bitwise_xor(scene_ref[0], k)], cot_ref[...])
        evens = jnp.concatenate(
            [grad[:, :quarter], grad[:, 2 * quarter : 3 * quarter]], axis=0
        )
        odds = jnp.concatenate(
            [grad[:, quarter : 2 * quarter], grad[:, 3 * quarter :]], axis=0
        )
        if i < 2:
            x_ref[i * size : (i + 1) * size, PAIR:] = evens.astype(BF)
        else:
            e_ref[i - 2] = evens
        if i in (1, 2):
            y_ref[(i - 1) * size : i * size, PAIR:] = odds.astype(BF)
        else:
            o_ref[i // 3] = odds
    left, right = left_ref[...], right_ref[...]
    y_ref[2 * size :, :] = (
        dot(t_ref[2 * size : 3 * size, :], left) + fx_ref[size:, :].astype(F32)
    ).astype(BF)
    x_ref[2 * size :, :] = (dot(t_ref[:size, :], right) + fy_ref[:size, :].astype(F32)).astype(BF)
    kl_ref[...] = dot(t_ref[3 * size :, :], left) + fx_ref[:size, :].astype(F32)
    kr_ref[...] = dot(t_ref[3 * size :, :], right) + fy_ref[size:, :].astype(F32)


def second_kernel(
    t_ref, q1_ref, q2_ref, key_ref, value_ref, ex_ref, ey_ref, lx_ref, ly_ref, e_ref, o_ref,
    x_ref, y_ref, kl_ref, kr_ref,
):
    size = t_ref.shape[0] // 4

    def term(place, query_ref, other_ref, extra, early_ref, late_ref, half):
        block = t_ref[place * size : (place + 1) * size, :]
        here = slice(half * size, (half + 1) * size)
        early, late = early_ref[here, :].astype(F32), late_ref[here, :].astype(F32)
        return jnp.concatenate(
            [
                dot(block, query_ref[...]) + early[:, :PAIR],
                dot(block, other_ref[...]) + late,
                extra + early[:, PAIR:],
            ],
            axis=1,
        )

    y_ref[...] = term(2, q1_ref, key_ref, e_ref[0], ex_ref, lx_ref, 1).astype(BF)
    x_ref[...] = term(0, q2_ref, value_ref, o_ref[0], ey_ref, ly_ref, 0).astype(BF)
    kl_ref[...] = term(3, q1_ref, key_ref, e_ref[1], ex_ref, lx_ref, 0)
    kr_ref[...] = term(3, q2_ref, value_ref, o_ref[1], ey_ref, ly_ref, 1)


def gate(value, *others):
    return lax.optimization_barrier((value,) + others)[0]


def pick_groups(array, axis, unit, core):
    size = array.shape[axis]
    picked = [
        jnp.where(
            core == 0,
            lax.slice_in_dim(array, at, at + unit, axis=axis),
            lax.slice_in_dim(array, at + unit, at + 2 * unit, axis=axis),
        )
        for at in range(0, size, 2 * unit)
    ]
    return jnp.concatenate(picked, axis=axis)


def spread_groups(array, axis, unit, core):
    groups = jnp.split(array, array.shape[axis] // unit, axis=axis)
    parts = []
    for group in groups:
        empty = jnp.zeros_like(group)
        parts += [jnp.where(core == 0, group, empty), jnp.where(core == 0, empty, group)]
    return jnp.concatenate(parts, axis=axis)


def in_order(core, own, other, axis):
    first = jnp.where(core == 0, own, other)
    second = jnp.where(core == 0, other, own)
    return jnp.concatenate([first, second], axis=axis)


def xor_blocks(blocks, index):
    odd = (index & 1) == 1
    high = (index & 2) == 2
    near = [jnp.where(odd, blocks[k ^ 1], blocks[k]) for k in range(4)]
    return [jnp.where(high, near[k ^ 2], near[k]) for k in range(4)]


ORDER = (1, 3, 2, 0)
CHUNKS = ((0, 3), (1, 2))


def square(value, step):
    return lax.ppermute(value, "fsdp", [(i, i ^ step) for i in range(4)])


def chips(value, step, n_vox):
    return lax.ppermute(value, "vox", [(i, i ^ (2 * step)) for i in range(n_vox)])


def on_device(
    tokens, gain, w_qkv, w_out, logit_scale, key_blocks, slot_count, valid_voxels, cotangent
):
    own_tokens = tokens[0]
    own_cotangent = cotangent[0]
    own_rows, model_width = own_tokens.shape
    rows = 2 * own_rows
    own_blocks = key_blocks.shape[1]
    blocks = 2 * own_blocks
    slot_total = key_blocks.shape[2]
    reach = own_blocks // 2
    margin = reach * BLK
    n_vox = lax.axis_size("vox")
    n_fsdp = lax.axis_size("fsdp")
    n_chip = n_vox // 2
    place = lax.axis_index("vox")
    scene = lax.axis_index("fsdp")
    core = place % 2
    chip = place // 2
    fast = n_vox == 8 and n_fsdp == 4
    unit = 128 if fast else 64
    swap = [(i, i ^ 1) for i in range(n_vox)]
    even, low = chip % 2 == 0, chip < 2
    even_flag, core_flag, scene_flag = [
        jnp.reshape(x, (1,)).astype(jnp.int32) for x in (even, core, scene)
    ]
    near_chips = [(i, i ^ 2) for i in range(n_vox)]
    far_chips = []
    for i in range(n_vox):
        to = i // 2 + (1 if i // 2 % 2 else -1)
        far_chips.append((i, 2 * to + i % 2 if 0 <= to < n_chip else i))
    part_width = model_width // 2

    def columns_of(array, pairs):
        return jnp.concatenate(
            [
                array[:, base + p * PAIR : base + (p + 1) * PAIR]
                for base in range(0, array.shape[1], part_width)
                for p in pairs
            ],
            axis=1,
        )

    if fast:
        top, low_half = pick_weights(w_qkv, w_out, core_flag)
        far_top, near_low = square(top, 2), square(low_half, 1)
        diag_top, diag_low = square(far_top, 1), square(near_low, 2)
        later_top, later_low = lax.optimization_barrier((top, low_half, far_top, near_low))[:2]
        near_top, far_low = square(later_top, 1), square(later_low, 2)
        near, diag = (near_top, near_low), (diag_top, diag_low)
        far, shard = (far_top, far_low), (top, low_half)
        wide = 3 * part_width // 2
        weights_0, weights_1 = [
            jnp.concatenate(
                [block[:, at : at + wide] for both in (near, diag, far, shard) for block in both],
                axis=0,
            )
            for at in (0, wide)
        ]
        wide = 2 * wide
        out_blocks = [
            jnp.concatenate([block[0][:, wide:], block[1][:, wide:]], axis=1)
            for block in (shard, near, far, diag)
        ]
        out_half = jnp.concatenate(xor_blocks(out_blocks, scene), axis=0)
    else:
        core_qkv = pick_groups(w_qkv, 1, unit, core)
        core_out = pick_groups(w_out, 0, unit, core)
        weights_0, weights_1 = [
            lax.all_gather(columns_of(core_qkv, pairs), "fsdp", axis=0, tiled=True)
            for pairs in CHUNKS
        ]
        out_half = lax.all_gather(core_out, "fsdp", axis=0, tiled=True)

    other_tokens = lax.ppermute(own_tokens, "vox", swap)
    other_cotangent = lax.ppermute(own_cotangent, "vox", swap)
    lists = jnp.concatenate([key_blocks[0], slot_count[0][:, None]], axis=1)
    all_lists = in_order(
        core, lists, lax.ppermute(lists.astype(F32), "vox", swap).astype(jnp.int32), 0
    )
    chip_tokens = in_order(core, own_tokens, other_tokens, 0)
    chip_cotangent = in_order(core, own_cotangent, other_cotangent, 0)

    first_block = chip * blocks
    pool_blocks = blocks + 2 * reach
    window_id = (
        all_lists[:, :slot_total] - first_block + reach
        - 2 * (jnp.arange(blocks, dtype=jnp.int32) // 2)[:, None]
    )
    used = jnp.arange(slot_total, dtype=jnp.int32)[None, :] < all_lists[:, slot_total:]
    hits = jnp.logical_and(
        window_id[:, :, None] == jnp.arange(WINDOW, dtype=jnp.int32), used[:, :, None]
    )
    mult = jnp.sum(hits.astype(jnp.int32), axis=1)
    scene_total = valid_voxels.shape[1]
    pool_ids = first_block - reach + jnp.arange(pool_blocks, dtype=jnp.int32)
    valid = jnp.take(valid_voxels[0], jnp.clip(pool_ids, 0, scene_total - 1))
    group_heads = unit // HD
    scales = pick_groups(logit_scale, 0, group_heads, core)

    wide = chip_tokens.astype(F32)
    inverse = lax.rsqrt(jnp.mean(wide * wide, axis=1, keepdims=True) + EPS)
    normed = (wide * inverse * gain).astype(BF)
    if fast:
        turned = xor_blocks(jnp.split(normed, 4, axis=1), scene)
        normed = jnp.concatenate([turned[k] for k in ORDER], axis=1)
        normed_t = small_kernel(turn_kernel, "turn", [], [normed], [(normed.shape[::-1], BF)])[0]

    def pairings(first, second):
        return lax.ppermute(first, "vox", near_chips), lax.ppermute(second, "vox", far_chips)

    def heads_of(packed, upstream, chunk, begin=0, count=2, carried=()):
        pairs = CHUNKS[chunk]
        used = pairs[begin : begin + count]
        chunk_scales = jnp.concatenate([scales[2 * p : 2 * p + 2] for p in used])
        return attention(
            packed, *halos, upstream, mult, valid, chunk_scales, even_flag, pairs, begin, count,
            4 * chunk, carried,
        )

    def with_rims(grad, first, second):
        first, second = first.astype(F32), second.astype(F32)
        return jnp.concatenate(
            [
                grad[:margin] + jnp.where(even, second, first),
                grad[margin : rows - margin],
                grad[rows - margin :] + jnp.where(even, first, second),
            ],
            axis=0,
        ).astype(BF)

    def key_value_grads(keys, values, rims):
        return [with_rims(g, rims[0][i], rims[1][i]) for i, g in enumerate((keys, values))]

    def out_rows(pairs):
        return jnp.concatenate([out_half[p * PAIR : (p + 1) * PAIR] for p in pairs], axis=0)

    def groups_of(left, right, chunk):
        half = 3 * PAIR
        groups = [left[:, k * PAIR : (k + 1) * PAIR] for k in range(3)]
        groups += [right[:, k * PAIR : (k + 1) * PAIR] for k in range(3)]
        sets = ((0, 3, 4), (1, 2, 5)) if chunk == 0 else ((0, 3, 2), (1, 4, 5))
        evens = jnp.concatenate([groups[k] for k in sets[0]] + [left[:, half:]], axis=1)
        odds = jnp.concatenate([groups[k] for k in sets[1]] + [right[:, half:]], axis=1)
        return jnp.where(even, evens, odds), jnp.where(even, odds, evens).astype(BF)

    def halves_of(kept):
        left, right = kept[:, : 2 * PAIR], kept[:, PAIR : 3 * PAIR]
        if kept.shape[1] > 3 * PAIR:
            more = kept[:, 3 * PAIR :]
            cut = more.shape[0] // 2
            left = jnp.concatenate([left, more[:cut]], axis=0)
            right = jnp.concatenate([right, more[cut:]], axis=0)
        return jnp.where(low, left, right), jnp.where(low, right, left).astype(BF)

    packed_0, packed_1 = [dot(normed, weight).astype(BF) for weight in (weights_0, weights_1)]
    query_width = part_width // 2
    top, bottom = [
        jnp.concatenate([packed[at, query_width:] for packed in (packed_0, packed_1)], axis=1)
        for at in (slice(0, margin), slice(rows - margin, rows))
    ]
    halos = pairings(jnp.where(even, bottom, top), jnp.where(even, top, bottom))
    upstream = dot(chip_cotangent, out_half, ((1,), (1,))).astype(BF)
    first = heads_of(packed_0, upstream, 0)
    rims_0 = pairings(first[4], first[5])
    third = heads_of(packed_1, gate(upstream, first[4], first[5]), 1, 0, 1)
    rims_0 = [gate(rim, third[6]) for rim in rims_0]
    half = 3 * query_width // 2
    if fast:
        left_0, right_0, to_x, to_y = small_kernel(
            rim_kernel, "rims_first", [even_flag],
            [normed_t, *rims_0, first[1], first[2], first[3]],
            [((rows, half), BF)] * 2 + [((model_width // 2, half), BF)] * 2,
        )
        from_x0, from_y0 = square(to_x, 1), square(to_y, 2)
        fourth_in = gate(upstream, to_x, to_y)
    else:
        key_0, value_0 = key_value_grads(first[2], first[3], rims_0)
        grad_0 = jnp.concatenate([first[1], key_0, value_0], axis=1)
        fourth_in = upstream
    fourth = heads_of(packed_1, fourth_in, 1, 1, 1, (third[0], third[4], third[5]))
    rims_1 = pairings(fourth[4], fourth[5])

    att_0 = gate(first[0], fourth[6])
    att_1 = fourth[0]
    if fast:
        quarter = model_width // 4
        key_1, value_1, to_x, to_y = small_kernel(
            rim_kernel, "rims_second", [even_flag],
            [normed_t, *rims_1, third[2], fourth[2], third[3], fourth[3]],
            [((rows, query_width), BF)] * 2 + [((model_width // 2, query_width), BF)] * 2,
        )
        late_x, late_y = square(to_x, 1), square(to_y, 2)
        to_x, to_y, left, right, evens, odds = small_kernel(
            leave_kernel, "leave_early", [scene_flag],
            [normed_t, first[7], third[7], fourth[7], gate(chip_cotangent, to_x, to_y), third[1], fourth[1],
             left_0, right_0, from_x0, from_y0],
            [((3 * quarter, half), BF)] * 2
            + [((quarter, half), F32)] * 2
            + [((2, quarter, quarter), F32)] * 2,
            [pltpu.VMEM((4, PAIR, rows), BF)],
        )
        early_x, early_y = square(to_x, 1), square(to_y, 2)

        left_0, key_1, value_1 = lax.optimization_barrier((left_0, key_1, value_1, to_x, to_y))[:3]
        grad_0 = jnp.concatenate([left_0, right_0], axis=1)
        ngrad_part = dot(grad_0, weights_0, ((1,), (1,))) + dot(
            jnp.concatenate([third[1], fourth[1], key_1, value_1], axis=1), weights_1, ((1,), (1,))
        )
        height = model_width // 4
        kept_0, sent = groups_of(
            left + early_y[2 * height :].astype(F32), right + early_x[2 * height :].astype(F32), 0
        )
        got_0 = chips(sent, 1, n_vox)
        to_x, to_y, left, right = small_kernel(
            second_kernel, "second_exchange", [],
            [normed_t, third[1], fourth[1], key_1, value_1, early_x, early_y, late_x, late_y, evens, odds],
            [((height, half + quarter), BF)] * 2 + [((height, half + quarter), F32)] * 2,
        )
        end_x, end_y = square(to_x, 1), square(to_y, 2)
        att_0, att_1, got_0 = lax.optimization_barrier((att_0, att_1, got_0, to_x, to_y))[:3]
    else:
        key_1, value_1 = key_value_grads(
            *[jnp.concatenate([third[i], fourth[i]], axis=1) for i in (2, 3)], rims_1
        )
        grad_1 = jnp.concatenate([third[1], fourth[1], key_1, value_1], axis=1)
        ngrad_part = dot(grad_0, weights_0, ((1,), (1,))) + dot(grad_1, weights_1, ((1,), (1,)))
    mixed_part = dot(att_0, out_rows(CHUNKS[0])) + dot(att_1, out_rows(CHUNKS[1]))
    mixed_mine = lax.dynamic_slice_in_dim(mixed_part, core * own_rows, own_rows, 0)
    mixed_theirs = lax.dynamic_slice_in_dim(mixed_part, (1 - core) * own_rows, own_rows, 0)
    mixed = (
        own_tokens.astype(F32) + (mixed_mine + lax.ppermute(mixed_theirs, "vox", swap))
    ).astype(BF)

    ngrad_mine = lax.dynamic_slice_in_dim(ngrad_part, core * own_rows, own_rows, 0)
    ngrad_theirs = lax.dynamic_slice_in_dim(ngrad_part, (1 - core) * own_rows, own_rows, 0)
    normed_grad = ngrad_mine + lax.ppermute(ngrad_theirs, "vox", swap)
    if fast:
        held = jnp.split(normed_grad, 4, axis=1)
        normed_grad = jnp.concatenate(
            xor_blocks([held[ORDER.index(k)] for k in range(4)], scene), axis=1
        )

    own_wide = own_tokens.astype(F32)
    own_inverse = lax.rsqrt(jnp.mean(own_wide * own_wide, axis=1, keepdims=True) + EPS)
    gain_grad = jnp.sum(normed_grad * own_wide * own_inverse, axis=0)
    scaled_grad = normed_grad * gain
    token_grad = (
        own_cotangent.astype(F32)
        + own_inverse
        * (
            scaled_grad
            - own_wide
            * own_inverse
            * own_inverse
            * jnp.mean(scaled_grad * own_wide, axis=1, keepdims=True)
        )
    ).astype(BF)

    scale_parts = {}
    for pairs, sums in zip(
        CHUNKS, (first[6], jnp.concatenate([third[6], fourth[6]], axis=0))
    ):
        sums = jnp.sum(sums.reshape(2, 8, 2, PAIR), axis=(1, 3))
        for i, p in enumerate(pairs):
            scale_parts[p] = sums[i]
    scale_part = jnp.concatenate([scale_parts[p] for p in range(len(scale_parts))])
    scale_grad = spread_groups(scale_part, 0, group_heads, core)

    if fast:
        small = jnp.concatenate([gain_grad, scale_grad, jnp.zeros((112,), F32)]).reshape(9, 128)
        end_x, end_y, small = lax.optimization_barrier((end_x, end_y, small))
        small = small + square(small, 1)
        kept_0, sent = halves_of(kept_0 + got_0.astype(F32))
        got_0 = chips(sent, 2, n_vox)
        kept_1, sent = groups_of(left + end_y.astype(F32), right + end_x.astype(F32), 1)
        got_1 = chips(sent, 1, n_vox)
        small = gate(small, sent)
        small = small + square(small, 2)
        small = small + lax.ppermute(small, "vox", swap)
        got_1, small, token_grad = lax.optimization_barrier((got_1, small, token_grad))
        kept_1, sent = halves_of(kept_1 + got_1.astype(F32))
        got_1 = chips(sent, 2, n_vox)
        small = gate(small, sent)
        small = small + chips(small, 1, n_vox)
        small = small + chips(small, 2, n_vox)
        got_1, small, mixed = lax.optimization_barrier((got_1, small, mixed))
        small = small.reshape(-1)
        summed_gain, summed_scale = small[:model_width], small[model_width : model_width + HEADS]
        kept_1 = kept_1 + got_1.astype(F32)
        qkv_sums = [kept_0 + got_0.astype(F32), kept_1[:height]]
        out_sum = kept_1[height:]
    else:
        out_sums = [dot(att, chip_cotangent, ((0,), (0,))) for att in (att_0, att_1)]
        qkv_sums = [dot(normed, grad, ((0,), (0,))) for grad in (grad_0, grad_1)]
        summed_gain, summed_scale = lax.psum((gain_grad, scale_grad), ("vox", "fsdp"))

    if fast:
        half = out_sum.shape[1] // 2
        first, second = out_sum[:, :half], out_sum[:, half:]
        out_other = lax.ppermute(jnp.where(core == 0, second, first), "vox", swap)
        summed_out = in_order(core, jnp.where(core == 0, first, second), out_other, 0)

        a0, a1 = qkv_sums[0][:, :PAIR], qkv_sums[0][:, PAIR:]
        b0, b1 = qkv_sums[1][:, :PAIR], qkv_sums[1][:, PAIR:]

        def by_chip(options):
            value = options[3]
            for k in range(3):
                value = jnp.where(chip == k, options[k], value)
            return value

        g0 = by_chip((a0, a0, b1, b0))
        g1 = by_chip((b0, a1, a0, b1))
        g2 = by_chip((b1, b0, a1, a1))
        got = lax.ppermute(jnp.where(core == 0, g2, g0), "vox", swap)
        summed_qkv = jnp.concatenate(
            [
                jnp.where(core == 0, g0, g1),
                got,
                jnp.where(core == 0, g1, g2),
            ],
            axis=1,
        )
    else:
        by_pair = {}
        cols = {}
        for pairs, out_total, qkv_total in zip(CHUNKS, out_sums, qkv_sums):
            for i, p in enumerate(pairs):
                by_pair[p] = out_total[i * PAIR : (i + 1) * PAIR]
                for j in range(3):
                    at = (2 * j + i) * PAIR
                    cols[4 * j + p] = qkv_total[:, at : at + PAIR]
        out_total = jnp.concatenate([by_pair[p] for p in range(4)], axis=0)
        qkv_total = jnp.concatenate([cols[k] for k in range(12)], axis=1)
        out_total = spread_groups(out_total, 0, unit, core)
        qkv_total = lax.psum_scatter(qkv_total, "fsdp", scatter_dimension=0, tiled=True)
        qkv_total = spread_groups(qkv_total, 1, unit, core)
        summed_qkv = lax.psum_scatter(qkv_total, "vox", scatter_dimension=1, tiled=True)
        out_total = lax.psum_scatter(out_total, "fsdp", scatter_dimension=0, tiled=True)
        summed_out = lax.psum_scatter(out_total, "vox", scatter_dimension=1, tiled=True)

    return (
        mixed[None],
        token_grad[None],
        summed_qkv,
        summed_out,
        summed_gain,
        summed_scale,
    )


def solution(mesh):
    return jax.shard_map(
        on_device,
        mesh=mesh,
        in_specs=(
            P("fsdp", "vox", None),
            P(),
            P("fsdp", None),
            P("fsdp", None),
            P(),
            P("fsdp", "vox", None),
            P("fsdp", "vox"),
            P("fsdp", None),
            P("fsdp", "vox", None),
        ),
        out_specs=(
            P("fsdp", "vox", None),
            P("fsdp", "vox", None),
            P("fsdp", "vox"),
            P("fsdp", "vox"),
            P(),
            P(),
        ),
        check_vma=False,
    )
```

```python
import functools

import jax
import jax.numpy as jnp
from jax import lax
from jax.experimental import pallas as pl
from jax.experimental.pallas import tpu as pltpu
from jax.sharding import PartitionSpec as P

HEADS = 16
HD = 64
PAIR = 2 * HD
BLK = 64
WINDOW = 8
EPS = 1e-06
LOG2E = 1.4426950408889634
BF = jnp.bfloat16
F32 = jnp.float32


def dot(a, b, dims=((1,), (0,))):
    return lax.dot_general(a, b, (dims, ((), ())), preferred_element_type=F32)


def head_sums(x, same_head):
    high = x.astype(BF)
    low = (x - high.astype(F32)).astype(BF)
    return dot(high, same_head) + dot(low, same_head)


def unit_rows(x, same_head):
    length = jnp.sqrt(head_sums(x * x, same_head) + EPS)
    return x / length, length


def unit_back(unit, length, grad, same_head):
    return (grad - unit * head_sums(unit * grad, same_head)) / length


def attention_kernel(
    mult_ref, valid_ref, scale_ref, even_ref,
    q_ref, k_ref, v_ref, k1_ref, v1_ref, k2_ref, v2_ref, u_ref,
    *refs,
):
    carried, refs = (refs[:3], refs[3:]) if len(refs) > 22 else ((), refs)
    att_ref, dq_ref, dk_ref, dv_ref, rim1_ref, rim2_ref, ds_ref, turn_ref = refs[:8]
    k_unit, k_len, k_low, k_turn, v_low, v_turn, bias = refs[8:15]
    scores, grads, raised, w_lows, c_lows, dk, dv = refs[15:]
    held = slice(PAIR, 2 * PAIR) if carried else slice(0, PAIR)
    if carried:
        att_ref[:, :PAIR] = carried[0][...]
        rim1_ref[:, :, :PAIR] = carried[1][...]
        rim2_ref[:, :, :PAIR] = carried[2][...]
    rows = q_ref.shape[0]
    margin = k1_ref.shape[0]
    even = even_ref[0] == 1
    pool = rows + 2 * margin
    reach = margin // BLK
    steps = rows // PAIR
    span = WINDOW * BLK
    pair = pl.program_id(0)

    lane = lax.broadcasted_iota(jnp.int32, (BLK, PAIR), 1)
    row = lax.broadcasted_iota(jnp.int32, (BLK, PAIR), 0)
    head_a = lax.broadcasted_iota(jnp.int32, (PAIR, PAIR), 0) < HD
    head_b = lax.broadcasted_iota(jnp.int32, (PAIR, PAIR), 1) < HD
    same_head = jnp.where(head_a == head_b, 1.0, 0.0).astype(BF)
    first_lanes = head_b

    @pl.when(pair == 0)
    def _():
        for t in range(steps):
            for w in range(WINDOW):
                count = jnp.where(lane < BLK, mult_ref[2 * t, w], mult_ref[2 * t + 1, w])
                live = row < valid_ref[2 * t + w]
                seen = jnp.where(live, count, 0).astype(F32)
                bias[t, w * BLK : (w + 1) * BLK, :] = jnp.where(
                    seen > 0.0, jnp.log2(jnp.maximum(seen, 1.0)), -1e30
                )

    def split_heads(x):
        return jnp.concatenate(
            [jnp.where(first_lanes, x, 0.0), jnp.where(first_lanes, 0.0, x)], axis=0
        ).astype(BF)

    def take(at, keys, values):
        unit, length = unit_rows(keys.astype(F32), same_head)
        place = slice(at, at + keys.shape[0])
        k_unit[place, :] = unit
        k_len[place, :] = length
        k_low[place, :] = unit.astype(BF)
        v_low[place, :] = values

    for part in range(0, margin, BLK):
        here = slice(part, part + BLK)
        k1, k2 = k1_ref[here, :].astype(F32), k2_ref[here, :].astype(F32)
        v1, v2 = v1_ref[here, :].astype(F32), v2_ref[here, :].astype(F32)
        take(part, jnp.where(even, k2, k1), jnp.where(even, v2, v1).astype(BF))
        take(margin + rows + part, jnp.where(even, k1, k2), jnp.where(even, v1, v2).astype(BF))
    for part in range(0, rows, PAIR):
        here = slice(part, part + PAIR)
        take(margin + part, k_ref[here, :], v_ref[here, :])
    for part in range(0, pool, 128):
        place = slice(part, part + 128)
        k_turn[:, place] = jnp.transpose(k_low[place, :].astype(F32)).astype(BF)
        v_turn[:, place] = jnp.transpose(v_low[place, :].astype(F32)).astype(BF)

    dk[...] = jnp.zeros_like(dk)
    dv[...] = jnp.zeros_like(dv)
    wide_lane = lax.broadcasted_iota(jnp.int32, (1, 2 * PAIR), 1)
    scale = jnp.where(wide_lane < PAIR, scale_ref[2 * pair], scale_ref[2 * pair + 1])
    ds = jnp.zeros((8, 2 * PAIR), F32)

    def window_of(t):
        return slice(t * PAIR, t * PAIR + span)

    def begin(t):
        own, window = slice(t * PAIR, (t + 1) * PAIR), window_of(t)
        q_unit, q_len = unit_rows(q_ref[own, :].astype(F32), same_head)
        q_split = split_heads(q_unit)
        live = jnp.concatenate(
            [row < valid_ref[2 * t + reach], row < valid_ref[2 * t + 1 + reach]], axis=0
        )
        u_split = split_heads(jnp.where(live, u_ref[own, :].astype(F32), 0.0))
        scores[t % 2] = dot(k_low[window, :], q_split, ((1,), (1,)))
        grads[t % 2] = dot(v_low[window, :], u_split, ((1,), (1,)))
        return q_unit, q_len, q_split, live, u_split

    stretch = scale * LOG2E
    parts = [slice(i, i + 32) for i in range(0, span, 32)]

    def fold(x):
        return x.reshape(4, 8, 2 * PAIR)

    following = begin(0)
    for t in range(steps):
        own, window = slice(t * PAIR, (t + 1) * PAIR), window_of(t)
        q_unit, q_len, q_split, live, u_split = following
        s_ref, g_ref, e_ref = scores.at[t % 2], grads.at[t % 2], raised.at[t % 2]
        w_low, c_low = w_lows.at[t % 2], c_lows.at[t % 2]
        if t + 1 < steps:
            following = begin(t + 1)

        peak = jnp.full((8, 2 * PAIR), -1e30, F32)
        for part in parts:
            half = bias[t, part, :]
            x = s_ref[part, :] * stretch + jnp.concatenate([half, half], axis=1)
            e_ref[part, :] = x
            peak = jnp.maximum(peak, jnp.max(fold(x), axis=0))
        peak = jnp.max(peak, axis=0, keepdims=True)
        total = jnp.zeros((8, 2 * PAIR), F32)
        centre = jnp.zeros((8, 2 * PAIR), F32)
        for part in parts:
            e = jnp.exp2(e_ref[part, :] - peak)
            e_ref[part, :] = e
            total = total + jnp.sum(fold(e), axis=0)
            centre = centre + jnp.sum(fold(e * g_ref[part, :]), axis=0)
        share = 1.0 / jnp.sum(total, axis=0, keepdims=True)
        centre = jnp.sum(centre, axis=0, keepdims=True) * share
        for part in parts:
            w = e_ref[part, :] * share
            w_low[part, :] = w.astype(BF)
            sg = w * (g_ref[part, :] - centre)
            ds = ds + jnp.sum(fold(sg * s_ref[part, :]), axis=0)
            c_low[part, :] = (sg * scale).astype(BF)

        def own_heads(turned):
            return jnp.concatenate([turned[:HD, :PAIR], turned[HD:, PAIR:]], axis=0)

        mixed = own_heads(dot(v_turn[:, window], w_low[...]))
        att_ref[own, held] = jnp.where(live, jnp.transpose(mixed), 0.0).astype(BF)
        row_lane = lax.broadcasted_iota(jnp.int32, (PAIR, PAIR), 1)
        limit = jnp.where(
            row_lane < BLK, valid_ref[2 * t + reach], valid_ref[2 * t + 1 + reach] + BLK
        )
        turn_ref[:, own] = jnp.where(row_lane < limit, mixed, 0.0).astype(BF)
        q_grad = jnp.transpose(own_heads(dot(k_turn[:, window], c_low[...])))
        dq_ref[own, :] = unit_back(q_unit, q_len, q_grad, same_head).astype(BF)
        dv[window, :] += dot(w_low[...], u_split)
        dk[window, :] += dot(c_low[...], q_split)

    def key_grad(part):
        place = slice(part, part + BLK)
        return unit_back(k_unit[place, :], k_len[place, :], dk[place, :], same_head)

    for part in range(0, rows, BLK):
        here = slice(part, part + BLK)
        dk_ref[here, :] = key_grad(margin + part)
        dv_ref[here, :] = dv[margin + part : margin + part + BLK, :]
    for part in range(0, margin, BLK):
        here = slice(part, part + BLK)
        far = margin + rows + part
        kb, ka = key_grad(part), key_grad(far)
        vb, va = dv[part : part + BLK, :], dv[far : far + BLK, :]
        rim1_ref[0, here, held] = jnp.where(even, ka, kb).astype(BF)
        rim1_ref[1, here, held] = jnp.where(even, va, vb).astype(BF)
        rim2_ref[0, here, held] = jnp.where(even, kb, ka).astype(BF)
        rim2_ref[1, here, held] = jnp.where(even, vb, va).astype(BF)
    ds_ref[0, :, :] = ds


def attention(packed, first, second, upstream, mult, valid, scales, even, pairs, begin=0, count=2, base=0, carried=()):
    rows = packed.shape[0]
    width = count * PAIR
    both = width + (PAIR if carried else 0)
    margin = first.shape[0]
    pool = rows + 2 * margin
    held = len(pairs)
    stride = pairs[1] - pairs[0]
    steps = rows // PAIR
    span = WINDOW * BLK

    def at(offset):
        return lambda p, *_: (0, offset + p)

    return pl.pallas_call(
        attention_kernel,
        grid_spec=pltpu.PrefetchScalarGridSpec(
            num_scalar_prefetch=4,
            grid=(count,),
            in_specs=[
                pl.BlockSpec((rows, PAIR), at(begin)),
                pl.BlockSpec((rows, PAIR), at(held + begin)),
                pl.BlockSpec((rows, PAIR), at(2 * held + begin)),
                pl.BlockSpec((margin, PAIR), at(base + begin)),
                pl.BlockSpec((margin, PAIR), at(base + held + begin)),
                pl.BlockSpec((margin, PAIR), at(base + begin)),
                pl.BlockSpec((margin, PAIR), at(base + held + begin)),
                pl.BlockSpec((rows, PAIR), lambda p, *_: (0, pairs[begin] + stride * p)),
            ]
            + [whole(array.shape) for array in carried],
            out_specs=[
                pl.BlockSpec((rows, both // count), at(0)),
                pl.BlockSpec((rows, PAIR), at(0)),
                pl.BlockSpec((rows, PAIR), at(0)),
                pl.BlockSpec((rows, PAIR), at(0)),
                pl.BlockSpec((2, margin, both // count), lambda p, *_: (0, 0, p)),
                pl.BlockSpec((2, margin, both // count), lambda p, *_: (0, 0, p)),
                pl.BlockSpec((1, 8, 2 * PAIR), lambda p, *_: (p, 0, 0)),
                pl.BlockSpec((PAIR, rows), lambda p, *_: (p, 0)),
            ],
            scratch_shapes=[
                pltpu.VMEM((pool, PAIR), F32),
                pltpu.VMEM((pool, PAIR), F32),
                pltpu.VMEM((pool, PAIR), BF),
                pltpu.VMEM((PAIR, pool), BF),
                pltpu.VMEM((pool, PAIR), BF),
                pltpu.VMEM((PAIR, pool), BF),
                pltpu.VMEM((steps, span, PAIR), F32),
                pltpu.VMEM((2, span, 2 * PAIR), F32),
                pltpu.VMEM((2, span, 2 * PAIR), F32),
                pltpu.VMEM((2, span, 2 * PAIR), F32),
                pltpu.VMEM((2, span, 2 * PAIR), BF),
                pltpu.VMEM((2, span, 2 * PAIR), BF),
                pltpu.VMEM((pool, PAIR), F32),
                pltpu.VMEM((pool, PAIR), F32),
            ],
        ),
        out_shape=[
            jax.ShapeDtypeStruct((rows, both), BF),
            jax.ShapeDtypeStruct((rows, width), BF),
            jax.ShapeDtypeStruct((rows, width), F32),
            jax.ShapeDtypeStruct((rows, width), F32),
            jax.ShapeDtypeStruct((2, margin, both), BF),
            jax.ShapeDtypeStruct((2, margin, both), BF),
            jax.ShapeDtypeStruct((count, 8, 2 * PAIR), F32),
            jax.ShapeDtypeStruct((width, rows), BF),
        ],
        compiler_params=pltpu.CompilerParams(vmem_limit_bytes=24 * 1024 * 1024),
        cost_estimate=pl.CostEstimate(
            flops=8 * 2 * 6 * count * steps * span * 256 * 128,
            bytes_accessed=rows * width * 20,
            transcendentals=count * steps * span * 256,
        ),
        name="block_attention",
    )(
        mult, valid, scales, even,
        packed, packed, packed, first, first, second, second, upstream, *carried,
    )


def pick_kernel(core_ref, qkv_ref, out_ref, top_ref, low_ref):
    core = core_ref[0]
    at = 0
    for pairs in CHUNKS:
        for base in range(0, qkv_ref.shape[1], 8 * PAIR):
            for p in pairs:
                start = pl.multiple_of(base + 2 * p * PAIR + core * PAIR, PAIR)
                top_ref[:, at : at + PAIR] = qkv_ref[:PAIR, pl.ds(start, PAIR)]
                low_ref[:, at : at + PAIR] = qkv_ref[PAIR:, pl.ds(start, PAIR)]
                at += PAIR
    half = out_ref.shape[1] // 2
    rows = out_ref[pl.ds(pl.multiple_of(core * PAIR, PAIR), PAIR), :]
    top_ref[:, at:] = rows[:, :half]
    low_ref[:, at:] = rows[:, half:]


def whole(shape):
    return pl.BlockSpec(shape, lambda *_: (0,) * len(shape))


def small_kernel(kernel, name, scalars, arrays, outs, scratch=()):
    return pl.pallas_call(
        kernel,
        grid_spec=pltpu.PrefetchScalarGridSpec(
            num_scalar_prefetch=len(scalars),
            grid=(1,),
            in_specs=[whole(a.shape) for a in arrays],
            out_specs=[whole(shape) for shape, _ in outs],
            scratch_shapes=list(scratch),
        ),
        out_shape=[jax.ShapeDtypeStruct(shape, kind) for shape, kind in outs],
        compiler_params=pltpu.CompilerParams(vmem_limit_bytes=24 * 1024 * 1024),
        name=name,
    )(*scalars, *arrays)


def pick_weights(w_qkv, w_out, core_flag):
    height, columns = w_qkv.shape
    wide = columns // 2 + w_out.shape[1] // 2
    return small_kernel(
        pick_kernel, "pick_weights", [core_flag], [w_qkv, w_out], [((height // 2, wide), BF)] * 2
    )


def turn_kernel(x_ref, turned_ref):
    for i in range(0, x_ref.shape[0], PAIR):
        for j in range(0, x_ref.shape[1], PAIR):
            tile = x_ref[i : i + PAIR, j : j + PAIR].astype(F32)
            turned_ref[j : j + PAIR, i : i + PAIR] = jnp.transpose(tile).astype(BF)


def with_returned(even, rim1_ref, rim2_ref, index, grad):
    margin, rows = rim1_ref.shape[1], grad.shape[0]
    one, two = rim1_ref[index].astype(F32), rim2_ref[index].astype(F32)
    return jnp.concatenate(
        [
            grad[:margin] + jnp.where(even, two, one),
            grad[margin : rows - margin],
            grad[rows - margin :] + jnp.where(even, one, two),
        ],
        axis=0,
    ).astype(BF)


def first_kernel(
    even_ref, t_ref, rim1_ref, rim2_ref, q_ref, dk_ref, dv_ref, left_ref, right_ref, x_ref, y_ref
):
    even = even_ref[0] == 1
    size = t_ref.shape[0] // 4
    keys = with_returned(even, rim1_ref, rim2_ref, 0, dk_ref[...])
    left_ref[:, : 2 * PAIR] = q_ref[...]
    left_ref[:, 2 * PAIR :] = keys[:, :PAIR]
    right_ref[:, :PAIR] = keys[:, PAIR:]
    right_ref[:, PAIR:] = with_returned(even, rim1_ref, rim2_ref, 1, dv_ref[...])
    x_ref[...] = dot(t_ref[: 2 * size, :], left_ref[...]).astype(BF)
    y_ref[...] = dot(t_ref[size : 3 * size, :], right_ref[...]).astype(BF)


def put_tiles(ref, at, stride, value):
    height = value.shape[0]
    for j in range(value.shape[1] // PAIR):
        start = at + j * stride
        ref[start : start + height, :] = value[:, j * PAIR : (j + 1) * PAIR].astype(BF)


def get_tiles(ref, at, stride, height, count):
    return jnp.concatenate(
        [ref[at + j * stride : at + j * stride + height, :].astype(F32) for j in range(count)],
        axis=1,
    )


def leave_kernel(
    scene_ref, even_ref, t_ref, rim1_ref, rim2_ref, ka_ref, kb_ref, va_ref, vb_ref,
    a0_ref, a1_ref, a2_ref, cot_ref, q1_ref, q2_ref, left_ref, right_ref, fx_ref, fy_ref,
    x_ref, y_ref, key_ref, value_ref, kept_ref, extra_ref, at_ref,
):
    even = even_ref[0] == 1
    size = t_ref.shape[0] // 4
    two = 2 * size
    quarter = cot_ref.shape[1] // 4
    key_ref[...] = with_returned(
        even, rim1_ref, rim2_ref, 0, jnp.concatenate([ka_ref[...], kb_ref[...]], axis=1)
    )
    value_ref[...] = with_returned(
        even, rim1_ref, rim2_ref, 1, jnp.concatenate([va_ref[...], vb_ref[...]], axis=1)
    )
    to_x, to_y = t_ref[:two, :], t_ref[size : 3 * size, :]
    put_tiles(x_ref, 0, two, dot(to_x, q1_ref[...]))
    put_tiles(y_ref, 0, two, dot(to_y, q2_ref[...]))
    put_tiles(x_ref, two, two, dot(to_x, key_ref[...]))
    put_tiles(y_ref, two, two, dot(to_y, value_ref[...]))
    at_ref[0] = a0_ref[:PAIR, :]
    at_ref[3] = a0_ref[PAIR:, :]
    at_ref[1] = a1_ref[...]
    at_ref[2] = a2_ref[...]
    for i, k in enumerate(ORDER):
        grad = dot(at_ref[jnp.bitwise_xor(scene_ref[0], k)], cot_ref[...])
        evens = jnp.concatenate([grad[:, :quarter], grad[:, 2 * quarter : 3 * quarter]], axis=0)
        odds = jnp.concatenate([grad[:, quarter : 2 * quarter], grad[:, 3 * quarter :]], axis=0)
        if i < 2:
            put_tiles(x_ref, 3 * two + i * size, two, evens)
        else:
            extra_ref[i - 2] = evens
        if i in (1, 2):
            put_tiles(y_ref, 3 * two + (i - 1) * size, two, odds)
        else:
            extra_ref[2 + i // 3] = odds
    left, right = left_ref[...], right_ref[...]
    put_tiles(
        y_ref, 5 * two, size, dot(t_ref[two : 3 * size, :], left) + fx_ref[size:, :].astype(F32)
    )
    put_tiles(x_ref, 5 * two, size, dot(t_ref[:size, :], right) + fy_ref[:size, :].astype(F32))
    kept_ref[0] = dot(t_ref[3 * size :, :], left) + fx_ref[:size, :].astype(F32)
    kept_ref[1] = dot(t_ref[3 * size :, :], right) + fy_ref[size:, :].astype(F32)


def second_kernel(
    even_ref, t_ref, q1_ref, q2_ref, key_ref, value_ref, fx_ref, fy_ref, kept_ref, extra_ref,
    x_ref, y_ref, both_ref, held_ref, sent_ref,
):
    size = t_ref.shape[0] // 4

    def term(place, query_ref, other_ref, extra, from_ref, half):
        block = t_ref[place * size : (place + 1) * size, :]
        value = [dot(block, query_ref[...]), dot(block, other_ref[...]), extra]
        return jnp.concatenate(value, axis=1) + get_tiles(
            from_ref, half * size, 2 * size, size, 5
        )

    y_ref[...] = term(2, q1_ref, key_ref, extra_ref[0], fx_ref, 1).astype(BF)
    x_ref[...] = term(0, q2_ref, value_ref, extra_ref[2], fy_ref, 0).astype(BF)
    both_ref[0] = term(3, q1_ref, key_ref, extra_ref[1], fx_ref, 0)
    both_ref[1] = term(3, q2_ref, value_ref, extra_ref[3], fy_ref, 1)
    left = kept_ref[0] + get_tiles(fy_ref, 10 * size, size, size, 3)
    right = kept_ref[1] + get_tiles(fx_ref, 10 * size, size, size, 3)
    evens = jnp.concatenate([left[:, :PAIR], right[:, : 2 * PAIR]], axis=1)
    odds = jnp.concatenate([left[:, PAIR:], right[:, 2 * PAIR :]], axis=1)
    even = even_ref[0] == 1
    held_ref[...] = jnp.where(even, evens, odds)
    sent_ref[...] = jnp.where(even, odds, evens).astype(BF)


def gate(value, *others):
    return lax.optimization_barrier((value,) + others)[0]


def pick_groups(array, axis, unit, core):
    size = array.shape[axis]
    picked = [
        jnp.where(
            core == 0,
            lax.slice_in_dim(array, at, at + unit, axis=axis),
            lax.slice_in_dim(array, at + unit, at + 2 * unit, axis=axis),
        )
        for at in range(0, size, 2 * unit)
    ]
    return jnp.concatenate(picked, axis=axis)


def spread_groups(array, axis, unit, core):
    groups = jnp.split(array, array.shape[axis] // unit, axis=axis)
    parts = []
    for group in groups:
        empty = jnp.zeros_like(group)
        parts += [jnp.where(core == 0, group, empty), jnp.where(core == 0, empty, group)]
    return jnp.concatenate(parts, axis=axis)


def in_order(core, own, other, axis):
    first = jnp.where(core == 0, own, other)
    second = jnp.where(core == 0, other, own)
    return jnp.concatenate([first, second], axis=axis)


def xor_blocks(blocks, index):
    odd = (index & 1) == 1
    high = (index & 2) == 2
    near = [jnp.where(odd, blocks[k ^ 1], blocks[k]) for k in range(4)]
    return [jnp.where(high, near[k ^ 2], near[k]) for k in range(4)]


ORDER = (1, 3, 2, 0)
CHUNKS = ((0, 3), (1, 2))


def square(value, step):
    return lax.ppermute(value, "fsdp", [(i, i ^ step) for i in range(4)])


def chips(value, step, n_vox):
    return lax.ppermute(value, "vox", [(i, i ^ (2 * step)) for i in range(n_vox)])


def on_device(
    tokens, gain, w_qkv, w_out, logit_scale, key_blocks, slot_count, valid_voxels, cotangent
):
    own_tokens = tokens[0]
    own_cotangent = cotangent[0]
    own_rows, model_width = own_tokens.shape
    rows = 2 * own_rows
    own_blocks = key_blocks.shape[1]
    blocks = 2 * own_blocks
    slot_total = key_blocks.shape[2]
    reach = own_blocks // 2
    margin = reach * BLK
    n_vox = lax.axis_size("vox")
    n_fsdp = lax.axis_size("fsdp")
    n_chip = n_vox // 2
    place = lax.axis_index("vox")
    scene = lax.axis_index("fsdp")
    core = place % 2
    chip = place // 2
    fast = n_vox == 8 and n_fsdp == 4
    unit = 128 if fast else 64
    swap = [(i, i ^ 1) for i in range(n_vox)]
    even, low = chip % 2 == 0, chip < 2
    even_flag, core_flag, scene_flag = [
        jnp.reshape(x, (1,)).astype(jnp.int32) for x in (even, core, scene)
    ]
    near_chips = [(i, i ^ 2) for i in range(n_vox)]
    far_chips = []
    for i in range(n_vox):
        to = i // 2 + (1 if i // 2 % 2 else -1)
        far_chips.append((i, 2 * to + i % 2 if 0 <= to < n_chip else i))
    part_width = model_width // 2

    def columns_of(array, pairs):
        return jnp.concatenate(
            [
                array[:, base + p * PAIR : base + (p + 1) * PAIR]
                for base in range(0, array.shape[1], part_width)
                for p in pairs
            ],
            axis=1,
        )

    if fast:
        top, low_half = pick_weights(w_qkv, w_out, core_flag)
        far_top, near_low = square(top, 2), square(low_half, 1)
        near_top, far_low = square(top, 1), square(low_half, 2)
        diag_top, diag_low = square(far_top, 1), square(near_low, 2)
        near, diag = (near_top, near_low), (diag_top, diag_low)
        far, shard = (far_top, far_low), (top, low_half)
        wide = 3 * part_width // 2
        weights_0, weights_1 = [
            jnp.concatenate(
                [block[:, at : at + wide] for both in (near, diag, far, shard) for block in both],
                axis=0,
            )
            for at in (0, wide)
        ]
        wide = 2 * wide
        out_blocks = [
            jnp.concatenate([block[0][:, wide:], block[1][:, wide:]], axis=1)
            for block in (shard, near, far, diag)
        ]
        out_half = jnp.concatenate(xor_blocks(out_blocks, scene), axis=0)
    else:
        core_qkv = pick_groups(w_qkv, 1, unit, core)
        core_out = pick_groups(w_out, 0, unit, core)
        weights_0, weights_1 = [
            lax.all_gather(columns_of(core_qkv, pairs), "fsdp", axis=0, tiled=True)
            for pairs in CHUNKS
        ]
        out_half = lax.all_gather(core_out, "fsdp", axis=0, tiled=True)

    other_tokens = lax.ppermute(own_tokens, "vox", swap)
    other_cotangent = lax.ppermute(own_cotangent, "vox", swap)
    lists = jnp.concatenate([key_blocks[0], slot_count[0][:, None]], axis=1)
    all_lists = in_order(
        core, lists, lax.ppermute(lists.astype(F32), "vox", swap).astype(jnp.int32), 0
    )
    chip_tokens = in_order(core, own_tokens, other_tokens, 0)
    chip_cotangent = in_order(core, own_cotangent, other_cotangent, 0)

    first_block = chip * blocks
    pool_blocks = blocks + 2 * reach
    window_id = (
        all_lists[:, :slot_total] - first_block + reach
        - 2 * (jnp.arange(blocks, dtype=jnp.int32) // 2)[:, None]
    )
    used = jnp.arange(slot_total, dtype=jnp.int32)[None, :] < all_lists[:, slot_total:]
    hits = jnp.logical_and(
        window_id[:, :, None] == jnp.arange(WINDOW, dtype=jnp.int32), used[:, :, None]
    )
    mult = jnp.sum(hits.astype(jnp.int32), axis=1)
    scene_total = valid_voxels.shape[1]
    pool_ids = first_block - reach + jnp.arange(pool_blocks, dtype=jnp.int32)
    valid = jnp.take(valid_voxels[0], jnp.clip(pool_ids, 0, scene_total - 1))
    group_heads = unit // HD
    scales = pick_groups(logit_scale, 0, group_heads, core)

    wide = chip_tokens.astype(F32)
    inverse = lax.rsqrt(jnp.mean(wide * wide, axis=1, keepdims=True) + EPS)
    normed = (wide * inverse * gain).astype(BF)
    if fast:
        turned = xor_blocks(jnp.split(normed, 4, axis=1), scene)
        normed = jnp.concatenate([turned[k] for k in ORDER], axis=1)
        normed_t = small_kernel(turn_kernel, "turn", [], [normed], [(normed.shape[::-1], BF)])[0]

    def pairings(first, second):
        return lax.ppermute(first, "vox", near_chips), lax.ppermute(second, "vox", far_chips)

    def heads_of(packed, upstream, chunk, begin=0, count=2, carried=()):
        pairs = CHUNKS[chunk]
        used = pairs[begin : begin + count]
        chunk_scales = jnp.concatenate([scales[2 * p : 2 * p + 2] for p in used])
        return attention(
            packed, *halos, upstream, mult, valid, chunk_scales, even_flag, pairs, begin, count,
            4 * chunk, carried,
        )

    def with_rims(grad, first, second):
        first, second = first.astype(F32), second.astype(F32)
        return jnp.concatenate(
            [
                grad[:margin] + jnp.where(even, second, first),
                grad[margin : rows - margin],
                grad[rows - margin :] + jnp.where(even, first, second),
            ],
            axis=0,
        ).astype(BF)

    def key_value_grads(keys, values, rims):
        return [with_rims(g, rims[0][i], rims[1][i]) for i, g in enumerate((keys, values))]

    def out_rows(pairs):
        return jnp.concatenate([out_half[p * PAIR : (p + 1) * PAIR] for p in pairs], axis=0)

    def groups_of(left, right, chunk):
        half = 3 * PAIR
        groups = [left[:, k * PAIR : (k + 1) * PAIR] for k in range(3)]
        groups += [right[:, k * PAIR : (k + 1) * PAIR] for k in range(3)]
        sets = ((0, 3, 4), (1, 2, 5)) if chunk == 0 else ((0, 3, 2), (1, 4, 5))
        evens = jnp.concatenate([groups[k] for k in sets[0]] + [left[:, half:]], axis=1)
        odds = jnp.concatenate([groups[k] for k in sets[1]] + [right[:, half:]], axis=1)
        return jnp.where(even, evens, odds), jnp.where(even, odds, evens).astype(BF)

    def halves_of(kept):
        left, right = kept[:, : 2 * PAIR], kept[:, PAIR : 3 * PAIR]
        if kept.shape[1] > 3 * PAIR:
            more = kept[:, 3 * PAIR :]
            cut = more.shape[0] // 2
            left = jnp.concatenate([left, more[:cut]], axis=0)
            right = jnp.concatenate([right, more[cut:]], axis=0)
        return jnp.where(low, left, right), jnp.where(low, right, left).astype(BF)

    packed_0, packed_1 = [dot(normed, weight).astype(BF) for weight in (weights_0, weights_1)]
    query_width = part_width // 2
    top, bottom = [
        jnp.concatenate([packed[at, query_width:] for packed in (packed_0, packed_1)], axis=1)
        for at in (slice(0, margin), slice(rows - margin, rows))
    ]
    halos = pairings(jnp.where(even, bottom, top), jnp.where(even, top, bottom))
    upstream = dot(chip_cotangent, out_half, ((1,), (1,))).astype(BF)
    first = heads_of(packed_0, upstream, 0)
    rims_0 = pairings(first[4], first[5])
    third = heads_of(packed_1, gate(upstream, first[4], first[5]), 1, 0, 1)
    rims_0 = [gate(rim, third[6]) for rim in rims_0]
    half = 3 * query_width // 2
    if fast:
        left_0, right_0, to_x, to_y = small_kernel(
            first_kernel, "leave_first", [even_flag],
            [normed_t, *rims_0, first[1], first[2], first[3]],
            [((rows, half), BF)] * 2 + [((model_width // 2, half), BF)] * 2,
        )
        from_x0, from_y0 = square(to_x, 1), square(to_y, 2)
        fourth_in = gate(upstream, to_x, to_y)
    else:
        key_0, value_0 = key_value_grads(first[2], first[3], rims_0)
        grad_0 = jnp.concatenate([first[1], key_0, value_0], axis=1)
        fourth_in = upstream
    fourth = heads_of(packed_1, fourth_in, 1, 1, 1, (third[0], third[4], third[5]))
    rims_1 = pairings(fourth[4], fourth[5])

    att_0 = gate(first[0], fourth[6])
    att_1 = fourth[0]
    if fast:
        quarter = model_width // 4
        tiles = 13 * quarter
        to_x, to_y, key_1, value_1, kept_0, extra = small_kernel(
            leave_kernel, "leave", [scene_flag, even_flag],
            [normed_t, *rims_1, third[2], fourth[2], third[3], fourth[3], first[7], third[7],
             fourth[7], chip_cotangent, third[1], fourth[1], left_0, right_0, from_x0, from_y0],
            [((tiles, PAIR), BF)] * 2
            + [((rows, query_width), BF)] * 2
            + [((2, quarter, half), F32), ((4, quarter, quarter), F32)],
            [pltpu.VMEM((4, PAIR, rows), BF)],
        )
        from_x, from_y = square(to_x, 1), square(to_y, 2)
        left_0, key_0, att_0, att_1 = lax.optimization_barrier(
            (left_0, key_1, att_0, att_1, to_x, to_y)
        )[:4]
        grad_0 = jnp.concatenate([left_0, right_0], axis=1)
        grad_1 = jnp.concatenate([third[1], fourth[1], key_0, value_1], axis=1)
    else:
        key_1, value_1 = key_value_grads(
            *[jnp.concatenate([third[i], fourth[i]], axis=1) for i in (2, 3)], rims_1
        )
        grad_1 = jnp.concatenate([third[1], fourth[1], key_1, value_1], axis=1)
    ngrad_part = dot(grad_0, weights_0, ((1,), (1,))) + dot(grad_1, weights_1, ((1,), (1,)))
    mixed_part = dot(att_0, out_rows(CHUNKS[0])) + dot(att_1, out_rows(CHUNKS[1]))
    mixed_mine = lax.dynamic_slice_in_dim(mixed_part, core * own_rows, own_rows, 0)
    mixed_theirs = lax.dynamic_slice_in_dim(mixed_part, (1 - core) * own_rows, own_rows, 0)
    mixed = (
        own_tokens.astype(F32) + (mixed_mine + lax.ppermute(mixed_theirs, "vox", swap))
    ).astype(BF)

    ngrad_mine = lax.dynamic_slice_in_dim(ngrad_part, core * own_rows, own_rows, 0)
    ngrad_theirs = lax.dynamic_slice_in_dim(ngrad_part, (1 - core) * own_rows, own_rows, 0)
    normed_grad = ngrad_mine + lax.ppermute(ngrad_theirs, "vox", swap)
    if fast:
        held = jnp.split(normed_grad, 4, axis=1)
        normed_grad = jnp.concatenate(
            xor_blocks([held[ORDER.index(k)] for k in range(4)], scene), axis=1
        )

    own_wide = own_tokens.astype(F32)
    own_inverse = lax.rsqrt(jnp.mean(own_wide * own_wide, axis=1, keepdims=True) + EPS)
    gain_grad = jnp.sum(normed_grad * own_wide * own_inverse, axis=0)
    scaled_grad = normed_grad * gain
    token_grad = (
        own_cotangent.astype(F32)
        + own_inverse
        * (
            scaled_grad
            - own_wide
            * own_inverse
            * own_inverse
            * jnp.mean(scaled_grad * own_wide, axis=1, keepdims=True)
        )
    ).astype(BF)

    scale_parts = {}
    for pairs, sums in zip(
        CHUNKS, (first[6], jnp.concatenate([third[6], fourth[6]], axis=0))
    ):
        sums = jnp.sum(sums.reshape(2, 8, 2, PAIR), axis=(1, 3))
        for i, p in enumerate(pairs):
            scale_parts[p] = sums[i]
    scale_part = jnp.concatenate([scale_parts[p] for p in range(len(scale_parts))])
    scale_grad = spread_groups(scale_part, 0, group_heads, core)

    if fast:
        small = jnp.concatenate([gain_grad, scale_grad, jnp.zeros((112,), F32)]).reshape(9, 128)
        from_x, from_y, small, mixed_part, _ = lax.optimization_barrier(
            (from_x, from_y, small, mixed_part, token_grad)
        )
        to_x, to_y, both, kept_0, sent = small_kernel(
            second_kernel, "second_exchange", [even_flag],
            [normed_t, third[1], fourth[1], key_1, value_1, from_x, from_y, kept_0, extra],
            [((quarter, half + quarter), BF)] * 2
            + [((2, quarter, half + quarter), F32), ((quarter, half), F32), ((quarter, half), BF)],
        )
        end_x, end_y = square(to_x, 1), square(to_y, 2)
        sent, small = lax.optimization_barrier((sent, small, to_x, to_y))[:2]
        got_0 = chips(sent, 1, n_vox)
        small = small + square(small, 1)
        kept_1, sent = groups_of(both[0] + end_y.astype(F32), both[1] + end_x.astype(F32), 1)
        got_1 = chips(sent, 1, n_vox)
        small, got_0 = lax.optimization_barrier((small, got_0, sent))[:2]
        small = small + square(small, 2)
        small = small + lax.ppermute(small, "vox", swap)
        kept_0, sent = halves_of(kept_0 + got_0.astype(F32))
        got_0 = chips(sent, 2, n_vox)
        got_1, small = lax.optimization_barrier((got_1, small))
        kept_1, sent = halves_of(kept_1 + got_1.astype(F32))
        got_1 = chips(sent, 2, n_vox)
        small = gate(small, sent)
        small = small + chips(small, 1, n_vox)
        small = small + chips(small, 2, n_vox)
        got_1, small = lax.optimization_barrier((got_1, small))
        small = small.reshape(-1)
        summed_gain, summed_scale = small[:model_width], small[model_width : model_width + HEADS]
        kept_1 = kept_1 + got_1.astype(F32)
        height = model_width // 4
        qkv_sums = [kept_0 + got_0.astype(F32), kept_1[:height]]
        out_sum = kept_1[height:]
    else:
        out_sums = [dot(att, chip_cotangent, ((0,), (0,))) for att in (att_0, att_1)]
        qkv_sums = [dot(normed, grad, ((0,), (0,))) for grad in (grad_0, grad_1)]
        summed_gain, summed_scale = lax.psum((gain_grad, scale_grad), ("vox", "fsdp"))

    if fast:
        half = out_sum.shape[1] // 2
        first, second = out_sum[:, :half], out_sum[:, half:]
        out_other = lax.ppermute(jnp.where(core == 0, second, first), "vox", swap)
        summed_out = in_order(core, jnp.where(core == 0, first, second), out_other, 0)

        a0, a1 = qkv_sums[0][:, :PAIR], qkv_sums[0][:, PAIR:]
        b0, b1 = qkv_sums[1][:, :PAIR], qkv_sums[1][:, PAIR:]

        def by_chip(options):
            value = options[3]
            for k in range(3):
                value = jnp.where(chip == k, options[k], value)
            return value

        g0 = by_chip((a0, a0, b1, b0))
        g1 = by_chip((b0, a1, a0, b1))
        g2 = by_chip((b1, b0, a1, a1))
        got = lax.ppermute(jnp.where(core == 0, g2, g0), "vox", swap)
        summed_qkv = jnp.concatenate(
            [
                jnp.where(core == 0, g0, g1),
                got,
                jnp.where(core == 0, g1, g2),
            ],
            axis=1,
        )
    else:
        by_pair = {}
        cols = {}
        for pairs, out_total, qkv_total in zip(CHUNKS, out_sums, qkv_sums):
            for i, p in enumerate(pairs):
                by_pair[p] = out_total[i * PAIR : (i + 1) * PAIR]
                for j in range(3):
                    at = (2 * j + i) * PAIR
                    cols[4 * j + p] = qkv_total[:, at : at + PAIR]
        out_total = jnp.concatenate([by_pair[p] for p in range(4)], axis=0)
        qkv_total = jnp.concatenate([cols[k] for k in range(12)], axis=1)
        out_total = spread_groups(out_total, 0, unit, core)
        qkv_total = lax.psum_scatter(qkv_total, "fsdp", scatter_dimension=0, tiled=True)
        qkv_total = spread_groups(qkv_total, 1, unit, core)
        summed_qkv = lax.psum_scatter(qkv_total, "vox", scatter_dimension=1, tiled=True)
        out_total = lax.psum_scatter(out_total, "fsdp", scatter_dimension=0, tiled=True)
        summed_out = lax.psum_scatter(out_total, "vox", scatter_dimension=1, tiled=True)

    return (
        mixed[None],
        token_grad[None],
        summed_qkv,
        summed_out,
        summed_gain,
        summed_scale,
    )


def solution(mesh):
    return jax.shard_map(
        on_device,
        mesh=mesh,
        in_specs=(
            P("fsdp", "vox", None),
            P(),
            P("fsdp", None),
            P("fsdp", None),
            P(),
            P("fsdp", "vox", None),
            P("fsdp", "vox"),
            P("fsdp", None),
            P("fsdp", "vox", None),
        ),
        out_specs=(
            P("fsdp", "vox", None),
            P("fsdp", "vox", None),
            P("fsdp", "vox"),
            P("fsdp", "vox"),
            P(),
            P(),
        ),
        check_vma=False,
    )
```

```python
import functools

import jax
import jax.numpy as jnp
from jax import lax
from jax.experimental import pallas as pl
from jax.experimental.pallas import tpu as pltpu
from jax.sharding import PartitionSpec as P

HEADS = 16
HD = 64
PAIR = 2 * HD
BLK = 64
WINDOW = 8
EPS = 1e-06
LOG2E = 1.4426950408889634
BF = jnp.bfloat16
F32 = jnp.float32


def dot(a, b, dims=((1,), (0,))):
    return lax.dot_general(a, b, (dims, ((), ())), preferred_element_type=F32)


def head_sums(x, same_head):
    high = x.astype(BF)
    low = (x - high.astype(F32)).astype(BF)
    return dot(high, same_head) + dot(low, same_head)


def unit_rows(x, same_head):
    length = jnp.sqrt(head_sums(x * x, same_head) + EPS)
    return x / length, length


def unit_back(unit, length, grad, same_head):
    return (grad - unit * head_sums(unit * grad, same_head)) / length


def attention_kernel(
    mult_ref, valid_ref, scale_ref, even_ref,
    q_ref, k_ref, v_ref, k1_ref, v1_ref, k2_ref, v2_ref, u_ref,
    *refs,
):
    carried, refs = (refs[:3], refs[3:]) if len(refs) > 22 else ((), refs)
    att_ref, dq_ref, dk_ref, dv_ref, rim1_ref, rim2_ref, ds_ref, turn_ref = refs[:8]
    k_unit, k_len, k_low, k_turn, v_low, v_turn, bias = refs[8:15]
    scores, grads, raised, w_lows, c_lows, dk, dv = refs[15:]
    held = slice(PAIR, 2 * PAIR) if carried else slice(0, PAIR)
    if carried:
        att_ref[:, :PAIR] = carried[0][...]
        rim1_ref[:, :, :PAIR] = carried[1][...]
        rim2_ref[:, :, :PAIR] = carried[2][...]
    rows = q_ref.shape[0]
    margin = k1_ref.shape[0]
    even = even_ref[0] == 1
    pool = rows + 2 * margin
    reach = margin // BLK
    steps = rows // PAIR
    span = WINDOW * BLK
    pair = pl.program_id(0)

    lane = lax.broadcasted_iota(jnp.int32, (BLK, PAIR), 1)
    row = lax.broadcasted_iota(jnp.int32, (BLK, PAIR), 0)
    head_a = lax.broadcasted_iota(jnp.int32, (PAIR, PAIR), 0) < HD
    head_b = lax.broadcasted_iota(jnp.int32, (PAIR, PAIR), 1) < HD
    same_head = jnp.where(head_a == head_b, 1.0, 0.0).astype(BF)
    first_lanes = head_b

    @pl.when(pair == 0)
    def _():
        for t in range(steps):
            for w in range(WINDOW):
                count = jnp.where(lane < BLK, mult_ref[2 * t, w], mult_ref[2 * t + 1, w])
                live = row < valid_ref[2 * t + w]
                seen = jnp.where(live, count, 0).astype(F32)
                bias[t, w * BLK : (w + 1) * BLK, :] = jnp.where(
                    seen > 0.0, jnp.log2(jnp.maximum(seen, 1.0)), -1e30
                )

    def split_heads(x):
        return jnp.concatenate(
            [jnp.where(first_lanes, x, 0.0), jnp.where(first_lanes, 0.0, x)], axis=0
        ).astype(BF)

    def take(at, keys, values):
        unit, length = unit_rows(keys.astype(F32), same_head)
        place = slice(at, at + keys.shape[0])
        k_unit[place, :] = unit
        k_len[place, :] = length
        k_low[place, :] = unit.astype(BF)
        v_low[place, :] = values

    for part in range(0, margin, BLK):
        here = slice(part, part + BLK)
        k1, k2 = k1_ref[here, :].astype(F32), k2_ref[here, :].astype(F32)
        v1, v2 = v1_ref[here, :].astype(F32), v2_ref[here, :].astype(F32)
        take(part, jnp.where(even, k2, k1), jnp.where(even, v2, v1).astype(BF))
        take(margin + rows + part, jnp.where(even, k1, k2), jnp.where(even, v1, v2).astype(BF))
    for part in range(0, rows, PAIR):
        here = slice(part, part + PAIR)
        take(margin + part, k_ref[here, :], v_ref[here, :])
    for part in range(0, pool, 128):
        place = slice(part, part + 128)
        k_turn[:, place] = jnp.transpose(k_low[place, :].astype(F32)).astype(BF)
        v_turn[:, place] = jnp.transpose(v_low[place, :].astype(F32)).astype(BF)

    dk[...] = jnp.zeros_like(dk)
    dv[...] = jnp.zeros_like(dv)
    wide_lane = lax.broadcasted_iota(jnp.int32, (1, 2 * PAIR), 1)
    scale = jnp.where(wide_lane < PAIR, scale_ref[2 * pair], scale_ref[2 * pair + 1])
    ds = jnp.zeros((8, 2 * PAIR), F32)

    def window_of(t):
        return slice(t * PAIR, t * PAIR + span)

    def begin(t):
        own, window = slice(t * PAIR, (t + 1) * PAIR), window_of(t)
        q_unit, q_len = unit_rows(q_ref[own, :].astype(F32), same_head)
        q_split = split_heads(q_unit)
        live = jnp.concatenate(
            [row < valid_ref[2 * t + reach], row < valid_ref[2 * t + 1 + reach]], axis=0
        )
        u_split = split_heads(jnp.where(live, u_ref[own, :].astype(F32), 0.0))
        scores[t % 2] = dot(k_low[window, :], q_split, ((1,), (1,)))
        grads[t % 2] = dot(v_low[window, :], u_split, ((1,), (1,)))
        return q_unit, q_len, q_split, live, u_split

    stretch = scale * LOG2E
    parts = [slice(i, i + 32) for i in range(0, span, 32)]

    def fold(x):
        return x.reshape(4, 8, 2 * PAIR)

    following = begin(0)
    for t in range(steps):
        own, window = slice(t * PAIR, (t + 1) * PAIR), window_of(t)
        q_unit, q_len, q_split, live, u_split = following
        s_ref, g_ref, e_ref = scores.at[t % 2], grads.at[t % 2], raised.at[t % 2]
        w_low, c_low = w_lows.at[t % 2], c_lows.at[t % 2]
        if t + 1 < steps:
            following = begin(t + 1)

        peak = jnp.full((8, 2 * PAIR), -1e30, F32)
        for part in parts:
            half = bias[t, part, :]
            x = s_ref[part, :] * stretch + jnp.concatenate([half, half], axis=1)
            e_ref[part, :] = x
            peak = jnp.maximum(peak, jnp.max(fold(x), axis=0))
        peak = jnp.max(peak, axis=0, keepdims=True)
        total = jnp.zeros((8, 2 * PAIR), F32)
        centre = jnp.zeros((8, 2 * PAIR), F32)
        for part in parts:
            e = jnp.exp2(e_ref[part, :] - peak)
            e_ref[part, :] = e
            total = total + jnp.sum(fold(e), axis=0)
            centre = centre + jnp.sum(fold(e * g_ref[part, :]), axis=0)
        share = 1.0 / jnp.sum(total, axis=0, keepdims=True)
        centre = jnp.sum(centre, axis=0, keepdims=True) * share
        for part in parts:
            w = e_ref[part, :] * share
            w_low[part, :] = w.astype(BF)
            sg = w * (g_ref[part, :] - centre)
            ds = ds + jnp.sum(fold(sg * s_ref[part, :]), axis=0)
            c_low[part, :] = (sg * scale).astype(BF)

        def own_heads(turned):
            return jnp.concatenate([turned[:HD, :PAIR], turned[HD:, PAIR:]], axis=0)

        mixed = own_heads(dot(v_turn[:, window], w_low[...]))
        att_ref[own, held] = jnp.where(live, jnp.transpose(mixed), 0.0).astype(BF)
        row_lane = lax.broadcasted_iota(jnp.int32, (PAIR, PAIR), 1)
        limit = jnp.where(
            row_lane < BLK, valid_ref[2 * t + reach], valid_ref[2 * t + 1 + reach] + BLK
        )
        turn_ref[:, own] = jnp.where(row_lane < limit, mixed, 0.0).astype(BF)
        q_grad = jnp.transpose(own_heads(dot(k_turn[:, window], c_low[...])))
        dq_ref[own, :] = unit_back(q_unit, q_len, q_grad, same_head).astype(BF)
        dv[window, :] += dot(w_low[...], u_split)
        dk[window, :] += dot(c_low[...], q_split)

    def key_grad(part):
        place = slice(part, part + BLK)
        return unit_back(k_unit[place, :], k_len[place, :], dk[place, :], same_head)

    for part in range(0, rows, BLK):
        here = slice(part, part + BLK)
        dk_ref[here, :] = key_grad(margin + part)
        dv_ref[here, :] = dv[margin + part : margin + part + BLK, :]
    for part in range(0, margin, BLK):
        here = slice(part, part + BLK)
        far = margin + rows + part
        kb, ka = key_grad(part), key_grad(far)
        vb, va = dv[part : part + BLK, :], dv[far : far + BLK, :]
        rim1_ref[0, here, held] = jnp.where(even, ka, kb).astype(BF)
        rim1_ref[1, here, held] = jnp.where(even, va, vb).astype(BF)
        rim2_ref[0, here, held] = jnp.where(even, kb, ka).astype(BF)
        rim2_ref[1, here, held] = jnp.where(even, vb, va).astype(BF)
    ds_ref[0, :, :] = ds


def attention(packed, first, second, upstream, mult, valid, scales, even, pairs, begin=0, count=2, base=0, carried=()):
    rows = packed.shape[0]
    width = count * PAIR
    both = width + (PAIR if carried else 0)
    margin = first.shape[0]
    pool = rows + 2 * margin
    held = len(pairs)
    stride = pairs[1] - pairs[0]
    steps = rows // PAIR
    span = WINDOW * BLK

    def at(offset):
        return lambda p, *_: (0, offset + p)

    return pl.pallas_call(
        attention_kernel,
        grid_spec=pltpu.PrefetchScalarGridSpec(
            num_scalar_prefetch=4,
            grid=(count,),
            in_specs=[
                pl.BlockSpec((rows, PAIR), at(begin)),
                pl.BlockSpec((rows, PAIR), at(held + begin)),
                pl.BlockSpec((rows, PAIR), at(2 * held + begin)),
                pl.BlockSpec((margin, PAIR), at(base + begin)),
                pl.BlockSpec((margin, PAIR), at(base + held + begin)),
                pl.BlockSpec((margin, PAIR), at(base + begin)),
                pl.BlockSpec((margin, PAIR), at(base + held + begin)),
                pl.BlockSpec((rows, PAIR), lambda p, *_: (0, pairs[begin] + stride * p)),
            ]
            + [whole(array.shape) for array in carried],
            out_specs=[
                pl.BlockSpec((rows, both // count), at(0)),
                pl.BlockSpec((rows, PAIR), at(0)),
                pl.BlockSpec((rows, PAIR), at(0)),
                pl.BlockSpec((rows, PAIR), at(0)),
                pl.BlockSpec((2, margin, both // count), lambda p, *_: (0, 0, p)),
                pl.BlockSpec((2, margin, both // count), lambda p, *_: (0, 0, p)),
                pl.BlockSpec((1, 8, 2 * PAIR), lambda p, *_: (p, 0, 0)),
                pl.BlockSpec((PAIR, rows), lambda p, *_: (p, 0)),
            ],
            scratch_shapes=[
                pltpu.VMEM((pool, PAIR), F32),
                pltpu.VMEM((pool, PAIR), F32),
                pltpu.VMEM((pool, PAIR), BF),
                pltpu.VMEM((PAIR, pool), BF),
                pltpu.VMEM((pool, PAIR), BF),
                pltpu.VMEM((PAIR, pool), BF),
                pltpu.VMEM((steps, span, PAIR), F32),
                pltpu.VMEM((2, span, 2 * PAIR), F32),
                pltpu.VMEM((2, span, 2 * PAIR), F32),
                pltpu.VMEM((2, span, 2 * PAIR), F32),
                pltpu.VMEM((2, span, 2 * PAIR), BF),
                pltpu.VMEM((2, span, 2 * PAIR), BF),
                pltpu.VMEM((pool, PAIR), F32),
                pltpu.VMEM((pool, PAIR), F32),
            ],
        ),
        out_shape=[
            jax.ShapeDtypeStruct((rows, both), BF),
            jax.ShapeDtypeStruct((rows, width), BF),
            jax.ShapeDtypeStruct((rows, width), F32),
            jax.ShapeDtypeStruct((rows, width), F32),
            jax.ShapeDtypeStruct((2, margin, both), BF),
            jax.ShapeDtypeStruct((2, margin, both), BF),
            jax.ShapeDtypeStruct((count, 8, 2 * PAIR), F32),
            jax.ShapeDtypeStruct((width, rows), BF),
        ],
        compiler_params=pltpu.CompilerParams(vmem_limit_bytes=24 * 1024 * 1024),
        cost_estimate=pl.CostEstimate(
            flops=8 * 2 * 6 * count * steps * span * 256 * 128,
            bytes_accessed=rows * width * 20,
            transcendentals=count * steps * span * 256,
        ),
        name="block_attention",
    )(
        mult, valid, scales, even,
        packed, packed, packed, first, first, second, second, upstream, *carried,
    )


def pick_kernel(core_ref, qkv_ref, out_ref, top_ref, low_ref):
    core = core_ref[0]
    at = 0
    for pairs in CHUNKS:
        for base in range(0, qkv_ref.shape[1], 8 * PAIR):
            for p in pairs:
                start = pl.multiple_of(base + 2 * p * PAIR + core * PAIR, PAIR)
                top_ref[:, at : at + PAIR] = qkv_ref[:PAIR, pl.ds(start, PAIR)]
                low_ref[:, at : at + PAIR] = qkv_ref[PAIR:, pl.ds(start, PAIR)]
                at += PAIR
    half = out_ref.shape[1] // 2
    rows = out_ref[pl.ds(pl.multiple_of(core * PAIR, PAIR), PAIR), :]
    top_ref[:, at:] = rows[:, :half]
    low_ref[:, at:] = rows[:, half:]


def whole(shape):
    return pl.BlockSpec(shape, lambda *_: (0,) * len(shape))


def small_kernel(kernel, name, scalars, arrays, outs, scratch=()):
    return pl.pallas_call(
        kernel,
        grid_spec=pltpu.PrefetchScalarGridSpec(
            num_scalar_prefetch=len(scalars),
            grid=(1,),
            in_specs=[whole(a.shape) for a in arrays],
            out_specs=[whole(shape) for shape, _ in outs],
            scratch_shapes=list(scratch),
        ),
        out_shape=[jax.ShapeDtypeStruct(shape, kind) for shape, kind in outs],
        compiler_params=pltpu.CompilerParams(vmem_limit_bytes=24 * 1024 * 1024),
        name=name,
    )(*scalars, *arrays)


def pick_weights(w_qkv, w_out, core_flag):
    height, columns = w_qkv.shape
    wide = columns // 2 + w_out.shape[1] // 2
    return small_kernel(
        pick_kernel, "pick_weights", [core_flag], [w_qkv, w_out], [((height // 2, wide), BF)] * 2
    )


def turn_kernel(x_ref, turned_ref):
    for i in range(0, x_ref.shape[0], PAIR):
        for j in range(0, x_ref.shape[1], PAIR):
            tile = x_ref[i : i + PAIR, j : j + PAIR].astype(F32)
            turned_ref[j : j + PAIR, i : i + PAIR] = jnp.transpose(tile).astype(BF)


def rim_kernel(even_ref, *refs):
    t_ref, rim1_ref, rim2_ref = refs[:3]
    even = even_ref[0] == 1
    margin = rim1_ref.shape[1]
    size = t_ref.shape[0] // 4

    def added(index, grad):
        rows = grad.shape[0]
        one, two = rim1_ref[index].astype(F32), rim2_ref[index].astype(F32)
        return jnp.concatenate(
            [
                grad[:margin] + jnp.where(even, two, one),
                grad[margin : rows - margin],
                grad[rows - margin :] + jnp.where(even, one, two),
            ],
            axis=0,
        ).astype(BF)

    if len(refs) == 10:
        q_ref, dk_ref, dv_ref, left_ref, right_ref, x_ref, y_ref = refs[3:]
        keys, values = added(0, dk_ref[...]), added(1, dv_ref[...])
        left_ref[:, : 2 * PAIR] = q_ref[...]
        left_ref[:, 2 * PAIR :] = keys[:, :PAIR]
        right_ref[:, :PAIR] = keys[:, PAIR:]
        right_ref[:, PAIR:] = values
    else:
        ka_ref, kb_ref, va_ref, vb_ref, left_ref, right_ref, x_ref, y_ref = refs[3:]
        left_ref[...] = added(0, jnp.concatenate([ka_ref[...], kb_ref[...]], axis=1))
        right_ref[...] = added(1, jnp.concatenate([va_ref[...], vb_ref[...]], axis=1))
    x_ref[...] = dot(t_ref[: 2 * size, :], left_ref[...]).astype(BF)
    y_ref[...] = dot(t_ref[size : 3 * size, :], right_ref[...]).astype(BF)


def leave_kernel(
    scene_ref, t_ref, a0_ref, a1_ref, a2_ref, cot_ref, q1_ref, q2_ref, left_ref, right_ref, fx_ref, fy_ref,
    x_ref, y_ref, kl_ref, kr_ref, e_ref, o_ref, at_ref,
):
    size = t_ref.shape[0] // 4
    quarter = cot_ref.shape[1] // 4
    at_ref[0] = a0_ref[:PAIR, :]
    at_ref[3] = a0_ref[PAIR:, :]
    at_ref[1] = a1_ref[...]
    at_ref[2] = a2_ref[...]
    x_ref[: 2 * size, :PAIR] = dot(t_ref[: 2 * size, :], q1_ref[...]).astype(BF)
    y_ref[: 2 * size, :PAIR] = dot(t_ref[size : 3 * size, :], q2_ref[...]).astype(BF)
    for i, k in enumerate(ORDER):
        grad = dot(at_ref[jnp.bitwise_xor(scene_ref[0], k)], cot_ref[...])
        evens = jnp.concatenate(
            [grad[:, :quarter], grad[:, 2 * quarter : 3 * quarter]], axis=0
        )
        odds = jnp.concatenate(
            [grad[:, quarter : 2 * quarter], grad[:, 3 * quarter :]], axis=0
        )
        if i < 2:
            x_ref[i * size : (i + 1) * size, PAIR:] = evens.astype(BF)
        else:
            e_ref[i - 2] = evens
        if i in (1, 2):
            y_ref[(i - 1) * size : i * size, PAIR:] = odds.astype(BF)
        else:
            o_ref[i // 3] = odds
    left, right = left_ref[...], right_ref[...]
    y_ref[2 * size :, :] = (
        dot(t_ref[2 * size : 3 * size, :], left) + fx_ref[size:, :].astype(F32)
    ).astype(BF)
    x_ref[2 * size :, :] = (dot(t_ref[:size, :], right) + fy_ref[:size, :].astype(F32)).astype(BF)
    kl_ref[...] = dot(t_ref[3 * size :, :], left) + fx_ref[:size, :].astype(F32)
    kr_ref[...] = dot(t_ref[3 * size :, :], right) + fy_ref[size:, :].astype(F32)


def second_kernel(
    t_ref, q1_ref, q2_ref, key_ref, value_ref, ex_ref, ey_ref, lx_ref, ly_ref, e_ref, o_ref,
    x_ref, y_ref, kl_ref, kr_ref,
):
    size = t_ref.shape[0] // 4

    def term(place, query_ref, other_ref, extra, early_ref, late_ref, half):
        block = t_ref[place * size : (place + 1) * size, :]
        here = slice(half * size, (half + 1) * size)
        early, late = early_ref[here, :].astype(F32), late_ref[here, :].astype(F32)
        return jnp.concatenate(
            [
                dot(block, query_ref[...]) + early[:, :PAIR],
                dot(block, other_ref[...]) + late,
                extra + early[:, PAIR:],
            ],
            axis=1,
        )

    y_ref[...] = term(2, q1_ref, key_ref, e_ref[0], ex_ref, lx_ref, 1).astype(BF)
    x_ref[...] = term(0, q2_ref, value_ref, o_ref[0], ey_ref, ly_ref, 0).astype(BF)
    kl_ref[...] = term(3, q1_ref, key_ref, e_ref[1], ex_ref, lx_ref, 0)
    kr_ref[...] = term(3, q2_ref, value_ref, o_ref[1], ey_ref, ly_ref, 1)


def gate(value, *others):
    return lax.optimization_barrier((value,) + others)[0]


def pick_groups(array, axis, unit, core):
    size = array.shape[axis]
    picked = [
        jnp.where(
            core == 0,
            lax.slice_in_dim(array, at, at + unit, axis=axis),
            lax.slice_in_dim(array, at + unit, at + 2 * unit, axis=axis),
        )
        for at in range(0, size, 2 * unit)
    ]
    return jnp.concatenate(picked, axis=axis)


def spread_groups(array, axis, unit, core):
    groups = jnp.split(array, array.shape[axis] // unit, axis=axis)
    parts = []
    for group in groups:
        empty = jnp.zeros_like(group)
        parts += [jnp.where(core == 0, group, empty), jnp.where(core == 0, empty, group)]
    return jnp.concatenate(parts, axis=axis)


def in_order(core, own, other, axis):
    first = jnp.where(core == 0, own, other)
    second = jnp.where(core == 0, other, own)
    return jnp.concatenate([first, second], axis=axis)


def xor_blocks(blocks, index):
    odd = (index & 1) == 1
    high = (index & 2) == 2
    near = [jnp.where(odd, blocks[k ^ 1], blocks[k]) for k in range(4)]
    return [jnp.where(high, near[k ^ 2], near[k]) for k in range(4)]


ORDER = (1, 3, 2, 0)
CHUNKS = ((0, 3), (1, 2))


def square(value, step):
    return lax.ppermute(value, "fsdp", [(i, i ^ step) for i in range(4)])


def chips(value, step, n_vox):
    return lax.ppermute(value, "vox", [(i, i ^ (2 * step)) for i in range(n_vox)])


def on_device(
    tokens, gain, w_qkv, w_out, logit_scale, key_blocks, slot_count, valid_voxels, cotangent
):
    own_tokens = tokens[0]
    own_cotangent = cotangent[0]
    own_rows, model_width = own_tokens.shape
    rows = 2 * own_rows
    own_blocks = key_blocks.shape[1]
    blocks = 2 * own_blocks
    slot_total = key_blocks.shape[2]
    reach = own_blocks // 2
    margin = reach * BLK
    n_vox = lax.axis_size("vox")
    n_fsdp = lax.axis_size("fsdp")
    n_chip = n_vox // 2
    place = lax.axis_index("vox")
    scene = lax.axis_index("fsdp")
    core = place % 2
    chip = place // 2
    fast = n_vox == 8 and n_fsdp == 4
    unit = 128 if fast else 64
    swap = [(i, i ^ 1) for i in range(n_vox)]
    even, low = chip % 2 == 0, chip < 2
    even_flag, core_flag, scene_flag = [
        jnp.reshape(x, (1,)).astype(jnp.int32) for x in (even, core, scene)
    ]
    near_chips = [(i, i ^ 2) for i in range(n_vox)]
    far_chips = []
    for i in range(n_vox):
        to = i // 2 + (1 if i // 2 % 2 else -1)
        far_chips.append((i, 2 * to + i % 2 if 0 <= to < n_chip else i))
    part_width = model_width // 2

    def columns_of(array, pairs):
        return jnp.concatenate(
            [
                array[:, base + p * PAIR : base + (p + 1) * PAIR]
                for base in range(0, array.shape[1], part_width)
                for p in pairs
            ],
            axis=1,
        )

    if fast:
        top, low_half = pick_weights(w_qkv, w_out, core_flag)
        far_top, near_low = square(top, 2), square(low_half, 1)
        near_top, far_low = square(top, 1), square(low_half, 2)
        diag_top, diag_low = square(far_top, 1), square(near_low, 2)
        near, diag = (near_top, near_low), (diag_top, diag_low)
        far, shard = (far_top, far_low), (top, low_half)
        wide = 3 * part_width // 2
        weights_0, weights_1 = [
            jnp.concatenate(
                [block[:, at : at + wide] for both in (near, diag, far, shard) for block in both],
                axis=0,
            )
            for at in (0, wide)
        ]
        wide = 2 * wide
        out_blocks = [
            jnp.concatenate([block[0][:, wide:], block[1][:, wide:]], axis=1)
            for block in (shard, near, far, diag)
        ]
        out_half = jnp.concatenate(xor_blocks(out_blocks, scene), axis=0)
    else:
        core_qkv = pick_groups(w_qkv, 1, unit, core)
        core_out = pick_groups(w_out, 0, unit, core)
        weights_0, weights_1 = [
            lax.all_gather(columns_of(core_qkv, pairs), "fsdp", axis=0, tiled=True)
            for pairs in CHUNKS
        ]
        out_half = lax.all_gather(core_out, "fsdp", axis=0, tiled=True)

    other_tokens = lax.ppermute(own_tokens, "vox", swap)
    other_cotangent = lax.ppermute(own_cotangent, "vox", swap)
    lists = jnp.concatenate([key_blocks[0], slot_count[0][:, None]], axis=1)
    all_lists = in_order(
        core, lists, lax.ppermute(lists.astype(F32), "vox", swap).astype(jnp.int32), 0
    )
    chip_tokens = in_order(core, own_tokens, other_tokens, 0)
    chip_cotangent = in_order(core, own_cotangent, other_cotangent, 0)

    first_block = chip * blocks
    pool_blocks = blocks + 2 * reach
    window_id = (
        all_lists[:, :slot_total] - first_block + reach
        - 2 * (jnp.arange(blocks, dtype=jnp.int32) // 2)[:, None]
    )
    used = jnp.arange(slot_total, dtype=jnp.int32)[None, :] < all_lists[:, slot_total:]
    hits = jnp.logical_and(
        window_id[:, :, None] == jnp.arange(WINDOW, dtype=jnp.int32), used[:, :, None]
    )
    mult = jnp.sum(hits.astype(jnp.int32), axis=1)
    scene_total = valid_voxels.shape[1]
    pool_ids = first_block - reach + jnp.arange(pool_blocks, dtype=jnp.int32)
    valid = jnp.take(valid_voxels[0], jnp.clip(pool_ids, 0, scene_total - 1))
    group_heads = unit // HD
    scales = pick_groups(logit_scale, 0, group_heads, core)

    wide = chip_tokens.astype(F32)
    inverse = lax.rsqrt(jnp.mean(wide * wide, axis=1, keepdims=True) + EPS)
    normed = (wide * inverse * gain).astype(BF)
    if fast:
        turned = xor_blocks(jnp.split(normed, 4, axis=1), scene)
        normed = jnp.concatenate([turned[k] for k in ORDER], axis=1)
        normed_t = small_kernel(turn_kernel, "turn", [], [normed], [(normed.shape[::-1], BF)])[0]

    def pairings(first, second):
        return lax.ppermute(first, "vox", near_chips), lax.ppermute(second, "vox", far_chips)

    def heads_of(packed, upstream, chunk, begin=0, count=2, carried=()):
        pairs = CHUNKS[chunk]
        used = pairs[begin : begin + count]
        chunk_scales = jnp.concatenate([scales[2 * p : 2 * p + 2] for p in used])
        return attention(
            packed, *halos, upstream, mult, valid, chunk_scales, even_flag, pairs, begin, count,
            4 * chunk, carried,
        )

    def with_rims(grad, first, second):
        first, second = first.astype(F32), second.astype(F32)
        return jnp.concatenate(
            [
                grad[:margin] + jnp.where(even, second, first),
                grad[margin : rows - margin],
                grad[rows - margin :] + jnp.where(even, first, second),
            ],
            axis=0,
        ).astype(BF)

    def key_value_grads(keys, values, rims):
        return [with_rims(g, rims[0][i], rims[1][i]) for i, g in enumerate((keys, values))]

    def out_rows(pairs):
        return jnp.concatenate([out_half[p * PAIR : (p + 1) * PAIR] for p in pairs], axis=0)

    def groups_of(left, right, chunk):
        half = 3 * PAIR
        groups = [left[:, k * PAIR : (k + 1) * PAIR] for k in range(3)]
        groups += [right[:, k * PAIR : (k + 1) * PAIR] for k in range(3)]
        sets = ((0, 3, 4), (1, 2, 5)) if chunk == 0 else ((0, 3, 2), (1, 4, 5))
        evens = jnp.concatenate([groups[k] for k in sets[0]] + [left[:, half:]], axis=1)
        odds = jnp.concatenate([groups[k] for k in sets[1]] + [right[:, half:]], axis=1)
        return jnp.where(even, evens, odds), jnp.where(even, odds, evens).astype(BF)

    def halves_of(kept):
        left, right = kept[:, : 2 * PAIR], kept[:, PAIR : 3 * PAIR]
        if kept.shape[1] > 3 * PAIR:
            more = kept[:, 3 * PAIR :]
            cut = more.shape[0] // 2
            left = jnp.concatenate([left, more[:cut]], axis=0)
            right = jnp.concatenate([right, more[cut:]], axis=0)
        return jnp.where(low, left, right), jnp.where(low, right, left).astype(BF)

    packed_0, packed_1 = [dot(normed, weight).astype(BF) for weight in (weights_0, weights_1)]
    query_width = part_width // 2
    top, bottom = [
        jnp.concatenate([packed[at, query_width:] for packed in (packed_0, packed_1)], axis=1)
        for at in (slice(0, margin), slice(rows - margin, rows))
    ]
    halos = pairings(jnp.where(even, bottom, top), jnp.where(even, top, bottom))
    upstream = dot(chip_cotangent, out_half, ((1,), (1,))).astype(BF)
    first = heads_of(packed_0, upstream, 0)
    rims_0 = pairings(first[4], first[5])
    third = heads_of(packed_1, gate(upstream, first[4], first[5]), 1, 0, 1)
    rims_0 = [gate(rim, third[6]) for rim in rims_0]
    half = 3 * query_width // 2
    if fast:
        left_0, right_0, to_x, to_y = small_kernel(
            rim_kernel, "rims_first", [even_flag],
            [normed_t, *rims_0, first[1], first[2], first[3]],
            [((rows, half), BF)] * 2 + [((model_width // 2, half), BF)] * 2,
        )
        from_x0, from_y0 = square(to_x, 1), square(to_y, 2)
        fourth_in = gate(upstream, to_x, to_y)
    else:
        key_0, value_0 = key_value_grads(first[2], first[3], rims_0)
        grad_0 = jnp.concatenate([first[1], key_0, value_0], axis=1)
        fourth_in = upstream
    fourth = heads_of(packed_1, fourth_in, 1, 1, 1, (third[0], third[4], third[5]))
    rims_1 = pairings(fourth[4], fourth[5])

    att_0 = gate(first[0], fourth[6])
    att_1 = fourth[0]
    if fast:
        quarter = model_width // 4
        key_1, value_1, to_x, to_y = small_kernel(
            rim_kernel, "rims_second", [even_flag],
            [normed_t, *rims_1, third[2], fourth[2], third[3], fourth[3]],
            [((rows, query_width), BF)] * 2 + [((model_width // 2, query_width), BF)] * 2,
        )
        late_x, late_y = square(to_x, 1), square(to_y, 2)
        to_x, to_y, left, right, evens, odds = small_kernel(
            leave_kernel, "leave_early", [scene_flag],
            [normed_t, first[7], third[7], fourth[7], gate(chip_cotangent, to_x, to_y), third[1], fourth[1],
             left_0, right_0, from_x0, from_y0],
            [((3 * quarter, half), BF)] * 2
            + [((quarter, half), F32)] * 2
            + [((2, quarter, quarter), F32)] * 2,
            [pltpu.VMEM((4, PAIR, rows), BF)],
        )
        early_x, early_y = square(to_x, 1), square(to_y, 2)

        left_0, key_1, value_1 = lax.optimization_barrier((left_0, key_1, value_1, to_x, to_y))[:3]
        grad_0 = jnp.concatenate([left_0, right_0], axis=1)
        ngrad_part = dot(grad_0, weights_0, ((1,), (1,))) + dot(
            jnp.concatenate([third[1], fourth[1], key_1, value_1], axis=1), weights_1, ((1,), (1,))
        )
        height = model_width // 4
        kept_0, sent = groups_of(
            left + early_y[2 * height :].astype(F32), right + early_x[2 * height :].astype(F32), 0
        )
        got_0 = chips(sent, 1, n_vox)
        to_x, to_y, left, right = small_kernel(
            second_kernel, "second_exchange", [],
            [normed_t, third[1], fourth[1], key_1, value_1, early_x, early_y, late_x, late_y, evens, odds],
            [((height, half + quarter), BF)] * 2 + [((height, half + quarter), F32)] * 2,
        )
        end_x, end_y = square(to_x, 1), square(to_y, 2)
        att_0, att_1, got_0 = lax.optimization_barrier((att_0, att_1, got_0, to_x, to_y))[:3]
    else:
        key_1, value_1 = key_value_grads(
            *[jnp.concatenate([third[i], fourth[i]], axis=1) for i in (2, 3)], rims_1
        )
        grad_1 = jnp.concatenate([third[1], fourth[1], key_1, value_1], axis=1)
        ngrad_part = dot(grad_0, weights_0, ((1,), (1,))) + dot(grad_1, weights_1, ((1,), (1,)))
    ngrad_mine = lax.dynamic_slice_in_dim(ngrad_part, core * own_rows, own_rows, 0)
    ngrad_theirs = lax.dynamic_slice_in_dim(ngrad_part, (1 - core) * own_rows, own_rows, 0)
    normed_grad = ngrad_mine + lax.ppermute(ngrad_theirs, "vox", swap)
    if fast:
        held = jnp.split(normed_grad, 4, axis=1)
        normed_grad = jnp.concatenate(
            xor_blocks([held[ORDER.index(k)] for k in range(4)], scene), axis=1
        )

    own_wide = own_tokens.astype(F32)
    own_inverse = lax.rsqrt(jnp.mean(own_wide * own_wide, axis=1, keepdims=True) + EPS)
    gain_grad = jnp.sum(normed_grad * own_wide * own_inverse, axis=0)
    scaled_grad = normed_grad * gain
    token_grad = (
        own_cotangent.astype(F32)
        + own_inverse
        * (
            scaled_grad
            - own_wide
            * own_inverse
            * own_inverse
            * jnp.mean(scaled_grad * own_wide, axis=1, keepdims=True)
        )
    ).astype(BF)

    scale_parts = {}
    for pairs, sums in zip(
        CHUNKS, (first[6], jnp.concatenate([third[6], fourth[6]], axis=0))
    ):
        sums = jnp.sum(sums.reshape(2, 8, 2, PAIR), axis=(1, 3))
        for i, p in enumerate(pairs):
            scale_parts[p] = sums[i]
    scale_part = jnp.concatenate([scale_parts[p] for p in range(len(scale_parts))])
    scale_grad = spread_groups(scale_part, 0, group_heads, core)

    if fast:
        small = jnp.concatenate([gain_grad, scale_grad, jnp.zeros((112,), F32)]).reshape(9, 128)
        end_x, end_y, small = lax.optimization_barrier((end_x, end_y, small))
        small = small + square(small, 1)
        kept_0, sent = halves_of(kept_0 + got_0.astype(F32))
        got_0 = chips(sent, 2, n_vox)
        kept_1, sent = groups_of(left + end_y.astype(F32), right + end_x.astype(F32), 1)
        got_1 = chips(sent, 1, n_vox)
        small, att_0, att_1 = lax.optimization_barrier((small, att_0, att_1, sent))[:3]
        small = small + square(small, 2)
        small = small + lax.ppermute(small, "vox", swap)
        got_1, small, token_grad = lax.optimization_barrier((got_1, small, token_grad))
        kept_1, sent = halves_of(kept_1 + got_1.astype(F32))
        got_1 = chips(sent, 2, n_vox)
        small = gate(small, sent)
        small = small + chips(small, 1, n_vox)
        small = small + chips(small, 2, n_vox)
        got_1, small = lax.optimization_barrier((got_1, small))
        small = small.reshape(-1)
        summed_gain, summed_scale = small[:model_width], small[model_width : model_width + HEADS]
        kept_1 = kept_1 + got_1.astype(F32)
        qkv_sums = [kept_0 + got_0.astype(F32), kept_1[:height]]
        out_sum = kept_1[height:]
    else:
        out_sums = [dot(att, chip_cotangent, ((0,), (0,))) for att in (att_0, att_1)]
        qkv_sums = [dot(normed, grad, ((0,), (0,))) for grad in (grad_0, grad_1)]
        summed_gain, summed_scale = lax.psum((gain_grad, scale_grad), ("vox", "fsdp"))

    mixed_part = dot(att_0, out_rows(CHUNKS[0])) + dot(att_1, out_rows(CHUNKS[1]))
    mixed_mine = lax.dynamic_slice_in_dim(mixed_part, core * own_rows, own_rows, 0)
    mixed_theirs = lax.dynamic_slice_in_dim(mixed_part, (1 - core) * own_rows, own_rows, 0)
    mixed = (
        own_tokens.astype(F32) + (mixed_mine + lax.ppermute(mixed_theirs, "vox", swap))
    ).astype(BF)

    if fast:
        half = out_sum.shape[1] // 2
        first, second = out_sum[:, :half], out_sum[:, half:]
        out_other = lax.ppermute(jnp.where(core == 0, second, first), "vox", swap)
        summed_out = in_order(core, jnp.where(core == 0, first, second), out_other, 0)

        a0, a1 = qkv_sums[0][:, :PAIR], qkv_sums[0][:, PAIR:]
        b0, b1 = qkv_sums[1][:, :PAIR], qkv_sums[1][:, PAIR:]

        def by_chip(options):
            value = options[3]
            for k in range(3):
                value = jnp.where(chip == k, options[k], value)
            return value

        g0 = by_chip((a0, a0, b1, b0))
        g1 = by_chip((b0, a1, a0, b1))
        g2 = by_chip((b1, b0, a1, a1))
        got = lax.ppermute(jnp.where(core == 0, g2, g0), "vox", swap)
        summed_qkv = jnp.concatenate(
            [
                jnp.where(core == 0, g0, g1),
                got,
                jnp.where(core == 0, g1, g2),
            ],
            axis=1,
        )
    else:
        by_pair = {}
        cols = {}
        for pairs, out_total, qkv_total in zip(CHUNKS, out_sums, qkv_sums):
            for i, p in enumerate(pairs):
                by_pair[p] = out_total[i * PAIR : (i + 1) * PAIR]
                for j in range(3):
                    at = (2 * j + i) * PAIR
                    cols[4 * j + p] = qkv_total[:, at : at + PAIR]
        out_total = jnp.concatenate([by_pair[p] for p in range(4)], axis=0)
        qkv_total = jnp.concatenate([cols[k] for k in range(12)], axis=1)
        out_total = spread_groups(out_total, 0, unit, core)
        qkv_total = lax.psum_scatter(qkv_total, "fsdp", scatter_dimension=0, tiled=True)
        qkv_total = spread_groups(qkv_total, 1, unit, core)
        summed_qkv = lax.psum_scatter(qkv_total, "vox", scatter_dimension=1, tiled=True)
        out_total = lax.psum_scatter(out_total, "fsdp", scatter_dimension=0, tiled=True)
        summed_out = lax.psum_scatter(out_total, "vox", scatter_dimension=1, tiled=True)

    return (
        mixed[None],
        token_grad[None],
        summed_qkv,
        summed_out,
        summed_gain,
        summed_scale,
    )


def solution(mesh):
    return jax.shard_map(
        on_device,
        mesh=mesh,
        in_specs=(
            P("fsdp", "vox", None),
            P(),
            P("fsdp", None),
            P("fsdp", None),
            P(),
            P("fsdp", "vox", None),
            P("fsdp", "vox"),
            P("fsdp", None),
            P("fsdp", "vox", None),
        ),
        out_specs=(
            P("fsdp", "vox", None),
            P("fsdp", "vox", None),
            P("fsdp", "vox"),
            P("fsdp", "vox"),
            P(),
            P(),
        ),
        check_vma=False,
    )
```
